32 devices in a mesh: dp: 8 (over z, x), tensor: 4 (over y, core).
Axes of the slice: x: 2, y: 2, z: 4, core: 2. Of those that a mesh axis runs over, the one named last changes fastest.
Arguments:
- inputs: bfloat16 [8192, 2048], P(('dp', 'tensor')), may hold values from -6 to 6
- lengths: int32 [8], P('dp'), may hold values from 128 to 1024, as said below
- cotangent: bfloat16 [8192, 2048], P(('dp', 'tensor')), may hold values from -6 to 6
- norm_attn: float32 [2048], replicated, may hold values from 0.5 to 1.5
- norm_ffn: float32 [2048], replicated, may hold values from 0.5 to 1.5
- norm_heads: float32 [256], replicated, may hold values from 0.5 to 1.5
- w_query: bfloat16 [2048, 2048], P('dp', 'tensor'), may hold values from -0.125 to 0.125
- w_key: bfloat16 [2048, 2048], P('dp', 'tensor'), may hold values from -0.125 to 0.125
- w_value: bfloat16 [2048, 4096], P('dp', 'tensor'), may hold values from -0.125 to 0.125
- w_out_gate: bfloat16 [2048, 4096], P('dp', 'tensor'), may hold values from -0.125 to 0.125
- w_decay: bfloat16 [2048, 16], P('dp', 'tensor'), may hold values from -0.125 to 0.125
- w_beta: bfloat16 [2048, 16], P('dp', 'tensor'), may hold values from -0.125 to 0.125
- w_output: bfloat16 [4096, 2048], P('tensor', 'dp'), may hold values from -0.1875 to 0.1875
- conv_query: float32 [4, 2048], replicated, may hold values from -3 to 3
- conv_key: float32 [4, 2048], replicated, may hold values from -3 to 3
- conv_value: float32 [4, 4096], replicated, may hold values from -3 to 3
- decay_log: float32 [16], replicated, may hold values from -7 to -2.5
- decay_bias: float32 [16], replicated, may hold values from -2 to 1
- w_ffn_gate: bfloat16 [2048, 5632], P('dp', 'tensor'), may hold values from -0.125 to 0.125
- w_ffn_up: bfloat16 [2048, 5632], P('dp', 'tensor'), may hold values from -0.125 to 0.125
- w_ffn_down: bfloat16 [5632, 2048], P('tensor', 'dp'), may hold values from -0.15625 to 0.15625
Outputs:
- outputs: bfloat16 [8192, 2048], P(('dp', 'tensor'))
- statistics: float32 [3], replicated
- grad_inputs: float32 [8192, 2048], P(('dp', 'tensor'))
- grad_norm_attn: float32 [2048], replicated
- grad_norm_ffn: float32 [2048], replicated
- grad_norm_heads: float32 [256], replicated
- grad_w_query: float32 [2048, 2048], P('dp', 'tensor')
- grad_w_key: float32 [2048, 2048], P('dp', 'tensor')
- grad_w_value: float32 [2048, 4096], P('dp', 'tensor')
- grad_w_out_gate: float32 [2048, 4096], P('dp', 'tensor')
- grad_w_decay: float32 [2048, 16], P('dp', 'tensor')
- grad_w_beta: float32 [2048, 16], P('dp', 'tensor')
- grad_w_output: float32 [4096, 2048], P('tensor', 'dp')
- grad_conv_query: float32 [4, 2048], replicated
- grad_conv_key: float32 [4, 2048], replicated
- grad_conv_value: float32 [4, 4096], replicated
- grad_decay_log: float32 [16], replicated
- grad_decay_bias: float32 [16], replicated
- grad_w_ffn_gate: float32 [2048, 5632], P('dp', 'tensor')
- grad_w_ffn_up: float32 [2048, 5632], P('dp', 'tensor')
- grad_w_ffn_down: float32 [5632, 2048], P('tensor', 'dp')
The draws below stay inside these ranges and needn't reach their ends.
Inputs may be any that keep to these rules, and one draw needn't show every extreme that they name: Each sequence fills the first lengths rows of its group's 1024 rows; some length equals 1024 in every draw.
All inputs are finite; a program needn't handle non-finite values.
Results may differ from the reference program's by a relative error of at most 0.014.
The reference program's roundings to bfloat16 on the way count: a program that leaves them out, or rounds other values in their place, can miss the bound.
Values may be sent and summed in bfloat16 or wider, within the bound.
No kernel may reach another device: no remote copies, remote signals or barrier semaphores. Data moves between devices by JAX's collectives and lax.ppermute only.
A program may use at most 320 MiB of HBM per device.

```python
import jax
import jax.numpy as jnp
from jax import lax

D = 2048
H = 16
DV = 256
FF = 5632
CONV = 4
SPAN = 64
SEQ = 1024
HK = 2048
HV = 4096
GROUPS = 8
TOKENS = 8192


def draw_lengths(key, part):
    first, second = jax.random.split(key)
    drawn = jax.random.randint(first, (GROUPS,), SEQ // 8, SEQ + 1)
    chosen = jax.random.randint(second, (), 0, GROUPS)
    return jnp.where(jnp.arange(GROUPS) == chosen, SEQ, drawn).astype(jnp.int32)


def levels(key, extent, cuts, low, largest):
    factor_of = 1.0
    for dim, blocks in cuts:
        draws = jax.random.uniform(jax.random.fold_in(jax.random.fold_in(key, 6), dim), (blocks,), jnp.float32, low / len(cuts), largest / len(cuts))
        factor_of = factor_of * jnp.repeat(jnp.exp(draws), extent[dim] // blocks).reshape((-1,) + (1,) * (len(extent) - 1 - dim))
    return factor_of


def scatter_about(rng, shape, scale, bound, pieces=(), kind=jnp.bfloat16):
    loudness = levels(rng, shape, pieces, -0.22, 0.18) if pieces else 1.0
    values = jax.random.normal(rng, shape, jnp.float32) * scale * loudness
    return jnp.minimum(jnp.maximum(values, -bound), bound).astype(kind)


def setup_inputs(seed: int = 0) -> dict:
    streams_of = jax.random.split(jax.random.key(seed), 22)
    return {
        "inputs": scatter_about(streams_of[0], (TOKENS, D), 1.0, 6.0, ((0, 32),)),
        "lengths": draw_lengths(jax.random.fold_in(streams_of[21], 71), 0),
        "cotangent": scatter_about(streams_of[2], (TOKENS, D), 1.0, 6.0, ((0, 32),)),
        "norm_attn": jnp.clip(1.0 + 0.1 * jax.random.normal(streams_of[3], (D,), jnp.float32), 0.5, 1.5),
        "norm_ffn": jnp.clip(1.0 + 0.1 * jax.random.normal(streams_of[4], (D,), jnp.float32), 0.5, 1.5),
        "norm_heads": jnp.clip(1.0 + 0.1 * jax.random.normal(streams_of[5], (DV,), jnp.float32), 0.5, 1.5),
        "w_query": scatter_about(streams_of[6], (D, HK), D ** -0.5, 0.125, ((0, 8), (1, 4))),
        "w_key": scatter_about(streams_of[7], (D, HK), D ** -0.5, 0.125, ((0, 8), (1, 4))),
        "w_value": scatter_about(streams_of[8], (D, HV), D ** -0.5, 0.125, ((0, 8), (1, 4))),
        "w_out_gate": scatter_about(streams_of[9], (D, HV), D ** -0.5, 0.125, ((0, 8), (1, 4))),
        "w_decay": scatter_about(streams_of[10], (D, H), D ** -0.5, 0.125, ((0, 8), (1, 4))),
        "w_beta": scatter_about(streams_of[11], (D, H), D ** -0.5, 0.125, ((0, 8), (1, 4))),
        "w_output": scatter_about(streams_of[12], (HV, D), (HV // 4) ** -0.5, 0.1875, ((0, 4), (1, 8))),
        "conv_query": scatter_about(streams_of[13], (CONV, HK), 0.5, 3.0, (), jnp.float32),
        "conv_key": scatter_about(streams_of[14], (CONV, HK), 0.5, 3.0, (), jnp.float32),
        "conv_value": scatter_about(streams_of[15], (CONV, HV), 0.5, 3.0, (), jnp.float32),
        "decay_log": jnp.clip(jax.random.uniform(streams_of[16], (H,), jnp.float32, -7.0, -2.5), -7.0, -2.5),
        "decay_bias": jnp.clip(jax.random.uniform(streams_of[17], (H,), jnp.float32, -2.0, 1.0), -2.0, 1.0),
        "w_ffn_gate": scatter_about(streams_of[18], (D, FF), D ** -0.5, 0.125, ((0, 8), (1, 4))),
        "w_ffn_up": scatter_about(streams_of[19], (D, FF), D ** -0.5, 0.125, ((0, 8), (1, 4))),
        "w_ffn_down": scatter_about(streams_of[20], (FF, D), (FF // 4) ** -0.5, 0.15625, ((0, 4), (1, 8))),
    }


@jax.custom_vjp
def low(v):
    return lax.optimization_barrier(v.astype(jnp.bfloat16)).astype(jnp.float32)

@jax.custom_vjp
def low_back(v):
    return v

def low_keep(v):
    return (low(v), None)

def low_pass(kept, grad):
    return (grad,)

def back_keep(v):
    return (v, None)

def back_low(kept, grad):
    return (low(grad),)
low.defvjp(low_keep, low_pass)
low_back.defvjp(back_keep, back_low)

def matmul(left, right):
    return jnp.dot(left, right, precision=lax.Precision.HIGHEST)

def rms_scale(values):
    return values * lax.rsqrt(lax.optimization_barrier(jnp.mean(values * values, axis=-1, keepdims=True)) + 1e-06)

def causal_conv(projected, kernel):
    width = kernel.shape[0]
    length = projected.shape[0]
    padded = jnp.pad(projected, ((width - 1, 0), (0, 0)))
    total = kernel[0] * padded[0:length]
    for offset in range(1, width):
        total = total + kernel[offset] * padded[offset:offset + length]
    return total

def unit_heads(mixed, heads, factor):
    shaped = mixed.reshape(mixed.shape[0], heads, -1)
    return shaped * lax.rsqrt(lax.optimization_barrier(jnp.sum(shaped * shaped, axis=-1, keepdims=True)) + 1e-06) * factor

def delta_rule(query, key, value, beta, log_decay):
    length, heads, key_size = query.shape
    value_size = value.shape[2]
    blocks = length // SPAN
    highest_precision = lax.Precision.HIGHEST

    def token_step(running_state, item):
        query_transposed, key_transposed, value_t, beta_t, decay_t = item
        factor = jnp.exp(decay_t)
        recalled_values = jnp.einsum('qf,qfe->qe', key_transposed, running_state, precision=highest_precision)
        written = (beta_t[:, None] * key_transposed)[:, :, None] * (value_t - factor[:, None] * recalled_values)[:, None, :]
        running_state = factor[:, None, None] * running_state + written
        return (running_state, jnp.einsum('qf,qfe->qe', query_transposed, running_state, precision=highest_precision))

    def block_step(running_state, items):
        return lax.scan(token_step, running_state, items)

    def arrange(array):
        return array.reshape((blocks, SPAN) + array.shape[1:])
    items = (arrange(query), arrange(key), arrange(value), arrange(beta), arrange(log_decay))
    running_state = jnp.zeros((heads, key_size, value_size), jnp.float32)
    _, output_rows = lax.scan(jax.checkpoint(block_step), running_state, items)
    return output_rows.reshape(length, heads, value_size)

def mixer_core(query_proj, key_proj, value_proj, gate_proj, decay_proj, beta_proj, conv_query, conv_key, conv_value, decay_log, decay_bias, norm_heads):
    heads = decay_proj.shape[1]
    length = query_proj.shape[0]
    key_size = query_proj.shape[1] // heads
    query = low(unit_heads(jax.nn.silu(causal_conv(query_proj, conv_query)), heads, key_size ** (-0.5)))
    key = low(unit_heads(jax.nn.silu(causal_conv(key_proj, conv_key)), heads, 1.0))
    value = low(jax.nn.silu(causal_conv(value_proj, conv_value)).reshape(length, heads, -1))
    beta = jax.nn.sigmoid(beta_proj)
    log_decay = -jnp.exp(decay_log) * jax.nn.softplus(decay_proj + decay_bias)
    heads_out = delta_rule(query, key, value, beta, log_decay)
    scaled = heads_out * lax.rsqrt(lax.optimization_barrier(jnp.mean(heads_out * heads_out, axis=-1, keepdims=True)) + 1e-05) * norm_heads
    gated = scaled * jax.nn.silu(gate_proj.reshape(length, heads, -1))
    return gated.reshape(length, -1)

def forward(stream_in, valid, params):
    norm_attn, norm_ffn, norm_heads, w_query, w_key, w_value, w_out_gate, w_decay, w_beta, w_output, conv_query, conv_key, conv_value, decay_log, decay_bias, w_ffn_gate, w_ffn_up, w_ffn_down = params
    normed_in = low(rms_scale(stream_in) * norm_attn)
    query_proj = low_back(matmul(normed_in, low(w_query)))
    key_proj = low_back(matmul(normed_in, low(w_key)))
    value_proj = low_back(matmul(normed_in, low(w_value)))
    gate_proj = low_back(matmul(normed_in, low(w_out_gate)))
    decay_proj = low_back(matmul(normed_in, low(w_decay)))
    beta_proj = low_back(matmul(normed_in, low(w_beta)))
    mixer = low(mixer_core(query_proj, key_proj, value_proj, gate_proj, decay_proj, beta_proj, conv_query, conv_key, conv_value, decay_log, decay_bias, norm_heads))
    branch_attn = low_back(matmul(mixer, low(w_output)))
    stream = stream_in + branch_attn
    normed_mid = low(rms_scale(stream) * norm_ffn)
    ffn_gate = low_back(matmul(normed_mid, low(w_ffn_gate)))
    ffn_up = low_back(matmul(normed_mid, low(w_ffn_up)))
    hidden = low(jax.nn.silu(ffn_gate) * ffn_up)
    branch_ffn = low_back(matmul(hidden, low(w_ffn_down)))
    outputs = valid * (stream + branch_ffn)
    return (outputs, (branch_attn, branch_ffn))

def reference(inputs, lengths, cotangent, norm_attn, norm_ffn, norm_heads, w_query, w_key, w_value, w_out_gate, w_decay, w_beta, w_output, conv_query, conv_key, conv_value, decay_log, decay_bias, w_ffn_gate, w_ffn_up, w_ffn_down):
    params = (norm_attn.astype(jnp.float32), norm_ffn.astype(jnp.float32), norm_heads.astype(jnp.float32), w_query.astype(jnp.float32), w_key.astype(jnp.float32), w_value.astype(jnp.float32), w_out_gate.astype(jnp.float32), w_decay.astype(jnp.float32), w_beta.astype(jnp.float32), w_output.astype(jnp.float32), conv_query.astype(jnp.float32), conv_key.astype(jnp.float32), conv_value.astype(jnp.float32), decay_log.astype(jnp.float32), decay_bias.astype(jnp.float32), w_ffn_gate.astype(jnp.float32), w_ffn_up.astype(jnp.float32), w_ffn_down.astype(jnp.float32))
    streams = inputs.astype(jnp.float32).reshape(GROUPS, SEQ, D)
    cotangents = cotangent.astype(jnp.float32).reshape(GROUPS, SEQ, D)
    positions = jnp.arange(SEQ, dtype=jnp.int32)

    def per_group(totals, item):
        stream_in, group_cot, length = item
        valid = (positions < length.astype(jnp.int32)).astype(jnp.float32)[:, None]

        def local_forward(stream_arg, param_arg):
            return forward(stream_arg, valid, param_arg)
        outputs, pullback, branches = jax.vjp(local_forward, stream_in, params, has_aux=True)
        grad_in, grad_params = pullback(group_cot)
        branch_attn, branch_ffn = branches
        sums = jnp.stack([jnp.sum(valid * stream_in * stream_in), jnp.sum(valid * branch_attn * branch_attn), jnp.sum(valid * branch_ffn * branch_ffn)])
        grad_totals = jax.tree.map(jnp.add, totals[0], grad_params)
        return ((grad_totals, totals[1] + sums, totals[2] + jnp.sum(valid)), (outputs, grad_in))
    start = (jax.tree.map(jnp.zeros_like, params), jnp.zeros((3,), jnp.float32), jnp.zeros((), jnp.float32))
    totals, results = lax.scan(per_group, start, (streams, cotangents, lengths))
    grads, sums, count = totals
    outputs, grad_in = results
    statistics = jnp.sqrt(sums / (count * D))
    return (outputs.reshape(TOKENS, D).astype(jnp.bfloat16), statistics, grad_in.reshape(TOKENS, D), grads[0], grads[1], grads[2], grads[3], grads[4], grads[5], grads[6], grads[7], grads[8], grads[9], grads[10], grads[11], grads[12], grads[13], grads[14], grads[15], grads[16], grads[17])
```

```python
import functools

import jax
import jax.numpy as jnp
from jax import lax
from jax.experimental import pallas as pl
from jax.experimental.pallas import tpu as pltpu
from jax.sharding import PartitionSpec as P

DK = 128
BF=jnp.bfloat16; F32=jnp.float32
CHUNK=128

def dot1(a,b,ca=1,cb=0):
    return lax.dot_general(a,b,(((ca,),(cb,)),((),())),preferred_element_type=F32)
def split(a):
    if a.dtype==BF: return a,None
    h=a.astype(BF); return h,(a-h.astype(F32)).astype(BF)
def mm(a,b,ca=1,cb=0):
    ah,al=a if isinstance(a,tuple) else split(a)
    bh,bl=b if isinstance(b,tuple) else split(b)
    r=dot1(ah,bh,ca,cb)
    if bl is not None: r=r+dot1(ah,bl,ca,cb)
    if al is not None: r=r+dot1(al,bh,ca,cb)
    return r

def inverses(As):
    C=As[0].shape[0]
    i=lax.broadcasted_iota(jnp.int32,(C,C),0); j=lax.broadcasted_iota(jnp.int32,(C,C),1)
    eye=jnp.where(i==j,1.0,0.0).astype(F32)
    same=lambda s: lax.shift_right_logical(i,s)==lax.shift_right_logical(j,s)
    m3=same(3)
    Bs=[jnp.where(m3,A,0.0) for A in As]
    B2=[mm(s,s) for s in map(split,Bs)]
    X=[eye-B for B in Bs]
    B2s=[split(b) for b in B2]
    B4=[mm(b,b) for b in B2s]
    X=[x+mm(x,b) for x,b in zip(X,B2s)]
    X=[x+mm(x,b) for x,b in zip(X,B4)]
    s=3
    while (1<<s)<C:
        m=jnp.logical_and(same(s+1),jnp.logical_not(same(s)))
        Xs=[split(x) for x in X]
        Y=[mm(jnp.where(m,A,0.0),x) for A,x in zip(As,Xs)]
        X=[x-mm(xs,y) for x,xs,y in zip(X,Xs,Y)]
        s+=1
    return X

def fwd_kernel(H,DK,DV,NC,q_ref,k_ref,v_ref,bc_ref,gc_ref,gr_ref,o_ref,u_ref,t_ref,s_ref,S):
    C=CHUNK
    @pl.when(pl.program_id(0)==0)
    def _():
        S[...]=jnp.zeros_like(S)
    i=lax.broadcasted_iota(jnp.int32,(C,C),0); j=lax.broadcasted_iota(jnp.int32,(C,C),1)
    low=i>=j; strict=i>j
    idx=[(c,h) for c in range(NC) for h in range(H)]
    rows=lambda c: slice(c*C,(c+1)*C)
    q={x:q_ref[rows(x[0]),x[1]*DK:(x[1]+1)*DK] for x in idx}
    k={x:k_ref[rows(x[0]),x[1]*DK:(x[1]+1)*DK] for x in idx}
    v={x:v_ref[rows(x[0]),x[1]*DV:(x[1]+1)*DV] for x in idx}
    b={x:bc_ref[rows(x[0]),x[1]:x[1]+1] for x in idx}
    g={x:gc_ref[rows(x[0]),x[1]:x[1]+1] for x in idx}
    gr={x:gr_ref[x[0],x[1]:x[1]+1,:] for x in idx}
    D={x:jnp.exp(jnp.where(low,g[x]-gr[x],-1e30)) for x in idx}
    A={x:jnp.where(strict,dot1(k[x],k[x],1,1)*b[x]*D[x],0.0) for x in idx}
    T=dict(zip(idx,inverses([A[x] for x in idx])))
    P={x:dot1(q[x],k[x],1,1)*D[x] for x in idx}
    gam={x:jnp.exp(g[x]) for x in idx}
    Ts={x:split(T[x]) for x in idx}
    TV={x:mm(Ts[x],b[x]*v[x].astype(F32)) for x in idx}
    W={x:mm(Ts[x],b[x]*gam[x]*k[x].astype(F32)) for x in idx}
    for c in range(NC):
        for h in range(H):
            x=(c,h)
            t_ref[rows(c),h*C:(h+1)*C]=T[x]
            S0=S[h*DK:(h+1)*DK,:]
            s_ref[c,h*DK:(h+1)*DK,:]=S0
            Ss=split(S0)
            U=TV[x]-mm(W[x],Ss)
            Us=split(U)
            u_ref[rows(c),h*DV:(h+1)*DV]=U
            o_ref[rows(c),h*DV:(h+1)*DV]=gam[x]*mm(q[x],Ss)+mm(P[x],Us)
            gl=gr[x][:,C-1:C]
            S[h*DK:(h+1)*DK,:]=jnp.exp(gl)*S0+mm(k[x].astype(F32)*jnp.exp(gl-g[x]),Us,0,0)

def bwd_kernel(H,DK,DV,NC,q_ref,k_ref,v_ref,bc_ref,gc_ref,gr_ref,u_ref,t_ref,s_ref,do_ref,
               dq_ref,dk_ref,dv_ref,dbc_ref,dgc_ref,dgr_ref,dS):
    C=CHUNK
    @pl.when(pl.program_id(0)==0)
    def _():
        dS[...]=jnp.zeros_like(dS)
    i=lax.broadcasted_iota(jnp.int32,(C,C),0); j=lax.broadcasted_iota(jnp.int32,(C,C),1)
    low=i>=j; strict=i>j
    last=lax.broadcasted_iota(jnp.int32,(C,1),0)==C-1
    rows=lambda c: slice(c*C,(c+1)*C)
    for c in reversed(range(NC)):
        for h in range(H):
            q=q_ref[rows(c),h*DK:(h+1)*DK]; k=k_ref[rows(c),h*DK:(h+1)*DK]
            v=v_ref[rows(c),h*DV:(h+1)*DV]
            b=bc_ref[rows(c),h:h+1]; g=gc_ref[rows(c),h:h+1]; gr=gr_ref[c,h:h+1,:]
            U=split(u_ref[rows(c),h*DV:(h+1)*DV]); T=split(t_ref[rows(c),h*C:(h+1)*C])
            S0=s_ref[c,h*DK:(h+1)*DK,:]; Ss=split(S0)
            dO=split(do_ref[rows(c),h*DV:(h+1)*DV])
            qf=q.astype(F32); kf=k.astype(F32)
            D=jnp.exp(jnp.where(low,g-gr,-1e30))
            kk=dot1(k,k,1,1); qk=dot1(q,k,1,1)
            bD=b*D
            A=jnp.where(strict,kk*bD,0.0); P=qk*D
            gam=jnp.exp(g); gl=gr[:,C-1:C]; e=jnp.exp(gl-g); G=jnp.exp(gl)
            dSv=dS[h*DK:(h+1)*DK,:]; dSs=split(dSv)
            dU=mm(P,dO,0,0)+mm(kf*e,dSs)
            dR=mm(T,dU,0,0); dRs=split(dR)
            dS[h*DK:(h+1)*DK,:]=G*dSv+mm(qf*gam,dO,0,0)-mm(kf*(b*gam),dRs,0,0)
            dP=jnp.where(low,mm(dO,U,1,1),0.0)
            dA=jnp.where(strict,-mm(dRs,U,1,1),0.0)
            Rb=v.astype(F32)-gam*mm(k,Ss)
            dv_ref[rows(c),h*DV:(h+1)*DV]=b*dR
            db=jnp.sum(dR*Rb,axis=1,keepdims=True)+jnp.sum(dA*kk*D,axis=1,keepdims=True)
            dOS=mm(dO,Ss,1,1); dRS=mm(dRs,Ss,1,1); UdS=mm(U,dSs,1,1)
            M1=split(dP*D); M2=split(dA*bD)
            dOS=gam*dOS; dRS=(b*gam)*dRS; UdS=e*UdS
            dq_ref[rows(c),h*DK:(h+1)*DK]=dOS+mm(M1,k)
            dk_ref[rows(c),h*DK:(h+1)*DK]=UdS-dRS+mm(M1,q,0,0)+mm(M2,k)+mm(M2,k,0,0)
            X=dP*P+dA*A
            uk=jnp.sum(UdS*kf,axis=1,keepdims=True)
            tot=jnp.sum(uk,axis=0,keepdims=True)+G*jnp.sum(jnp.sum(S0*dSv,axis=1,keepdims=True),axis=0,keepdims=True)
            dgc=jnp.sum(dOS*qf-dRS*kf+X,axis=1,keepdims=True)-uk
            dbc_ref[rows(c),h:h+1]=db
            dgc_ref[rows(c),h:h+1]=dgc+jnp.where(last,tot,0.0)
            dgr_ref[c,h:h+1,:]=jnp.sum(X,axis=0,keepdims=True)

def specs(C,H,DK,DV,NC,rev,n):
    ix=(lambda s: n-1-s) if rev else (lambda s: s)
    r=lambda w: pl.BlockSpec((NC*C,w),lambda s:(ix(s),0))
    t=lambda a,w: pl.BlockSpec((NC,a,w),lambda s:(ix(s),0,0))
    return r,t
def delta_fwd(q,k,v,bc,gc,gr,NC=1):
    L,HK=q.shape; H=bc.shape[1]; DK=HK//H; DV=v.shape[1]//H; C=CHUNK; n=L//C//NC
    r,t=specs(C,H,DK,DV,NC,False,n)
    return pl.pallas_call(functools.partial(fwd_kernel,H,DK,DV,NC),grid=(n,),
        in_specs=[r(HK),r(HK),r(H*DV),r(H),r(H),t(H,C)],
        out_specs=[r(H*DV),r(H*DV),r(H*C),t(H*DK,DV)],
        out_shape=[jax.ShapeDtypeStruct((L,H*DV),F32),jax.ShapeDtypeStruct((L,H*DV),F32),jax.ShapeDtypeStruct((L,H*C),F32),jax.ShapeDtypeStruct((L//C,H*DK,DV),F32)],
        scratch_shapes=[pltpu.VMEM((H*DK,DV),F32)],
        compiler_params=pltpu.CompilerParams(vmem_limit_bytes=56*2**20),name="delta_fwd")(q,k,v,bc,gc,gr)
def delta_bwd(q,k,v,bc,gc,gr,u,tt,s,do,NC=1):
    L,HK=q.shape; H=bc.shape[1]; DK=HK//H; DV=v.shape[1]//H; C=CHUNK; n=L//C//NC
    r,t=specs(C,H,DK,DV,NC,True,n)
    return pl.pallas_call(functools.partial(bwd_kernel,H,DK,DV,NC),grid=(n,),
        in_specs=[r(HK),r(HK),r(H*DV),r(H),r(H),t(H,C),r(H*DV),r(H*C),t(H*DK,DV),r(H*DV)],
        out_specs=[r(HK),r(HK),r(H*DV),r(H),r(H),t(H,C)],
        out_shape=[jax.ShapeDtypeStruct((L,HK),F32),jax.ShapeDtypeStruct((L,HK),F32),jax.ShapeDtypeStruct((L,H*DV),F32),jax.ShapeDtypeStruct((L,H),F32),jax.ShapeDtypeStruct((L,H),F32),jax.ShapeDtypeStruct((L//C,H,C),F32)],
        scratch_shapes=[pltpu.VMEM((H*DK,DV),F32)],
        compiler_params=pltpu.CompilerParams(vmem_limit_bytes=56*2**20),name="delta_bwd")(q,k,v,bc,gc,gr,u,tt,s,do)


def causal_conv(projected, kernel):
    width = kernel.shape[0]
    length = projected.shape[0]
    padded = jnp.pad(projected, ((width - 1, 0), (0, 0)))
    total = kernel[0] * padded[0:length]
    for offset in range(1, width):
        total = total + kernel[offset] * padded[offset : offset + length]
    return total


def unit_heads(mixed, heads, factor):
    shaped = mixed.reshape(mixed.shape[0], heads, -1)
    scaled = shaped * lax.rsqrt(jnp.sum(shaped * shaped, axis=-1, keepdims=True) + 1e-06) * factor
    return scaled.reshape(mixed.shape)


def mixer_front(query_proj, key_proj, value_proj, conv_query, conv_key, conv_value):
    heads = query_proj.shape[1] // DK
    query = unit_heads(jax.nn.silu(causal_conv(query_proj, conv_query)), heads, DK ** (-0.5))
    key = unit_heads(jax.nn.silu(causal_conv(key_proj, conv_key)), heads, 1.0)
    value = jax.nn.silu(causal_conv(value_proj, conv_value))
    return (query, key, value)


def decay_terms(decay_proj, beta_proj, decay_log, decay_bias):
    beta = jax.nn.sigmoid(beta_proj)
    log_decay = -jnp.exp(decay_log) * jax.nn.softplus(decay_proj + decay_bias)
    return (beta, running_sum(log_decay))


def running_sum(values):
    length, heads = values.shape
    blocks = values.reshape(length // CHUNK, CHUNK, heads)
    order = jnp.arange(CHUNK)
    ones = (order[:, None] >= order[None, :]).astype(jnp.float32)
    return jnp.einsum("ts,bsh->bth", ones, blocks, precision=lax.Precision.HIGHEST).reshape(
        length, heads
    )


def gated_heads(heads_out, gate_proj, norm_heads):
    length = heads_out.shape[0]
    shaped = heads_out.reshape(length, -1, norm_heads.shape[0])
    scaled = (
        shaped * lax.rsqrt(jnp.mean(shaped * shaped, axis=-1, keepdims=True) + 1e-05) * norm_heads
    )
    gated = scaled * jax.nn.silu(gate_proj.reshape(shaped.shape))
    return gated.reshape(length, -1)


def spread_rows(normed):
    return lax.all_gather(normed, "tensor", axis=0, tiled=True)


def spread_grads(grads):
    return lax.all_gather(grads, "tensor", axis=0, tiled=True)


def fetch_attention(w_query, w_key, w_value, w_out_gate, w_decay, w_beta, w_output):
    return (
        lax.all_gather(w_query, "dp", axis=0, tiled=True),
        lax.all_gather(w_key, "dp", axis=0, tiled=True),
        lax.all_gather(w_value, "dp", axis=0, tiled=True),
        lax.all_gather(w_out_gate, "dp", axis=0, tiled=True),
        lax.all_gather(w_decay, "dp", axis=0, tiled=True),
        lax.all_gather(w_beta, "dp", axis=0, tiled=True),
        lax.all_gather(w_output, "dp", axis=1, tiled=True),
    )


def fetch_ffn(w_ffn_gate, w_ffn_up, w_ffn_down):
    return (
        lax.all_gather(w_ffn_gate, "dp", axis=0, tiled=True),
        lax.all_gather(w_ffn_up, "dp", axis=0, tiled=True),
        lax.all_gather(w_ffn_down, "dp", axis=1, tiled=True),
    )


def branch_rows(left, right):
    return lax.psum_scatter(
        jnp.dot(left, right, preferred_element_type=jnp.float32),
        "tensor",
        scatter_dimension=0,
        tiled=True,
    )


def back_rows(pairs, rows):
    total = jnp.zeros((lax.axis_size("tensor") * rows, pairs[0][1].shape[0]), jnp.float32)
    for grad_part, weight in pairs:
        total = total + lax.dot_general(
            grad_part, weight, (((1,), (1,)), ((), ())), preferred_element_type=jnp.float32
        )
    return lax.psum_scatter(total, "tensor", scatter_dimension=0, tiled=True)


def contract_rows(left, right):
    return lax.dot_general(
        left, right, (((0,), (0,)), ((), ())), preferred_element_type=jnp.float32
    )


def times_transposed(left, right):
    return lax.dot_general(
        left, right, (((1,), (1,)), ((), ())), preferred_element_type=jnp.float32
    )


def own_rows(grad, dim):
    return lax.psum_scatter(
        grad.astype(jnp.bfloat16), "dp", scatter_dimension=dim, tiled=True
    ).astype(jnp.float32)


def norm_back(values, inverse, gain, incoming):
    scaled = incoming * gain
    width = values.shape[1]
    grad_values = (
        inverse * scaled
        - values
        * inverse
        * inverse
        * inverse
        * jnp.sum(scaled * values, axis=1, keepdims=True)
        / width
    )
    grad_gain = jnp.sum(incoming * values * inverse, axis=0)
    return (grad_values, grad_gain)


def place_slice(local, whole, rank, axis):
    return lax.dynamic_update_slice_in_dim(
        jnp.zeros_like(whole), local, rank * local.shape[axis], axis
    )


def shards(
    inputs,
    lengths,
    cotangent,
    norm_attn,
    norm_ffn,
    norm_heads,
    w_query,
    w_key,
    w_value,
    w_out_gate,
    w_decay,
    w_beta,
    w_output,
    conv_query,
    conv_key,
    conv_value,
    decay_log,
    decay_bias,
    w_ffn_gate,
    w_ffn_up,
    w_ffn_down,
):
    rows = inputs.shape[0]
    width = inputs.shape[1]
    tensor_rank = lax.axis_index("tensor")
    positions = tensor_rank * rows + jnp.arange(rows, dtype=jnp.int32)
    valid = (positions < lengths[0]).astype(jnp.float32)[:, None]
    stream_in = inputs.astype(jnp.float32)
    inverse_in = lax.rsqrt(jnp.mean(stream_in * stream_in, axis=1, keepdims=True) + 1e-06)
    normed_in = (stream_in * inverse_in * norm_attn).astype(jnp.bfloat16)
    full_in = spread_rows(normed_in)
    query_full, key_full, value_full, gate_full, decay_full, beta_full, output_full = (
        fetch_attention(w_query, w_key, w_value, w_out_gate, w_decay, w_beta, w_output)
    )
    query_proj = jnp.dot(full_in, query_full, preferred_element_type=jnp.float32)
    key_proj = jnp.dot(full_in, key_full, preferred_element_type=jnp.float32)
    value_proj = jnp.dot(full_in, value_full, preferred_element_type=jnp.float32)
    gate_proj = jnp.dot(full_in, gate_full, preferred_element_type=jnp.float32)
    decay_proj = jnp.dot(full_in, decay_full, preferred_element_type=jnp.float32)
    beta_proj = jnp.dot(full_in, beta_full, preferred_element_type=jnp.float32)
    heads_here = decay_full.shape[1]
    conv_query_here = lax.dynamic_slice_in_dim(
        conv_query, tensor_rank * query_full.shape[1], query_full.shape[1], 1
    )
    conv_key_here = lax.dynamic_slice_in_dim(
        conv_key, tensor_rank * key_full.shape[1], key_full.shape[1], 1
    )
    conv_value_here = lax.dynamic_slice_in_dim(
        conv_value, tensor_rank * value_full.shape[1], value_full.shape[1], 1
    )
    decay_log_here = lax.dynamic_slice_in_dim(decay_log, tensor_rank * heads_here, heads_here, 0)
    decay_bias_here = lax.dynamic_slice_in_dim(decay_bias, tensor_rank * heads_here, heads_here, 0)
    front_values, front_pullback = jax.vjp(
        mixer_front,
        query_proj,
        key_proj,
        value_proj,
        conv_query_here,
        conv_key_here,
        conv_value_here,
    )
    query_low, key_low, value_low = (part.astype(jnp.bfloat16) for part in front_values)
    (beta, running), decay_pullback = jax.vjp(
        decay_terms, decay_proj, beta_proj, decay_log_here, decay_bias_here
    )
    running_rows = jnp.moveaxis(running.reshape(-1, CHUNK, heads_here), 1, 2)
    delta_args = (query_low, key_low, value_low, beta, running, running_rows)
    heads_out, written, inverse, states = delta_fwd(*delta_args, NC=2)
    mixer_value, gated_pullback = jax.vjp(gated_heads, heads_out, gate_proj, norm_heads)
    mixer = mixer_value.astype(jnp.bfloat16)
    branch_attn = branch_rows(mixer, output_full)
    stream = stream_in + branch_attn
    inverse_mid = lax.rsqrt(jnp.mean(stream * stream, axis=1, keepdims=True) + 1e-06)
    normed_mid = (stream * inverse_mid * norm_ffn).astype(jnp.bfloat16)
    full_mid = spread_rows(normed_mid)
    gate_ffn, up_ffn, down_ffn = fetch_ffn(w_ffn_gate, w_ffn_up, w_ffn_down)
    ffn_gate = jnp.dot(full_mid, gate_ffn, preferred_element_type=jnp.float32)
    ffn_up = jnp.dot(full_mid, up_ffn, preferred_element_type=jnp.float32)
    sigma = jax.nn.sigmoid(ffn_gate)
    silu_gate = ffn_gate * sigma
    hidden = (silu_gate * ffn_up).astype(jnp.bfloat16)
    branch_ffn = branch_rows(hidden, down_ffn)
    outputs = (valid * (stream + branch_ffn)).astype(jnp.bfloat16)
    sum_inputs = jnp.sum(valid * stream_in * stream_in)
    sum_attn = jnp.sum(valid * branch_attn * branch_attn)
    sum_ffn = jnp.sum(valid * branch_ffn * branch_ffn)
    count_here = jnp.sum(valid)
    stat_sums = lax.psum((sum_inputs, sum_attn, sum_ffn, count_here), ("dp", "tensor"))
    grad_out = valid * cotangent.astype(jnp.float32)
    grad_ffn = spread_grads(grad_out.astype(jnp.bfloat16))
    grad_hidden = times_transposed(grad_ffn, down_ffn)
    grad_gate_in = (grad_hidden * ffn_up * sigma * (1.0 + ffn_gate * (1.0 - sigma))).astype(
        jnp.bfloat16
    )
    grad_up_in = (grad_hidden * silu_gate).astype(jnp.bfloat16)
    grad_mid = back_rows(((grad_gate_in, gate_ffn), (grad_up_in, up_ffn)), rows)
    grad_down = contract_rows(hidden, grad_ffn)
    grad_gate_weight = contract_rows(full_mid, grad_gate_in)
    grad_up_weight = contract_rows(full_mid, grad_up_in)
    owned_gate, owned_up, owned_down = (
        own_rows(grad_gate_weight, 0),
        own_rows(grad_up_weight, 0),
        own_rows(grad_down, 1),
    )
    grad_through, grad_norm_ffn = norm_back(stream, inverse_mid, norm_ffn, grad_mid)
    grad_stream = grad_out + grad_through
    grad_attn = spread_grads(grad_stream.astype(jnp.bfloat16))
    grad_output_weight = contract_rows(mixer, grad_attn)
    grad_mixer = times_transposed(grad_attn, output_full)
    grad_heads, grad_gate, heads_gain_grad = gated_pullback(grad_mixer)
    grad_query, grad_key, grad_value, grad_beta, grad_run, grad_run_rows = delta_bwd(
        *delta_args, written, inverse, states, grad_heads, NC=1
    )
    grad_run = grad_run - jnp.moveaxis(grad_run_rows, 1, 2).reshape(grad_run.shape)
    grad_decay, grad_beta_in, grad_decay_log, grad_decay_bias = decay_pullback((grad_beta, grad_run))
    front_grads = front_pullback((grad_query, grad_key, grad_value))
    grad_query_proj = front_grads[0].astype(jnp.bfloat16)
    grad_key_proj = front_grads[1].astype(jnp.bfloat16)
    grad_value_proj = front_grads[2].astype(jnp.bfloat16)
    grad_gate_proj = grad_gate.astype(jnp.bfloat16)
    grad_decay_proj = grad_decay.astype(jnp.bfloat16)
    grad_beta_proj = grad_beta_in.astype(jnp.bfloat16)
    grad_query_weight = contract_rows(full_in, grad_query_proj)
    grad_key_weight = contract_rows(full_in, grad_key_proj)
    grad_value_weight = contract_rows(full_in, grad_value_proj)
    grad_gate_weight_attn = contract_rows(full_in, grad_gate_proj)
    grad_decay_weight = contract_rows(full_in, grad_decay_proj)
    grad_beta_weight = contract_rows(full_in, grad_beta_proj)
    grad_normed = back_rows(
        (
            (grad_query_proj, query_full),
            (grad_key_proj, key_full),
            (grad_value_proj, value_full),
            (grad_gate_proj, gate_full),
            (grad_decay_proj, decay_full),
            (grad_beta_proj, beta_full),
        ),
        rows,
    )
    owned_query, owned_key, owned_value, owned_out_gate, owned_decay, owned_beta, owned_output = (
        own_rows(grad_query_weight, 0),
        own_rows(grad_key_weight, 0),
        own_rows(grad_value_weight, 0),
        own_rows(grad_gate_weight_attn, 0),
        own_rows(grad_decay_weight, 0),
        own_rows(grad_beta_weight, 0),
        own_rows(grad_output_weight, 1),
    )
    grad_through_in, grad_norm_attn = norm_back(stream_in, inverse_in, norm_attn, grad_normed)
    grad_inputs = grad_stream + grad_through_in
    conv_query_grad = place_slice(front_grads[3], conv_query, tensor_rank, 1)
    conv_key_grad = place_slice(front_grads[4], conv_key, tensor_rank, 1)
    conv_value_grad = place_slice(front_grads[5], conv_value, tensor_rank, 1)
    decay_log_grad = place_slice(grad_decay_log, decay_log, tensor_rank, 0)
    decay_bias_grad = place_slice(grad_decay_bias, decay_bias, tensor_rank, 0)
    (
        total_attn_gain,
        total_ffn_gain,
        total_heads_gain,
        total_conv_query,
        total_conv_key,
        total_conv_value,
        total_decay_log,
        total_decay_bias,
    ) = lax.psum(
        (
            grad_norm_attn,
            grad_norm_ffn,
            heads_gain_grad,
            conv_query_grad,
            conv_key_grad,
            conv_value_grad,
            decay_log_grad,
            decay_bias_grad,
        ),
        ("dp", "tensor"),
    )
    denominator = stat_sums[3] * width
    statistics = jnp.sqrt(jnp.stack([stat_sums[0], stat_sums[1], stat_sums[2]]) / denominator)
    return (
        outputs,
        statistics,
        grad_inputs,
        total_attn_gain,
        total_ffn_gain,
        total_heads_gain,
        owned_query,
        owned_key,
        owned_value,
        owned_out_gate,
        owned_decay,
        owned_beta,
        owned_output,
        total_conv_query,
        total_conv_key,
        total_conv_value,
        total_decay_log,
        total_decay_bias,
        owned_gate,
        owned_up,
        owned_down,
    )


def solution(mesh):
    in_specs = (
        P(("dp", "tensor"), None),
        P("dp"),
        P(("dp", "tensor"), None),
        P(),
        P(),
        P(),
        P("dp", "tensor"),
        P("dp", "tensor"),
        P("dp", "tensor"),
        P("dp", "tensor"),
        P("dp", "tensor"),
        P("dp", "tensor"),
        P("tensor", "dp"),
        P(),
        P(),
        P(),
        P(),
        P(),
        P("dp", "tensor"),
        P("dp", "tensor"),
        P("tensor", "dp"),
    )
    out_specs = (
        P(("dp", "tensor"), None),
        P(),
        P(("dp", "tensor"), None),
        P(),
        P(),
        P(),
        P("dp", "tensor"),
        P("dp", "tensor"),
        P("dp", "tensor"),
        P("dp", "tensor"),
        P("dp", "tensor"),
        P("dp", "tensor"),
        P("tensor", "dp"),
        P(),
        P(),
        P(),
        P(),
        P(),
        P("dp", "tensor"),
        P("dp", "tensor"),
        P("tensor", "dp"),
    )
    return jax.shard_map(shards, mesh=mesh, in_specs=in_specs, out_specs=out_specs, check_vma=False)
```

```python
import functools

import jax
import jax.numpy as jnp
from jax import lax
from jax.experimental import pallas as pl
from jax.experimental.pallas import tpu as pltpu
from jax.sharding import PartitionSpec as P

BF=jnp.bfloat16; F32=jnp.float32
DK = 128
CHUNK = 128
HALO = 8


def dot1(a, b, ca=1, cb=0):
    return lax.dot_general(a, b, (((ca,), (cb,)), ((), ())), preferred_element_type=F32)


def split(a):
    if a.dtype == BF:
        return a, None
    high = a.astype(BF)
    return high, (a - high.astype(F32)).astype(BF)


def mm(a, b, ca=1, cb=0):
    a_high, a_low = a if isinstance(a, tuple) else split(a)
    b_high, b_low = b if isinstance(b, tuple) else split(b)
    total = dot1(a_high, b_high, ca, cb)
    if b_low is not None:
        total = total + dot1(a_high, b_low, ca, cb)
    if a_low is not None:
        total = total + dot1(a_low, b_high, ca, cb)
    return total


def exact_sum(ones, values, ca):
    high, rest = split(values)
    middle, low = split(values - high.astype(F32))
    return dot1(ones, high, ca) + (dot1(ones, middle, ca) + dot1(ones, low, ca))


def grids(size):
    return (
        lax.broadcasted_iota(jnp.int32, (size, size), 0),
        lax.broadcasted_iota(jnp.int32, (size, size), 1),
    )


def inverses(couplings):
    size = couplings[0].shape[0]
    i, j = grids(size)
    eye = jnp.where(i == j, 1.0, 0.0).astype(F32)

    def same(bits):
        return lax.shift_right_logical(i, bits) == lax.shift_right_logical(j, bits)

    inside = same(3)
    near = [jnp.where(inside, a, 0.0) for a in couplings]
    second = [split(mm(a, a)) for a in map(split, near)]
    fourth = [mm(a, a) for a in second]
    found = [eye - a for a in near]
    found = [x + mm(x, a) for x, a in zip(found, second)]
    found = [x + mm(x, a) for x, a in zip(found, fourth)]
    bits = 3
    while (1 << bits) < size:
        across = jnp.logical_and(same(bits + 1), jnp.logical_not(same(bits)))
        parts = [split(x) for x in found]
        moved = [mm(jnp.where(across, a, 0.0), x) for a, x in zip(couplings, parts)]
        found = [x - mm(p, y) for x, p, y in zip(found, parts, moved)]
        bits += 1
    return found


def conv_of(taps_ref, ext, columns, rows, start=HALO - 3):
    total = taps_ref[0:1, columns] * ext[start : start + rows, columns]
    for tap in range(1, 4):
        total = total + taps_ref[tap : tap + 1, columns] * ext[
            start + tap : start + tap + rows, columns
        ]
    return total


def decay_of(tail, par_ref):
    i, j = grids(CHUNK)
    ones = jnp.where(i >= j, 1.0, 0.0).astype(BF)
    raised = tail + par_ref[1:2, :]
    log_decay = par_ref[0:1, :] * (
        jnp.maximum(raised, 0.0) + jnp.log1p(jnp.exp(-jnp.abs(raised)))
    )
    return exact_sum(ones, log_decay, 1), log_decay, jax.nn.sigmoid(tail), raised


def fwd_kernel(H, DV, NC, p_ref, taps_ref, par_ref, o_ref, u_ref, t_ref, s_ref, S, ext):
    C = CHUNK
    R = NC * C
    W = H * (2 * DK + DV)

    @pl.when(pl.program_id(0) == 0)
    def _():
        S[...] = jnp.zeros_like(S)
        ext[0:HALO, :] = jnp.zeros((HALO, W), F32)

    @pl.when(pl.program_id(0) > 0)
    def _():
        ext[0:HALO, :] = ext[R : R + HALO, :]

    ext[HALO : HALO + R, :] = p_ref[:, 0:W]
    i, j = grids(C)
    low, strict = i >= j, i > j
    idx = [(c, h) for c in range(NC) for h in range(H)]
    rows = [slice(c * C, (c + 1) * C) for c in range(NC)]
    q, k, v, b, g, gr = {}, {}, {}, {}, {}, {}
    for h in range(H):
        for part, out, base, size, factor in (
            (0, q, h * DK, DK, DK**-0.5),
            (1, k, H * DK + h * DK, DK, 1.0),
            (2, v, 2 * H * DK + h * DV, DV, None),
        ):
            mixed = conv_of(taps_ref, ext, slice(base, base + size), R)
            mixed = mixed * jax.nn.sigmoid(mixed)
            if factor is not None:
                mixed = mixed * (
                    lax.rsqrt(jnp.sum(mixed * mixed, axis=1, keepdims=True) + 1e-06) * factor
                )
            mixed = mixed.astype(BF)
            for c in range(NC):
                out[c, h] = mixed[rows[c], :]
    for c in range(NC):
        running, _, beta, _ = decay_of(p_ref[rows[c], W : W + 128], par_ref)
        across = jnp.transpose(running)
        for h in range(H):
            b[c, h] = beta[:, H + h : H + h + 1]
            g[c, h] = running[:, h : h + 1]
            gr[c, h] = across[h : h + 1, :]
    D = {x: jnp.exp(jnp.where(low, g[x] - gr[x], -1e30)) for x in idx}
    A = [jnp.where(strict, dot1(k[x], k[x], 1, 1) * b[x] * D[x], 0.0) for x in idx]
    T = dict(zip(idx, inverses(A)))
    P = {x: dot1(q[x], k[x], 1, 1) * D[x] for x in idx}
    gam = {x: jnp.exp(g[x]) for x in idx}
    Ts = {x: split(T[x]) for x in idx}
    TV = {x: mm(Ts[x], b[x] * v[x].astype(F32)) for x in idx}
    TK = {x: mm(Ts[x], b[x] * gam[x] * k[x].astype(F32)) for x in idx}
    for c in range(NC):
        for h in range(H):
            x = (c, h)
            t_ref[rows[c], h * C : (h + 1) * C] = T[x]
            S0 = S[h * DK : (h + 1) * DK, :]
            s_ref[c, h * DK : (h + 1) * DK, :] = S0
            Ss = split(S0)
            U = TV[x] - mm(TK[x], Ss)
            Us = split(U)
            u_ref[rows[c], h * DV : (h + 1) * DV] = U
            o_ref[rows[c], h * DV : (h + 1) * DV] = gam[x] * mm(q[x], Ss) + mm(P[x], Us)
            last = gr[x][:, C - 1 : C]
            S[h * DK : (h + 1) * DK, :] = jnp.exp(last) * S0 + mm(
                k[x].astype(F32) * jnp.exp(last - g[x]), Us, 0, 0
            )


def bwd_kernel(
    H, DV, steps, p_ref, halo_ref, taps_ref, par_ref, u_ref, t_ref, s_ref, do_ref,
    dp_ref, dtaps_ref, dpar_ref, dS, ext, dext,
):
    C = CHUNK
    W = H * (2 * DK + DV)
    step = pl.program_id(0)

    @pl.when(step == 0)
    def _():
        dS[...] = jnp.zeros_like(dS)
        dext[C : C + HALO, :] = jnp.zeros((HALO, W), F32)
        dtaps_ref[...] = jnp.zeros_like(dtaps_ref)
        dpar_ref[...] = jnp.zeros_like(dpar_ref)

    @pl.when(step > 0)
    def _():
        dext[C : C + HALO, :] = dext[0:HALO, :]

    @pl.when(step == steps - 1)
    def _():
        ext[0:HALO, :] = jnp.zeros((HALO, W), F32)

    @pl.when(step < steps - 1)
    def _():
        ext[0:HALO, :] = halo_ref[:, 0:W]

    ext[HALO : HALO + C, :] = p_ref[:, 0:W]
    i, j = grids(C)
    low, strict = i >= j, i > j
    lane = lax.broadcasted_iota(jnp.int32, (C, 128), 1)
    last_row = lax.broadcasted_iota(jnp.int32, (C, 1), 0) == C - 1
    tail = p_ref[:, W : W + 128]
    running, log_decay, beta, raised = decay_of(tail, par_ref)
    across = jnp.transpose(running)
    d_running = jnp.zeros((C, 128), F32)
    d_beta = jnp.zeros((C, 128), F32)

    def gradient_in(columns, mixed, sig, d_act):
        dext[0:C, columns] = d_act * sig * (1.0 + mixed * (1.0 - sig))

    for h in range(H):
        q_columns = slice(h * DK, (h + 1) * DK)
        k_columns = slice(H * DK + h * DK, H * DK + (h + 1) * DK)
        v_columns = slice(2 * H * DK + h * DV, 2 * H * DK + (h + 1) * DV)
        q_mixed = conv_of(taps_ref, ext, q_columns, C)
        k_mixed = conv_of(taps_ref, ext, k_columns, C)
        v_mixed = conv_of(taps_ref, ext, v_columns, C)
        q_sig, k_sig, v_sig = (jax.nn.sigmoid(x) for x in (q_mixed, k_mixed, v_mixed))
        q_act, k_act = q_mixed * q_sig, k_mixed * k_sig
        q_inv = lax.rsqrt(jnp.sum(q_act * q_act, axis=1, keepdims=True) + 1e-06)
        k_inv = lax.rsqrt(jnp.sum(k_act * k_act, axis=1, keepdims=True) + 1e-06)
        q = (q_act * (q_inv * DK**-0.5)).astype(BF)
        k = (k_act * k_inv).astype(BF)
        v = (v_mixed * v_sig).astype(BF)
        b, g, gr = beta[:, H + h : H + h + 1], running[:, h : h + 1], across[h : h + 1, :]
        hv = slice(h * DV, (h + 1) * DV)
        hk = slice(h * DK, (h + 1) * DK)
        U = split(u_ref[:, hv])
        T = split(t_ref[:, h * C : (h + 1) * C])
        S0 = s_ref[0, hk, :]
        Ss = split(S0)
        dO = split(do_ref[:, hv])
        qf, kf = q.astype(F32), k.astype(F32)
        D = jnp.exp(jnp.where(low, g - gr, -1e30))
        kk, qk = dot1(k, k, 1, 1), dot1(q, k, 1, 1)
        bD = b * D
        A, P = jnp.where(strict, kk * bD, 0.0), qk * D
        last = gr[:, C - 1 : C]
        gam, e, G = jnp.exp(g), jnp.exp(last - g), jnp.exp(last)
        dS1 = dS[hk, :]
        dSs = split(dS1)
        dU = mm(P, dO, 0, 0) + mm(kf * e, dSs)
        dR = mm(T, dU, 0, 0)
        dRs = split(dR)
        dS[hk, :] = G * dS1 + mm(qf * gam, dO, 0, 0) - mm(kf * (b * gam), dRs, 0, 0)
        dP = jnp.where(low, mm(dO, U, 1, 1), 0.0)
        dA = jnp.where(strict, -mm(dRs, U, 1, 1), 0.0)
        Rb = v.astype(F32) - gam * mm(k, Ss)
        db = jnp.sum(dR * Rb, axis=1, keepdims=True) + jnp.sum(dA * kk * D, axis=1, keepdims=True)
        dOS = gam * mm(dO, Ss, 1, 1)
        dRS = (b * gam) * mm(dRs, Ss, 1, 1)
        UdS = e * mm(U, dSs, 1, 1)
        M1, M2 = split(dP * D), split(dA * bD)
        dq = dOS + mm(M1, k)
        dk = UdS - dRS + mm(M1, q, 0, 0) + mm(M2, k) + mm(M2, k, 0, 0)
        X = dP * P + dA * A
        uk = jnp.sum(UdS * kf, axis=1, keepdims=True)
        total = jnp.sum(uk, axis=0, keepdims=True) + G * jnp.sum(
            jnp.sum(S0 * dS1, axis=1, keepdims=True), axis=0, keepdims=True
        )
        dg = (
            jnp.sum(dOS * qf - dRS * kf + X - jnp.transpose(X), axis=1, keepdims=True)
            - uk
            + jnp.where(last_row, total, 0.0)
        )
        d_running = jnp.where(lane == h, dg, d_running)
        d_beta = jnp.where(lane == H + h, db, d_beta)
        q_in = jnp.sum(dq * q_act, axis=1, keepdims=True) * (q_inv * q_inv)
        gradient_in(q_columns, q_mixed, q_sig, (q_inv * DK**-0.5) * (dq - q_act * q_in))
        k_in = jnp.sum(dk * k_act, axis=1, keepdims=True) * (k_inv * k_inv)
        gradient_in(k_columns, k_mixed, k_sig, k_inv * (dk - k_act * k_in))
        gradient_in(v_columns, v_mixed, v_sig, b * dR)
    for start in range(0, W, 512):
        columns = slice(start, start + 512)
        here = dext[0:C, columns]
        total = taps_ref[3:4, columns] * here
        dtaps_ref[3:4, columns] += jnp.sum(
            here * ext[HALO : HALO + C, columns], axis=0, keepdims=True
        )
        for tap in range(3):
            total = total + taps_ref[tap : tap + 1, columns] * dext[3 - tap : 3 - tap + C, columns]
            dtaps_ref[tap : tap + 1, columns] += jnp.sum(
                here * ext[HALO - 3 + tap : HALO - 3 + tap + C, columns], axis=0, keepdims=True
            )
        dp_ref[:, columns] = total.astype(BF)
    ones = jnp.where(i >= j, 1.0, 0.0).astype(BF)
    d_log = exact_sum(ones, d_running, 0)
    d_raised = d_log * par_ref[0:1, :] * jax.nn.sigmoid(raised)
    d_tail = d_raised + d_beta * beta * (1.0 - beta)
    dp_ref[:, W : W + 128] = d_tail.astype(BF)
    dpar_ref[0:1, :] += jnp.sum(d_log * log_decay, axis=0, keepdims=True)
    dpar_ref[1:2, :] += jnp.sum(d_raised, axis=0, keepdims=True)


LIMIT = pltpu.CompilerParams(vmem_limit_bytes=56 * 2**20)


def row_block(rows, width, at=lambda s: s):
    return pl.BlockSpec((rows, width), lambda s: (at(s), 0))


def whole_block(array):
    return pl.BlockSpec(array.shape, lambda s: (0,) * array.ndim)


def mixer_fwd(projected, taps, par, heads, NC=2):
    L, wide = projected.shape
    H, C = heads, CHUNK
    DV = taps.shape[1] // H - 2 * DK
    f = jax.ShapeDtypeStruct
    return pl.pallas_call(
        functools.partial(fwd_kernel, H, DV, NC),
        grid=(L // C // NC,),
        in_specs=[row_block(NC * C, wide), whole_block(taps), whole_block(par)],
        out_specs=[
            row_block(NC * C, H * DV),
            row_block(NC * C, H * DV),
            row_block(NC * C, H * C),
            pl.BlockSpec((NC, H * DK, DV), lambda s: (s, 0, 0)),
        ],
        out_shape=[
            f((L, H * DV), F32), f((L, H * DV), F32), f((L, H * C), F32), f((L // C, H * DK, DV), F32),
        ],
        scratch_shapes=[pltpu.VMEM((H * DK, DV), F32), pltpu.VMEM((NC * C + HALO, taps.shape[1]), F32)],
        compiler_params=LIMIT,
        cost_estimate=pl.CostEstimate(flops=35 * 10**9, bytes_accessed=30 * 2**20, transcendentals=0),
        name="mixer_fwd",
    )(projected, taps, par)


def mixer_bwd(projected, taps, par, written, inverse, states, grad_heads, heads):
    L, wide = projected.shape
    H, C = heads, CHUNK
    DV = taps.shape[1] // H - 2 * DK
    W = taps.shape[1]
    n = L // C
    f = jax.ShapeDtypeStruct

    def back(s):
        return n - 1 - s

    return pl.pallas_call(
        functools.partial(bwd_kernel, H, DV, n),
        grid=(n,),
        in_specs=[
            row_block(C, wide, back),
            row_block(HALO, wide, lambda s: jnp.maximum(back(s) * (C // HALO) - 1, 0)),
            whole_block(taps),
            whole_block(par),
            row_block(C, H * DV, back),
            row_block(C, H * C, back),
            pl.BlockSpec((1, H * DK, DV), lambda s: (back(s), 0, 0)),
            row_block(C, H * DV, back),
        ],
        out_specs=[row_block(C, wide, back), whole_block(taps), whole_block(par)],
        out_shape=[f((L, wide), BF), f(taps.shape, F32), f(par.shape, F32)],
        scratch_shapes=[
            pltpu.VMEM((H * DK, DV), F32),
            pltpu.VMEM((C + HALO, W), F32),
            pltpu.VMEM((C + HALO, W), F32),
        ],
        compiler_params=LIMIT,
        cost_estimate=pl.CostEstimate(flops=55 * 10**9, bytes_accessed=36 * 2**20, transcendentals=0),
        name="mixer_bwd",
    )(projected, projected, taps, par, written, inverse, states, grad_heads)


def gate_fwd_kernel(DV, o_ref, gate_ref, gain_ref, out_ref):
    for start in range(0, o_ref.shape[1], DV):
        cut = slice(start, start + DV)
        heads, gate = o_ref[:, cut], gate_ref[:, cut]
        inverse = lax.rsqrt(jnp.mean(heads * heads, axis=1, keepdims=True) + 1e-05)
        out_ref[:, cut] = (heads * inverse * gain_ref[...] * (gate * jax.nn.sigmoid(gate))).astype(BF)


def gate_fwd(heads_out, gate_proj, gain):
    L, width = heads_out.shape
    rows = L // 8
    return pl.pallas_call(
        functools.partial(gate_fwd_kernel, gain.shape[1]),
        grid=(8,),
        in_specs=[row_block(rows, width), row_block(rows, width), whole_block(gain)],
        out_specs=row_block(rows, width),
        out_shape=jax.ShapeDtypeStruct((L, width), BF),
        cost_estimate=pl.CostEstimate(flops=5 * 10**9, bytes_accessed=10 * 2**20, transcendentals=0),
        name="gate_fwd",
    )(heads_out, gate_proj, gain)


def gate_bwd_kernel(DV, o_ref, gate_ref, gain_ref, in_ref, do_ref, dgate_ref, dgain_ref):
    @pl.when(pl.program_id(0) == 0)
    def _():
        dgain_ref[...] = jnp.zeros_like(dgain_ref)

    for start in range(0, o_ref.shape[1], DV):
        cut = slice(start, start + DV)
        heads, gate, grad = o_ref[:, cut], gate_ref[:, cut], in_ref[:, cut]
        inverse = lax.rsqrt(jnp.mean(heads * heads, axis=1, keepdims=True) + 1e-05)
        normed = heads * inverse
        sig = jax.nn.sigmoid(gate)
        dgate_ref[:, cut] = (
            grad * (normed * gain_ref[...]) * (sig * (1.0 + gate * (1.0 - sig)))
        ).astype(BF)
        d_scaled = grad * (gate * sig)
        dgain_ref[...] += jnp.sum(d_scaled * normed, axis=0, keepdims=True)
        d_normed = d_scaled * gain_ref[...]
        do_ref[:, cut] = inverse * (
            d_normed - normed * jnp.mean(d_normed * normed, axis=1, keepdims=True)
        )


def gate_bwd(heads_out, gate_proj, gain, grad_mixer):
    L, width = heads_out.shape
    rows = L // 8
    f = jax.ShapeDtypeStruct
    return pl.pallas_call(
        functools.partial(gate_bwd_kernel, gain.shape[1]),
        grid=(8,),
        in_specs=[row_block(rows, width), row_block(rows, width), whole_block(gain), row_block(rows, width)],
        out_specs=[row_block(rows, width), row_block(rows, width), whole_block(gain)],
        out_shape=[f((L, width), F32), f((L, width), BF), f(gain.shape, F32)],
        cost_estimate=pl.CostEstimate(flops=7 * 10**9, bytes_accessed=18 * 2**20, transcendentals=0),
        name="gate_bwd",
    )(heads_out, gate_proj, gain, grad_mixer)


def at_place(place, n):
    return jnp.where(place < n // 2, 2 * place, 2 * (n - place) - 1)


def place_of(index, n):
    return jnp.where(index % 2 == 0, index // 2, n - (index + 1) // 2)


def ring_pairs(n):
    order = list(range(0, n, 2)) + list(range(n - 1, 0, -2))
    ahead = [(order[i], order[(i + 1) % n]) for i in range(n)]
    return ahead, [(d, s) for s, d in ahead]


def to_relative(array):
    n = lax.axis_size("dp")
    block = array.shape[-1] // n
    place = place_of(lax.axis_index("dp"), n)
    return jnp.concatenate(
        [
            lax.dynamic_slice_in_dim(
                array, at_place((place - d + n) % n, n) * block, block, array.ndim - 1
            )
            for d in range(n)
        ],
        axis=-1,
    )


def to_absolute(array):
    n = lax.axis_size("dp")
    block = array.shape[-1] // n
    place = place_of(lax.axis_index("dp"), n)
    return jnp.concatenate(
        [
            lax.dynamic_slice_in_dim(
                array,
                ((place - place_of(jnp.int32(index), n) + n) % n) * block,
                block,
                array.ndim - 1,
            )
            for index in range(n)
        ],
        axis=-1,
    )


def after(array, other):
    return lax.optimization_barrier((array, other))[0]


def ring_gather(shard, earlier=None, hops=0):
    n = lax.axis_size("dp")
    ahead, behind = ring_pairs(n)
    half = shard.shape[0] // 2
    if earlier is not None:
        shard = after(shard, earlier[min(hops, n - 1)][0])
    first, second = [shard[:half]], [shard[half:]]
    for _ in range(n - 1):
        first.append(lax.ppermute(first[-1], "dp", ahead))
        second.append(lax.ppermute(second[-1], "dp", behind))
    return [(first[d], second[(n - d) % n]) for d in range(n)]


def stacked(pieces):
    return jnp.concatenate([half for pair in pieces for half in pair], axis=0)


def side_by_side(pieces):
    return jnp.concatenate([jnp.concatenate(pair, axis=0) for pair in pieces], axis=1)


def ring_scatter(first_of, second_of, earlier=()):
    n = lax.axis_size("dp")
    ahead, behind = ring_pairs(n)
    first, second = first_of(1 % n).astype(BF), second_of(n - 1).astype(BF)
    first, second = after((first, second), earlier)
    hops = []
    for step in range(n - 1):
        first, second = lax.ppermute(first, "dp", ahead), lax.ppermute(second, "dp", behind)
        hops.append(first)
        first = first.astype(F32) + first_of((step + 2) % n)
        second = second.astype(F32) + second_of(n - 2 - step)
        if step < n - 2:
            first, second = first.astype(BF), second.astype(BF)
    return jnp.concatenate((first, second), axis=0), hops


def contract_rows(left, right):
    return lax.dot_general(
        left, right, (((0,), (0,)), ((), ())), preferred_element_type=jnp.float32
    )


def times_transposed(left, right):
    return lax.dot_general(
        left, right, (((1,), (1,)), ((), ())), preferred_element_type=jnp.float32
    )


def scatter_rows_of(features, grads, earlier=()):
    block = features.shape[1] // lax.axis_size("dp")
    half = block // 2

    def part(d, start):
        return contract_rows(features[:, d * block + start : d * block + start + half], grads)

    return ring_scatter(lambda d: part(d, 0), lambda d: part(d, half), earlier)


def scatter_columns_of(features, grads, earlier=()):
    block = grads.shape[1] // lax.axis_size("dp")
    half = features.shape[1] // 2

    def part(d, left):
        return contract_rows(left, grads[:, d * block : (d + 1) * block])

    return ring_scatter(
        lambda d: part(d, features[:, :half]), lambda d: part(d, features[:, half:]), earlier
    )


CORES = [(0, 1), (1, 0), (2, 3), (3, 2)]
PAIRS = [(0, 2), (2, 0), (1, 3), (3, 1)]


def spread_rows(block):
    if lax.axis_size("tensor") != 4:
        return lax.all_gather(block, "tensor", axis=0, tiled=True)
    rank = lax.axis_index("tensor")
    rows = block.shape[0]
    far = lax.ppermute(block, "tensor", PAIRS)
    near = lax.ppermute(block, "tensor", CORES)
    far_near = lax.ppermute(far, "tensor", CORES)
    out = jnp.zeros((4 * rows,) + block.shape[1:], block.dtype)
    for part, flip in ((block, 0), (near, 1), (far, 2), (far_near, 3)):
        out = lax.dynamic_update_slice_in_dim(out, part, (rank ^ flip) * rows, 0)
    return out


def sum_rows(product, rows):
    if lax.axis_size("tensor") != 4:
        whole = jnp.concatenate([product(i * rows) for i in range(lax.axis_size("tensor"))], axis=0)
        return lax.psum_scatter(whole, "tensor", scatter_dimension=0, tiled=True)
    rank = lax.axis_index("tensor")
    far_near = lax.ppermute(product((rank ^ 3) * rows).astype(BF), "tensor", CORES)
    far = product((rank ^ 2) * rows) + far_near.astype(F32)
    far = lax.ppermute(far.astype(BF), "tensor", PAIRS)
    near = lax.ppermute(product((rank ^ 1) * rows).astype(BF), "tensor", CORES)
    return product(rank * rows) + near.astype(F32) + far.astype(F32)


def branch_rows(left, right, rows):
    return sum_rows(
        lambda start: jnp.dot(
            lax.dynamic_slice_in_dim(left, start, rows, 0), right, preferred_element_type=F32
        ),
        rows,
    )


def back_rows(pairs, rows):
    def product(start):
        total = None
        for grads, weight in pairs:
            part = times_transposed(lax.dynamic_slice_in_dim(grads, start, rows, 0), weight)
            total = part if total is None else total + part
        return total

    return sum_rows(product, rows)


def sum_over(values, axis):
    n = lax.axis_size(axis)
    if n & (n - 1):
        return lax.psum(values, axis)
    step = 1
    while step < n:
        values = values + lax.ppermute(values, axis, [(i, i ^ step) for i in range(n)])
        step *= 2
    return values


def packed(arrays):
    flat = jnp.concatenate([a.reshape(-1) for a in arrays])
    pad = -flat.shape[0] % 1024
    return jnp.pad(flat, (0, pad)).reshape(-1, 128)


def unpacked(values, shapes):
    flat = values.reshape(-1)
    out, start = [], 0
    for shape in shapes:
        size = 1
        for extent in shape:
            size *= extent
        out.append(flat[start : start + size].reshape(shape))
        start += size
    return out


def norm_back(values, inverse, gain, incoming):
    scaled = incoming * gain
    width = values.shape[1]
    grad_values = (
        inverse * scaled
        - values
        * inverse
        * inverse
        * inverse
        * jnp.sum(scaled * values, axis=1, keepdims=True)
        / width
    )
    grad_gain = jnp.sum(incoming * values * inverse, axis=0)
    return (grad_values, grad_gain)


def place_slice(local, whole, rank, axis):
    return lax.dynamic_update_slice_in_dim(
        jnp.zeros_like(whole), local, rank * local.shape[axis], axis
    )


def columns(array, widths):
    out, start = [], 0
    for width in widths:
        out.append(array[:, start : start + width])
        start += width
    return out


def shards(
    inputs,
    lengths,
    cotangent,
    norm_attn,
    norm_ffn,
    norm_heads,
    w_query,
    w_key,
    w_value,
    w_out_gate,
    w_decay,
    w_beta,
    w_output,
    conv_query,
    conv_key,
    conv_value,
    decay_log,
    decay_bias,
    w_ffn_gate,
    w_ffn_up,
    w_ffn_down,
):
    rows = inputs.shape[0]
    width = inputs.shape[1]
    tensor_rank = lax.axis_index("tensor")
    positions = tensor_rank * rows + jnp.arange(rows, dtype=jnp.int32)
    valid = (positions < lengths[0]).astype(jnp.float32)[:, None]
    heads_here = w_decay.shape[1]
    widths = [w.shape[1] for w in (w_query, w_key, w_value, w_decay, w_beta)]
    fill = -sum(widths) % 128
    mixed_shard = jnp.pad(
        jnp.concatenate((w_query, w_key, w_value, w_decay, w_beta), axis=1), ((0, 0), (0, fill))
    )
    ffn_width = w_ffn_gate.shape[1]
    mixed_ring = ring_gather(mixed_shard)
    gate_ring = ring_gather(w_out_gate, mixed_ring, 6)
    output_ring = ring_gather(w_output, mixed_ring, 7)
    ffn_ring = ring_gather(jnp.concatenate((w_ffn_gate, w_ffn_up), axis=1), gate_ring, 6)
    down_ring = ring_gather(w_ffn_down, ffn_ring, 6)
    mixed_full, gate_full, ffn_full = stacked(mixed_ring), stacked(gate_ring), stacked(ffn_ring)
    output_full, down_full = side_by_side(output_ring), side_by_side(down_ring)

    gain_attn = to_relative(norm_attn)
    gain_ffn = to_relative(norm_ffn)
    stream_in = to_relative(inputs).astype(jnp.float32)
    grad_out = valid * to_relative(cotangent).astype(jnp.float32)
    inverse_in = lax.rsqrt(jnp.mean(stream_in * stream_in, axis=1, keepdims=True) + 1e-06)
    full_in = spread_rows((stream_in * inverse_in * gain_attn).astype(jnp.bfloat16))
    grad_ffn = spread_rows(grad_out.astype(jnp.bfloat16))

    projected = jnp.dot(full_in, mixed_full, preferred_element_type=jnp.float32)
    gate_proj = jnp.dot(full_in, gate_full, preferred_element_type=jnp.float32)

    def here(array):
        size = array.shape[-1] // lax.axis_size("tensor")
        return lax.dynamic_slice_in_dim(array, tensor_rank * size, size, array.ndim - 1)

    taps = jnp.concatenate((here(conv_query), here(conv_key), here(conv_value)), axis=1)
    par = jnp.pad(
        jnp.stack((-jnp.exp(here(decay_log)), here(decay_bias))), ((0, 6), (0, 128 - heads_here))
    )
    gain_heads = norm_heads[None, :]
    heads_out, written, inverse, states = mixer_fwd(projected, taps, par, heads_here)
    mixer = gate_fwd(heads_out, gate_proj, gain_heads)
    branch_attn = branch_rows(mixer, output_full, rows)
    stream = stream_in + branch_attn
    inverse_mid = lax.rsqrt(jnp.mean(stream * stream, axis=1, keepdims=True) + 1e-06)
    full_mid = spread_rows((stream * inverse_mid * gain_ffn).astype(jnp.bfloat16))
    ffn_in = jnp.dot(full_mid, ffn_full, preferred_element_type=jnp.float32)
    ffn_gate, ffn_up = ffn_in[:, :ffn_width], ffn_in[:, ffn_width:]
    sigma = jax.nn.sigmoid(ffn_gate)
    silu_gate = ffn_gate * sigma
    hidden = (silu_gate * ffn_up).astype(jnp.bfloat16)
    branch_ffn = branch_rows(hidden, down_full, rows)
    outputs = to_absolute((valid * (stream + branch_ffn)).astype(jnp.bfloat16))
    stat_sums = jnp.stack(
        [
            jnp.sum(valid * stream_in * stream_in),
            jnp.sum(valid * branch_attn * branch_attn),
            jnp.sum(valid * branch_ffn * branch_ffn),
            jnp.sum(valid),
        ]
    )

    owned_down, down_hops = scatter_columns_of(hidden, grad_ffn)
    grad_hidden = times_transposed(grad_ffn, down_full)
    grad_gate_in = grad_hidden * ffn_up * sigma * (1.0 + ffn_gate * (1.0 - sigma))
    grad_up_in = grad_hidden * silu_gate
    grad_ffn_in = jnp.concatenate((grad_gate_in, grad_up_in), axis=1).astype(jnp.bfloat16)
    grad_mid = back_rows(((grad_ffn_in, ffn_full),), rows)
    owned_ffn, ffn_hops = scatter_rows_of(full_mid, grad_ffn_in, [down_hops[-3]])
    owned_gate, owned_up = columns(owned_ffn, [ffn_width] * 2)
    grad_through, grad_norm_ffn = norm_back(stream, inverse_mid, gain_ffn, grad_mid)
    grad_stream = grad_out + grad_through
    grad_attn = spread_rows(grad_stream.astype(jnp.bfloat16))
    grad_mixer = times_transposed(grad_attn, output_full)
    owned_output, output_hops = scatter_columns_of(mixer, grad_attn, [ffn_hops[-2]])
    grad_heads, grad_gate_proj, heads_gain_grad = gate_bwd(
        heads_out, gate_proj, gain_heads, grad_mixer
    )
    owned_out_gate, gate_hops = scatter_rows_of(full_in, grad_gate_proj, [ffn_hops[-1]])
    grad_projected, grad_taps, grad_par = mixer_bwd(
        projected, taps, par, written, inverse, states, grad_heads, heads_here
    )
    grad_normed = back_rows(((grad_gate_proj, gate_full), (grad_projected, mixed_full)), rows)
    owned_mixed, _ = scatter_rows_of(full_in, grad_projected, [output_hops[-1], gate_hops[-2]])
    owned_query, owned_key, owned_value, owned_decay, owned_beta = columns(owned_mixed, widths)
    grad_through_in, grad_norm_attn = norm_back(stream_in, inverse_in, gain_attn, grad_normed)
    grad_inputs = to_absolute(grad_stream + grad_through_in)

    local = columns(grad_taps, widths[:3]) + [grad_par[0, :heads_here], grad_par[1, :heads_here]]
    whole = [conv_query, conv_key, conv_value, decay_log, decay_bias]
    common = [stat_sums, to_absolute(grad_norm_ffn), heads_gain_grad[0]]
    sums = sum_over(packed(common + local), "dp")
    sums = unpacked(sums, [a.shape for a in common + local])
    spread = [
        place_slice(part, array, tensor_rank, part.ndim - 1)
        for part, array in zip(sums[3:], whole)
    ]
    sums = sum_over(packed(sums[:3] + spread), "tensor")
    (
        stat_sums,
        total_ffn_gain,
        total_heads_gain,
        total_conv_query,
        total_conv_key,
        total_conv_value,
        total_decay_log,
        total_decay_bias,
    ) = unpacked(sums, [a.shape for a in common + whole])
    last = packed([to_absolute(grad_norm_attn)])
    [total_attn_gain] = unpacked(sum_over(sum_over(last, "dp"), "tensor"), [norm_attn.shape])
    statistics = jnp.sqrt(stat_sums[:3] / (stat_sums[3] * width))
    return (
        outputs,
        statistics,
        grad_inputs,
        total_attn_gain,
        total_ffn_gain,
        total_heads_gain,
        owned_query,
        owned_key,
        owned_value,
        owned_out_gate,
        owned_decay,
        owned_beta,
        owned_output,
        total_conv_query,
        total_conv_key,
        total_conv_value,
        total_decay_log,
        total_decay_bias,
        owned_gate,
        owned_up,
        owned_down,
    )


def solution(mesh):
    in_specs = (
        P(("dp", "tensor"), None),
        P("dp"),
        P(("dp", "tensor"), None),
        P(),
        P(),
        P(),
        P("dp", "tensor"),
        P("dp", "tensor"),
        P("dp", "tensor"),
        P("dp", "tensor"),
        P("dp", "tensor"),
        P("dp", "tensor"),
        P("tensor", "dp"),
        P(),
        P(),
        P(),
        P(),
        P(),
        P("dp", "tensor"),
        P("dp", "tensor"),
        P("tensor", "dp"),
    )
    out_specs = (
        P(("dp", "tensor"), None),
        P(),
        P(("dp", "tensor"), None),
        P(),
        P(),
        P(),
        P("dp", "tensor"),
        P("dp", "tensor"),
        P("dp", "tensor"),
        P("dp", "tensor"),
        P("dp", "tensor"),
        P("dp", "tensor"),
        P("tensor", "dp"),
        P(),
        P(),
        P(),
        P(),
        P(),
        P("dp", "tensor"),
        P("dp", "tensor"),
        P("tensor", "dp"),
    )
    return jax.shard_map(shards, mesh=mesh, in_specs=in_specs, out_specs=out_specs, check_vma=False)
```

```python
import functools

import jax
import jax.numpy as jnp
from jax import lax
from jax.experimental import pallas as pl
from jax.experimental.pallas import tpu as pltpu
from jax.sharding import PartitionSpec as P

BF=jnp.bfloat16; F32=jnp.float32
DK = 128
CHUNK = 128
HALO = 8


def dot1(a, b, ca=1, cb=0):
    return lax.dot_general(a, b, (((ca,), (cb,)), ((), ())), preferred_element_type=F32)


def split(a):
    if a.dtype == BF:
        return a, None
    high = a.astype(BF)
    return high, (a - high.astype(F32)).astype(BF)


def mm(a, b, ca=1, cb=0):
    a_high, a_low = a if isinstance(a, tuple) else split(a)
    b_high, b_low = b if isinstance(b, tuple) else split(b)
    total = dot1(a_high, b_high, ca, cb)
    if b_low is not None:
        total = total + dot1(a_high, b_low, ca, cb)
    if a_low is not None:
        total = total + dot1(a_low, b_high, ca, cb)
    return total


def exact_sum(ones, values, ca):
    high, rest = split(values)
    middle, low = split(values - high.astype(F32))
    return dot1(ones, high, ca) + (dot1(ones, middle, ca) + dot1(ones, low, ca))


def grids(size):
    return (
        lax.broadcasted_iota(jnp.int32, (size, size), 0),
        lax.broadcasted_iota(jnp.int32, (size, size), 1),
    )


def inverses(couplings):
    size = couplings[0].shape[0]
    i, j = grids(size)
    eye = jnp.where(i == j, 1.0, 0.0).astype(F32)

    def same(bits):
        return lax.shift_right_logical(i, bits) == lax.shift_right_logical(j, bits)

    inside = same(3)
    near = [jnp.where(inside, a, 0.0) for a in couplings]
    second = [split(mm(a, a)) for a in map(split, near)]
    fourth = [mm(a, a) for a in second]
    found = [eye - a for a in near]
    found = [x + mm(x, a) for x, a in zip(found, second)]
    found = [x + mm(x, a) for x, a in zip(found, fourth)]
    bits = 3
    while (1 << bits) < size:
        across = jnp.logical_and(same(bits + 1), jnp.logical_not(same(bits)))
        parts = [split(x) for x in found]
        moved = [mm(jnp.where(across, a, 0.0), x) for a, x in zip(couplings, parts)]
        found = [x - mm(p, y) for x, p, y in zip(found, parts, moved)]
        bits += 1
    return found


def conv_of(taps_ref, ext, columns, rows, start=HALO - 3):
    total = taps_ref[0:1, columns] * ext[start : start + rows, columns]
    for tap in range(1, 4):
        total = total + taps_ref[tap : tap + 1, columns] * ext[
            start + tap : start + tap + rows, columns
        ]
    return total


def decay_of(tail, par_ref):
    i, j = grids(CHUNK)
    ones = jnp.where(i >= j, 1.0, 0.0).astype(BF)
    raised = tail + par_ref[1:2, :]
    log_decay = par_ref[0:1, :] * (
        jnp.maximum(raised, 0.0) + jnp.log1p(jnp.exp(-jnp.abs(raised)))
    )
    return exact_sum(ones, log_decay, 1), log_decay, jax.nn.sigmoid(tail), raised


def fwd_kernel(H, DV, NC, start, p_ref, halo_ref, taps_ref, par_ref, *refs):
    C = CHUNK
    R = NC * C
    W = H * (2 * DK + DV)
    o_ref, u_ref, t_ref, s_ref, S, ext = refs[-6:]
    step = pl.program_id(0)

    if start == 0:

        @pl.when(step == 0)
        def _():
            S[...] = jnp.zeros_like(S)
            ext[0:HALO, :] = jnp.zeros((HALO, W), F32)

        @pl.when(step > 0)
        def _():
            ext[0:HALO, :] = halo_ref[:, 0:W]

    else:

        @pl.when(step == 0)
        def _():
            S[...] = refs[0][...]

        ext[0:HALO, :] = halo_ref[:, 0:W]

    ext[HALO : HALO + R, :] = p_ref[:, 0:W]
    i, j = grids(C)
    low, strict = i >= j, i > j
    idx = [(c, h) for c in range(NC) for h in range(H)]
    rows = [slice(c * C, (c + 1) * C) for c in range(NC)]
    q, k, v, b, g, gr = {}, {}, {}, {}, {}, {}
    for h in range(H):
        for part, out, base, size, factor in (
            (0, q, h * DK, DK, DK**-0.5),
            (1, k, H * DK + h * DK, DK, 1.0),
            (2, v, 2 * H * DK + h * DV, DV, None),
        ):
            mixed = conv_of(taps_ref, ext, slice(base, base + size), R)
            mixed = mixed * jax.nn.sigmoid(mixed)
            if factor is not None:
                mixed = mixed * (
                    lax.rsqrt(jnp.sum(mixed * mixed, axis=1, keepdims=True) + 1e-06) * factor
                )
            mixed = mixed.astype(BF)
            for c in range(NC):
                out[c, h] = mixed[rows[c], :]
    for c in range(NC):
        running, _, beta, _ = decay_of(p_ref[rows[c], W : W + 128], par_ref)
        across = jnp.transpose(running)
        for h in range(H):
            b[c, h] = beta[:, H + h : H + h + 1]
            g[c, h] = running[:, h : h + 1]
            gr[c, h] = across[h : h + 1, :]
    D = {x: jnp.exp(jnp.where(low, g[x] - gr[x], -1e30)) for x in idx}
    A = [jnp.where(strict, dot1(k[x], k[x], 1, 1) * b[x] * D[x], 0.0) for x in idx]
    T = dict(zip(idx, inverses(A)))
    P = {x: dot1(q[x], k[x], 1, 1) * D[x] for x in idx}
    gam = {x: jnp.exp(g[x]) for x in idx}
    Ts = {x: split(T[x]) for x in idx}
    TV = {x: mm(Ts[x], b[x] * v[x].astype(F32)) for x in idx}
    TK = {x: mm(Ts[x], b[x] * gam[x] * k[x].astype(F32)) for x in idx}
    for c in range(NC):
        for h in range(H):
            x = (c, h)
            t_ref[rows[c], h * C : (h + 1) * C] = T[x]
            S0 = S[h * DK : (h + 1) * DK, :]
            s_ref[c, h * DK : (h + 1) * DK, :] = S0
            Ss = split(S0)
            U = TV[x] - mm(TK[x], Ss)
            Us = split(U)
            u_ref[rows[c], h * DV : (h + 1) * DV] = U
            o_ref[rows[c], h * DV : (h + 1) * DV] = gam[x] * mm(q[x], Ss) + mm(P[x], Us)
            last = gr[x][:, C - 1 : C]
            S[h * DK : (h + 1) * DK, :] = jnp.exp(last) * S0 + mm(
                k[x].astype(F32) * jnp.exp(last - g[x]), Us, 0, 0
            )


def bwd_kernel(
    H, DV, end, first, p_ref, halo_ref, taps_ref, par_ref, u_ref, t_ref, s_ref, do_ref, *refs
):
    C = CHUNK
    W = H * (2 * DK + DV)
    dp_ref, dtaps_ref, dpar_ref, dS, carry_ref, ext, dext = refs[-7:]
    step = pl.program_id(0)

    @pl.when(step == 0)
    def _():
        if first:
            dS[...] = jnp.zeros_like(dS)
            dext[C : C + HALO, :] = jnp.zeros((HALO, W), F32)
            dtaps_ref[...] = jnp.zeros_like(dtaps_ref)
            dpar_ref[...] = jnp.zeros_like(dpar_ref)
        else:
            dS[...] = refs[3][...]
            dext[C : C + HALO, :] = refs[4][...]
            dtaps_ref[...] = refs[1][...]
            dpar_ref[...] = refs[2][...]

    @pl.when(step > 0)
    def _():
        dext[C : C + HALO, :] = dext[0:HALO, :]

    @pl.when(step == end)
    def _():
        ext[0:HALO, :] = jnp.zeros((HALO, W), F32)

    @pl.when(step < end)
    def _():
        ext[0:HALO, :] = halo_ref[:, 0:W]

    ext[HALO : HALO + C, :] = p_ref[:, 0:W]
    i, j = grids(C)
    low, strict = i >= j, i > j
    lane = lax.broadcasted_iota(jnp.int32, (C, 128), 1)
    last_row = lax.broadcasted_iota(jnp.int32, (C, 1), 0) == C - 1
    tail = p_ref[:, W : W + 128]
    running, log_decay, beta, raised = decay_of(tail, par_ref)
    across = jnp.transpose(running)
    d_running = jnp.zeros((C, 128), F32)
    d_beta = jnp.zeros((C, 128), F32)

    def gradient_in(columns, mixed, sig, d_act):
        dext[0:C, columns] = d_act * sig * (1.0 + mixed * (1.0 - sig))

    for h in range(H):
        q_columns = slice(h * DK, (h + 1) * DK)
        k_columns = slice(H * DK + h * DK, H * DK + (h + 1) * DK)
        v_columns = slice(2 * H * DK + h * DV, 2 * H * DK + (h + 1) * DV)
        q_mixed = conv_of(taps_ref, ext, q_columns, C)
        k_mixed = conv_of(taps_ref, ext, k_columns, C)
        v_mixed = conv_of(taps_ref, ext, v_columns, C)
        q_sig, k_sig, v_sig = (jax.nn.sigmoid(x) for x in (q_mixed, k_mixed, v_mixed))
        q_act, k_act = q_mixed * q_sig, k_mixed * k_sig
        q_inv = lax.rsqrt(jnp.sum(q_act * q_act, axis=1, keepdims=True) + 1e-06)
        k_inv = lax.rsqrt(jnp.sum(k_act * k_act, axis=1, keepdims=True) + 1e-06)
        q = (q_act * (q_inv * DK**-0.5)).astype(BF)
        k = (k_act * k_inv).astype(BF)
        v = (v_mixed * v_sig).astype(BF)
        b, g, gr = beta[:, H + h : H + h + 1], running[:, h : h + 1], across[h : h + 1, :]
        hv = slice(h * DV, (h + 1) * DV)
        hk = slice(h * DK, (h + 1) * DK)
        U = split(u_ref[:, hv])
        T = split(t_ref[:, h * C : (h + 1) * C])
        S0 = s_ref[0, hk, :]
        Ss = split(S0)
        dO = split(do_ref[:, hv])
        qf, kf = q.astype(F32), k.astype(F32)
        D = jnp.exp(jnp.where(low, g - gr, -1e30))
        kk, qk = dot1(k, k, 1, 1), dot1(q, k, 1, 1)
        bD = b * D
        A, P = jnp.where(strict, kk * bD, 0.0), qk * D
        last = gr[:, C - 1 : C]
        gam, e, G = jnp.exp(g), jnp.exp(last - g), jnp.exp(last)
        dS1 = dS[hk, :]
        dSs = split(dS1)
        dU = mm(P, dO, 0, 0) + mm(kf * e, dSs)
        dR = mm(T, dU, 0, 0)
        dRs = split(dR)
        dS[hk, :] = G * dS1 + mm(qf * gam, dO, 0, 0) - mm(kf * (b * gam), dRs, 0, 0)
        dP = jnp.where(low, mm(dO, U, 1, 1), 0.0)
        dA = jnp.where(strict, -mm(dRs, U, 1, 1), 0.0)
        Rb = v.astype(F32) - gam * mm(k, Ss)
        db = jnp.sum(dR * Rb, axis=1, keepdims=True) + jnp.sum(dA * kk * D, axis=1, keepdims=True)
        dOS = gam * mm(dO, Ss, 1, 1)
        dRS = (b * gam) * mm(dRs, Ss, 1, 1)
        UdS = e * mm(U, dSs, 1, 1)
        M1, M2 = split(dP * D), split(dA * bD)
        dq = dOS + mm(M1, k)
        dk = UdS - dRS + mm(M1, q, 0, 0) + mm(M2, k) + mm(M2, k, 0, 0)
        X = dP * P + dA * A
        uk = jnp.sum(UdS * kf, axis=1, keepdims=True)
        total = jnp.sum(uk, axis=0, keepdims=True) + G * jnp.sum(
            jnp.sum(S0 * dS1, axis=1, keepdims=True), axis=0, keepdims=True
        )
        dg = (
            jnp.sum(dOS * qf - dRS * kf + X - jnp.transpose(X), axis=1, keepdims=True)
            - uk
            + jnp.where(last_row, total, 0.0)
        )
        d_running = jnp.where(lane == h, dg, d_running)
        d_beta = jnp.where(lane == H + h, db, d_beta)
        q_in = jnp.sum(dq * q_act, axis=1, keepdims=True) * (q_inv * q_inv)
        gradient_in(q_columns, q_mixed, q_sig, (q_inv * DK**-0.5) * (dq - q_act * q_in))
        k_in = jnp.sum(dk * k_act, axis=1, keepdims=True) * (k_inv * k_inv)
        gradient_in(k_columns, k_mixed, k_sig, k_inv * (dk - k_act * k_in))
        gradient_in(v_columns, v_mixed, v_sig, b * dR)
    for start in range(0, W, 512):
        columns = slice(start, start + 512)
        here = dext[0:C, columns]
        total = taps_ref[3:4, columns] * here
        dtaps_ref[3:4, columns] += jnp.sum(
            here * ext[HALO : HALO + C, columns], axis=0, keepdims=True
        )
        for tap in range(3):
            total = total + taps_ref[tap : tap + 1, columns] * dext[3 - tap : 3 - tap + C, columns]
            dtaps_ref[tap : tap + 1, columns] += jnp.sum(
                here * ext[HALO - 3 + tap : HALO - 3 + tap + C, columns], axis=0, keepdims=True
            )
        dp_ref[:, columns] = total.astype(BF)
    ones = jnp.where(i >= j, 1.0, 0.0).astype(BF)
    d_log = exact_sum(ones, d_running, 0)
    d_raised = d_log * par_ref[0:1, :] * jax.nn.sigmoid(raised)
    d_tail = d_raised + d_beta * beta * (1.0 - beta)
    dp_ref[:, W : W + 128] = d_tail.astype(BF)
    dpar_ref[0:1, :] += jnp.sum(d_log * log_decay, axis=0, keepdims=True)
    dpar_ref[1:2, :] += jnp.sum(d_raised, axis=0, keepdims=True)
    carry_ref[...] = dext[0:HALO, :]


def room(mebibytes):
    return pltpu.CompilerParams(vmem_limit_bytes=mebibytes * 2**20)


def row_block(rows, width, at=lambda s: s):
    return pl.BlockSpec((rows, width), lambda s: (at(s), 0))


def whole_block(array):
    return pl.BlockSpec(array.shape, lambda s: (0,) * array.ndim)


def mixer_fwd(projected, taps, par, heads, start, count, before=None, NC=2):
    L, wide = projected.shape
    H, C = heads, CHUNK
    W = taps.shape[1]
    DV = W // H - 2 * DK
    f = jax.ShapeDtypeStruct
    base = start // NC
    shapes = [f((L, H * DV), F32), f((L, H * DV), F32), f((L, H * C), F32), f((L // C, H * DK, DV), F32)]
    more, more_specs, aliases = [], [], {}
    if before is not None:
        more = [before[4]] + list(before[:4])
        more_specs = [whole_block(before[4])] + [pl.BlockSpec(memory_space=pl.ANY)] * 4
        aliases = {5 + n: n for n in range(4)}
    return pl.pallas_call(
        functools.partial(fwd_kernel, H, DV, NC, start),
        grid=(count // NC,),
        in_specs=[
            row_block(NC * C, wide, lambda s: base + s),
            row_block(HALO, wide, lambda s: jnp.maximum((base + s) * (NC * C // HALO) - 1, 0)),
            whole_block(taps),
            whole_block(par),
        ]
        + more_specs,
        out_specs=[
            row_block(NC * C, H * DV, lambda s: base + s),
            row_block(NC * C, H * DV, lambda s: base + s),
            row_block(NC * C, H * C, lambda s: base + s),
            pl.BlockSpec((NC, H * DK, DV), lambda s: (base + s, 0, 0)),
            pl.BlockSpec((H * DK, DV), lambda s: (0, 0)),
        ],
        out_shape=shapes + [f((H * DK, DV), F32)],
        scratch_shapes=[pltpu.VMEM((NC * C + HALO, W), F32)],
        input_output_aliases=aliases,
        compiler_params=room(22),
        cost_estimate=pl.CostEstimate(
            flops=3 * 10**9 * count, bytes_accessed=3 * 2**20 * count, transcendentals=0
        ),
        name="mixer_fwd",
    )(projected, projected, taps, par, *more)


def mixer_bwd(projected, taps, par, written, inverse, states, grad_heads, heads, end, count, before=None):
    L, wide = projected.shape
    H, C = heads, CHUNK
    W = taps.shape[1]
    DV = W // H - 2 * DK
    f = jax.ShapeDtypeStruct

    def back(s):
        return end - s

    more, more_specs, aliases = [], [], {}
    if before is not None:
        more = list(before)
        more_specs = [pl.BlockSpec(memory_space=pl.ANY)] + [whole_block(a) for a in before[1:]]
        aliases = {8: 0}
    state, halo = f((H * DK, DV), F32), f((HALO, W), F32)
    return pl.pallas_call(
        functools.partial(bwd_kernel, H, DV, end, before is None),
        grid=(count,),
        in_specs=[
            row_block(C, wide, back),
            row_block(HALO, wide, lambda s: jnp.maximum(back(s) * (C // HALO) - 1, 0)),
            whole_block(taps),
            whole_block(par),
            row_block(C, H * DV, back),
            row_block(C, H * C, back),
            pl.BlockSpec((1, H * DK, DV), lambda s: (back(s), 0, 0)),
            row_block(C, H * DV, back),
        ]
        + more_specs,
        out_specs=[
            row_block(C, wide, back),
            whole_block(taps),
            whole_block(par),
            whole_block(state),
            whole_block(halo),
        ],
        out_shape=[f((L, wide), BF), f(taps.shape, F32), f(par.shape, F32), state, halo],
        scratch_shapes=[pltpu.VMEM((C + HALO, W), F32), pltpu.VMEM((C + HALO, W), F32)],
        input_output_aliases=aliases,
        compiler_params=room(22),
        cost_estimate=pl.CostEstimate(
            flops=6 * 10**9 * count, bytes_accessed=4 * 2**20 * count, transcendentals=0
        ),
        name="mixer_bwd",
    )(projected, projected, taps, par, written, inverse, states, grad_heads, *more)


def gate_fwd_kernel(DV, o_ref, gate_ref, gain_ref, out_ref):
    for start in range(0, o_ref.shape[1], DV):
        cut = slice(start, start + DV)
        heads, gate = o_ref[:, cut], gate_ref[:, cut]
        inverse = lax.rsqrt(jnp.mean(heads * heads, axis=1, keepdims=True) + 1e-05)
        out_ref[:, cut] = (heads * inverse * gain_ref[...] * (gate * jax.nn.sigmoid(gate))).astype(BF)


def gate_fwd(heads_out, gate_proj, gain):
    L, width = heads_out.shape
    rows = L // 8
    return pl.pallas_call(
        functools.partial(gate_fwd_kernel, gain.shape[1]),
        grid=(8,),
        in_specs=[row_block(rows, width), row_block(rows, width), whole_block(gain)],
        out_specs=row_block(rows, width),
        out_shape=jax.ShapeDtypeStruct((L, width), BF),
        compiler_params=room(12),
        cost_estimate=pl.CostEstimate(flops=5 * 10**9, bytes_accessed=10 * 2**20, transcendentals=0),
        name="gate_fwd",
    )(heads_out, gate_proj, gain)


def gate_bwd_kernel(DV, o_ref, gate_ref, gain_ref, in_ref, do_ref, dgate_ref, dgain_ref):
    @pl.when(pl.program_id(0) == 0)
    def _():
        dgain_ref[...] = jnp.zeros_like(dgain_ref)

    for start in range(0, o_ref.shape[1], DV):
        cut = slice(start, start + DV)
        heads, gate, grad = o_ref[:, cut], gate_ref[:, cut], in_ref[:, cut]
        inverse = lax.rsqrt(jnp.mean(heads * heads, axis=1, keepdims=True) + 1e-05)
        normed = heads * inverse
        sig = jax.nn.sigmoid(gate)
        dgate_ref[:, cut] = (
            grad * (normed * gain_ref[...]) * (sig * (1.0 + gate * (1.0 - sig)))
        ).astype(BF)
        d_scaled = grad * (gate * sig)
        dgain_ref[...] += jnp.sum(d_scaled * normed, axis=0, keepdims=True)
        d_normed = d_scaled * gain_ref[...]
        do_ref[:, cut] = inverse * (
            d_normed - normed * jnp.mean(d_normed * normed, axis=1, keepdims=True)
        )


def gate_bwd(heads_out, gate_proj, gain, grad_mixer):
    L, width = heads_out.shape
    rows = L // 8
    f = jax.ShapeDtypeStruct
    return pl.pallas_call(
        functools.partial(gate_bwd_kernel, gain.shape[1]),
        grid=(8,),
        in_specs=[row_block(rows, width), row_block(rows, width), whole_block(gain), row_block(rows, width)],
        out_specs=[row_block(rows, width), row_block(rows, width), whole_block(gain)],
        out_shape=[f((L, width), F32), f((L, width), BF), f(gain.shape, F32)],
        compiler_params=room(14),
        cost_estimate=pl.CostEstimate(flops=7 * 10**9, bytes_accessed=18 * 2**20, transcendentals=0),
        name="gate_bwd",
    )(heads_out, gate_proj, gain, grad_mixer)


def at_place(place, n):
    return jnp.where(place < n // 2, 2 * place, 2 * (n - place) - 1)


def place_of(index, n):
    return jnp.where(index % 2 == 0, index // 2, n - (index + 1) // 2)


def ring_pairs(n):
    order = list(range(0, n, 2)) + list(range(n - 1, 0, -2))
    ahead = [(order[i], order[(i + 1) % n]) for i in range(n)]
    return ahead, [(d, s) for s, d in ahead]


def behind(d):
    n = lax.axis_size("dp")
    return at_place((place_of(lax.axis_index("dp"), n) - d + n) % n, n)


def after(values, token):
    return lax.optimization_barrier((values, token))[0]


class GatherRing:
    def __init__(self, shard):
        half = shard.shape[0] // 2
        self.first, self.second = [shard[:half]], [shard[half:]]
        self.n = lax.axis_size("dp")

    def send(self, token):
        ahead, back = ring_pairs(self.n)
        first, second = after((self.first[-1], self.second[-1]), token)
        self.first.append(lax.ppermute(first, "dp", ahead))
        self.second.append(lax.ppermute(second, "dp", back))

    def last(self):
        return self.first[-1], self.second[-1]

    def through(self):
        return len(self.first) == self.n

    def finish(self, widths):
        half = self.first[0].shape[0]
        fulls = [jnp.zeros((self.n * 2 * half, width), BF) for width in widths]
        for hop in range(self.n):
            for piece, at in (
                (self.first[hop], behind(hop) * 2 * half),
                (self.second[hop], behind(self.n - hop) * 2 * half + half),
            ):
                fulls = [
                    lax.dynamic_update_slice(full, part, (at, 0))
                    for full, part in zip(fulls, columns(piece, widths))
                ]
        return fulls


def land_kernel(widths, *refs):
    count = len(widths)
    first, second = refs[0], refs[1]
    terms = refs[2 : 2 + 2 * count]
    for arrived, mine, out in (
        (first, terms[:count], refs[-2]),
        (second, terms[count:], refs[-1]),
    ):
        start = 0
        for width, term in zip(widths, mine):
            cut = slice(start, start + width)
            out[:, cut] = (arrived[:, cut].astype(F32) + term[...].astype(F32)).astype(BF)
            start += width


def landed(flying, terms):
    widths = [term.shape[1] for term in terms[0]]
    rows, wide = flying[0].shape
    steps = 2
    arrays = list(flying) + list(terms[0]) + list(terms[1])
    return pl.pallas_call(
        functools.partial(land_kernel, widths),
        grid=(steps,),
        in_specs=[row_block(rows // steps, a.shape[1]) for a in arrays],
        out_specs=[row_block(rows // steps, wide)] * 2,
        out_shape=[jax.ShapeDtypeStruct((rows, wide), BF)] * 2,
        compiler_params=room(10),
        cost_estimate=pl.CostEstimate(flops=10**6, bytes_accessed=10**6, transcendentals=0),
        name="land",
    )(*arrays)


class ScatterRing:
    def __init__(self, pairs, token):
        self.n = lax.axis_size("dp")
        self.hop = 0
        self.pairs = pairs
        self.sums = tuple(
            jnp.concatenate(terms, axis=1).astype(BF)
            for terms in (self.terms_of(1, 0, token), self.terms_of(self.n - 1, 1, token))
        )

    def terms_of(self, place, side, token):
        terms = []
        for features, grads in self.pairs:
            half = features.shape[1] // self.n // 2
            at = behind(place % self.n) * (2 * half) + side * half
            left = lax.dynamic_slice_in_dim(features, at, half, 1)
            terms.append(contract_rows(*after((left, grads), token)))
        return terms

    def send(self, token):
        ahead, back = ring_pairs(self.n)
        first, second = after(self.sums, token)
        self.flying = lax.ppermute(first, "dp", ahead), lax.ppermute(second, "dp", back)

    def multiply(self, token):
        kind = F32 if self.hop == self.n - 2 else BF
        terms = (
            self.terms_of(self.hop + 2, 0, token),
            self.terms_of(2 * self.n - 2 - self.hop, 1, token),
        )
        self.terms = lax.optimization_barrier([[t.astype(kind) for t in side] for side in terms])
        return self.terms

    def land(self, token):
        self.hop += 1
        flying, terms = after((self.flying, self.terms), token)
        if self.hop == self.n - 1:
            self.sums = tuple(
                [
                    x.astype(F32) + y
                    for x, y in zip(columns(arrived, [term.shape[1] for term in mine]), mine)
                ]
                for arrived, mine in zip(flying, terms)
            )
        else:
            self.sums = tuple(landed(flying, terms))
        return self.sums

    def done(self):
        return self.hop == self.n - 1

    def results(self):
        return [jnp.concatenate(halves, axis=0) for halves in zip(*self.sums)]


def slot(token, rings, pieces=(), gathers=()):
    rings = [ring for ring in rings if not ring.done()]
    gathers = [ring for ring in gathers if not ring.through()]
    for ring in rings:
        ring.send(token)
    for ring in gathers:
        ring.send(token)
    token = [ring.multiply(token) for ring in rings] or token
    for piece in pieces:
        token = piece(token)
    token = [ring.land(token) for ring in rings] or token
    if gathers:
        token = token, [ring.last() for ring in gathers]
    return token


def run_out(token, rings, pieces=(), gathers=()):
    pieces = list(pieces)
    while (
        pieces
        or any(not ring.done() for ring in rings)
        or any(not ring.through() for ring in gathers)
    ):
        token = slot(token, rings, [pieces.pop(0)] if pieces else (), gathers)
    return token


def contract_rows(left, right):
    return lax.dot_general(
        left, right, (((0,), (0,)), ((), ())), preferred_element_type=jnp.float32
    )


def times_transposed(left, right):
    return lax.dot_general(
        left, right, (((1,), (1,)), ((), ())), preferred_element_type=jnp.float32
    )


CORES = [(0, 1), (1, 0), (2, 3), (3, 2)]
PAIRS = [(0, 2), (2, 0), (1, 3), (3, 1)]


class Spread:
    def __init__(self, block):
        self.block = block
        self.plain = lax.axis_size("tensor") != 4
        if not self.plain:
            self.far = lax.ppermute(block, "tensor", PAIRS)
            self.near = lax.ppermute(block, "tensor", CORES)

    def turn(self, token):
        if self.plain:
            return token
        far = after(self.far, token)
        self.far_near = lax.ppermute(far, "tensor", CORES)
        return far

    def rows(self, token=()):
        if self.plain:
            return lax.all_gather(after(self.block, token), "tensor", axis=0, tiled=True)
        rank = lax.axis_index("tensor")
        rows, width = self.block.shape
        out = jnp.zeros((4 * rows, width), self.block.dtype)
        parts = after((self.block, self.near, self.far, self.far_near), token)
        for flip, part in enumerate(parts):
            out = lax.dynamic_update_slice_in_dim(out, part, (rank ^ flip) * rows, 0)
        return out


def spread_rows(block):
    spread = Spread(block)
    spread.turn(())
    return spread.rows()


class RowSum:
    def __init__(self, product, rows):
        self.product, self.rows = product, rows
        self.rank = lax.axis_index("tensor")
        self.plain = lax.axis_size("tensor") != 4

    def term(self, flip, token):
        return self.product((self.rank ^ flip) * self.rows, token)

    def far(self, token):
        if self.plain:
            whole = [self.product(i * self.rows, token) for i in range(lax.axis_size("tensor"))]
            self.total = lax.psum_scatter(
                jnp.concatenate(whole, axis=0), "tensor", scatter_dimension=0, tiled=True
            )
            return self.total
        self.sent = self.term(3, token).astype(BF)
        self.far_near = lax.ppermute(self.sent, "tensor", CORES)
        return self.sent

    def far_sum(self, token):
        if self.plain:
            return token
        total = (self.term(2, token) + self.far_near.astype(F32)).astype(BF)
        self.from_far = lax.ppermute(total, "tensor", PAIRS)
        return total

    def near(self, token):
        if self.plain:
            return token
        sent = self.term(1, token).astype(BF)
        self.from_near = lax.ppermute(sent, "tensor", CORES)
        return sent

    def own(self, token):
        if self.plain:
            return token
        self.mine = self.term(0, token)
        return self.mine

    def result(self, token):
        if self.plain:
            return after(self.total, token)
        mine = after(self.mine, token)
        return mine + self.from_near.astype(F32) + self.from_far.astype(F32)

    def pieces(self):
        return [self.far, self.far_sum, self.near, self.own]


def summed_rows(pairs, rows):
    def product(start, token):
        total = None
        for grads, weight in pairs:
            part, other = after((lax.dynamic_slice_in_dim(grads, start, rows, 0), weight), token)
            part = times_transposed(part, other)
            total = part if total is None else total + part
        return total

    return RowSum(product, rows)


def sum_over(values, axis):
    n = lax.axis_size(axis)
    if n & (n - 1):
        return lax.psum(values, axis)
    step = 1
    while step < n:
        values = values + lax.ppermute(values, axis, [(i, i ^ step) for i in range(n)])
        step *= 2
    return values


def packed(arrays):
    flat = jnp.concatenate([a.reshape(-1) for a in arrays])
    pad = -flat.shape[0] % 1024
    return jnp.pad(flat, (0, pad)).reshape(-1, 128)


def unpacked(values, shapes):
    flat = values.reshape(-1)
    out, start = [], 0
    for shape in shapes:
        size = 1
        for extent in shape:
            size *= extent
        out.append(flat[start : start + size].reshape(shape))
        start += size
    return out


def norm_back(values, inverse, gain, incoming):
    scaled = incoming * gain
    width = values.shape[1]
    grad_values = (
        inverse * scaled
        - values
        * inverse
        * inverse
        * inverse
        * jnp.sum(scaled * values, axis=1, keepdims=True)
        / width
    )
    grad_gain = jnp.sum(incoming * values * inverse, axis=0)
    return (grad_values, grad_gain)


def place_slice(local, whole, rank, axis):
    return lax.dynamic_update_slice_in_dim(
        jnp.zeros_like(whole), local, rank * local.shape[axis], axis
    )


def columns(array, widths):
    out, start = [], 0
    for width in widths:
        out.append(array[:, start : start + width])
        start += width
    return out


def shards(
    inputs,
    lengths,
    cotangent,
    norm_attn,
    norm_ffn,
    norm_heads,
    w_query,
    w_key,
    w_value,
    w_out_gate,
    w_decay,
    w_beta,
    w_output,
    conv_query,
    conv_key,
    conv_value,
    decay_log,
    decay_bias,
    w_ffn_gate,
    w_ffn_up,
    w_ffn_down,
):
    rows = inputs.shape[0]
    width = inputs.shape[1]
    tensor_rank = lax.axis_index("tensor")
    positions = tensor_rank * rows + jnp.arange(rows, dtype=jnp.int32)
    valid = (positions < lengths[0]).astype(jnp.float32)[:, None]
    heads_here = w_decay.shape[1]
    widths = [w.shape[1] for w in (w_query, w_key, w_value, w_decay, w_beta)]
    fill = -sum(widths) % 128
    mixed_shard = jnp.pad(
        jnp.concatenate((w_query, w_key, w_value, w_decay, w_beta), axis=1), ((0, 0), (0, fill))
    )
    ffn_width = w_ffn_gate.shape[1]
    kept = {}
    mixed_ring = GatherRing(mixed_shard)
    mixed_ring.send(())
    gate_shards, ffn_shards, rows_in = after(
        ((w_out_gate, w_output), (w_ffn_gate, w_ffn_up, w_ffn_down), (inputs, cotangent)),
        mixed_ring.last(),
    )
    inputs, cotangent = rows_in
    token = run_out(mixed_ring.last(), (), (), (mixed_ring,))
    gate_ring = GatherRing(jnp.concatenate((gate_shards[0], gate_shards[1].T), axis=1))
    ffn_ring = GatherRing(
        jnp.concatenate((ffn_shards[0], ffn_shards[1], ffn_shards[2].T), axis=1)
    )
    [mixed_full] = mixed_ring.finish([mixed_shard.shape[1]])

    gain_attn = norm_attn
    gain_ffn = norm_ffn
    stream_in = inputs.astype(jnp.float32)
    grad_out = valid * cotangent.astype(jnp.float32)
    inverse_in = lax.rsqrt(jnp.mean(stream_in * stream_in, axis=1, keepdims=True) + 1e-06)
    full_in = spread_rows((stream_in * inverse_in * gain_attn).astype(jnp.bfloat16))

    def here(array):
        size = array.shape[-1] // lax.axis_size("tensor")
        return lax.dynamic_slice_in_dim(array, tensor_rank * size, size, array.ndim - 1)

    taps = jnp.concatenate((here(conv_query), here(conv_key), here(conv_value)), axis=1)
    par = jnp.pad(
        jnp.stack((-jnp.exp(here(decay_log)), here(decay_bias))), ((0, 6), (0, 128 - heads_here))
    )
    gain_heads = norm_heads[None, :]
    chunks = full_in.shape[0] // CHUNK
    parts = 4

    def project(token):
        kept["projected"] = jnp.dot(
            *after((full_in, mixed_full), token), preferred_element_type=jnp.float32
        )
        kept["forward"] = None
        return kept["projected"]

    def forward_part(start):
        def piece(token):
            kept["forward"] = mixer_fwd(
                after(kept["projected"], token),
                taps,
                par,
                heads_here,
                start,
                chunks // parts,
                kept["forward"],
            )
            return kept["forward"][4]

        return piece

    token = run_out(
        token,
        (),
        [project] + [forward_part(i * (chunks // parts)) for i in range(parts)],
        (gate_ring,),
    )
    projected = kept["projected"]
    heads_out, written, inverse, states, _ = kept["forward"]
    gate_full, output_full = gate_ring.finish([w_out_gate.shape[1], w_output.shape[0]])

    def gate(token):
        kept["gate"] = jnp.dot(
            *after((full_in, gate_full), token), preferred_element_type=jnp.float32
        )
        kept["mixer"] = gate_fwd(heads_out, kept["gate"], gain_heads)
        return kept["mixer"]

    def attend(token):
        kept["attn"] = summed_rows(((kept["mixer"], output_full),), rows)
        return kept["attn"].far_sum(kept["attn"].far(token))

    def attend_own(token):
        return kept["attn"].own(kept["attn"].near(token))

    def middle(token):
        kept["branch"] = kept["attn"].result(token)
        stream = stream_in + kept["branch"]
        kept["stream"] = stream
        kept["inverse"] = lax.rsqrt(jnp.mean(stream * stream, axis=1, keepdims=True) + 1e-06)
        normed = (stream * kept["inverse"] * gain_ffn).astype(jnp.bfloat16)
        kept["full_mid"] = spread_rows(normed)
        return normed

    token = run_out(token, (), [gate, attend, attend_own, middle], (ffn_ring,))
    gate_proj, mixer, branch_attn = kept["gate"], kept["mixer"], kept["branch"]
    stream, inverse_mid, full_mid = kept["stream"], kept["inverse"], kept["full_mid"]
    ffn_gate_full, ffn_up_full, down_full = ffn_ring.finish(
        [ffn_width, ffn_width, w_ffn_down.shape[0]]
    )
    grad_ffn = spread_rows(after(grad_out.astype(jnp.bfloat16), full_mid))

    token, full_mid_in = after((token, full_mid), ffn_ring.last())
    ffn_gate = jnp.dot(full_mid_in, ffn_gate_full, preferred_element_type=jnp.float32)
    ffn_up = jnp.dot(full_mid_in, ffn_up_full, preferred_element_type=jnp.float32)
    sigma = jax.nn.sigmoid(ffn_gate)
    silu_gate = ffn_gate * sigma
    hidden = (silu_gate * ffn_up).astype(jnp.bfloat16)
    grad_hidden = jnp.dot(grad_ffn, down_full, preferred_element_type=jnp.float32)
    grad_gate_in = grad_hidden * ffn_up * sigma * (1.0 + ffn_gate * (1.0 - sigma))
    grad_gate_in = grad_gate_in.astype(jnp.bfloat16)
    grad_up_in = (grad_hidden * silu_gate).astype(jnp.bfloat16)
    token = grad_gate_in, grad_up_in, hidden
    ffn_scatter = ScatterRing(
        ((full_mid, grad_gate_in), (full_mid, grad_up_in), (grad_ffn, hidden)), token
    )
    token = ffn_scatter.sums
    mid_sum = summed_rows(((grad_gate_in, ffn_gate_full), (grad_up_in, ffn_up_full)), rows)

    def mid_own(token):
        return mid_sum.own(mid_sum.near(token))

    def middle_back(token):
        through, kept["norm_ffn"] = norm_back(stream, inverse_mid, gain_ffn, mid_sum.result(token))
        kept["grad_stream"] = grad_out + through
        low = kept["grad_stream"].astype(jnp.bfloat16)
        kept["spread"] = Spread(low)
        return low

    def turn(token):
        token = ffn_sum.far_sum(ffn_sum.far(token))
        return kept["spread"].turn(token)

    def attend_back(token):
        kept["grad_attn"] = kept["spread"].rows(token)
        grad_mixer = jnp.dot(
            *after((kept["grad_attn"], output_full), token), preferred_element_type=jnp.float32
        )
        kept["gate_back"] = gate_bwd(heads_out, gate_proj, gain_heads, grad_mixer)
        kept["backward"] = None
        return kept["gate_back"][0]

    def backward_part(end):
        def piece(token):
            kept["backward"] = mixer_bwd(
                projected,
                taps,
                par,
                written,
                inverse,
                states,
                after(kept["gate_back"][0], token),
                heads_here,
                end,
                chunks // parts,
                kept["backward"],
            )
            return kept["backward"][3]

        return piece

    ffn_sum = summed_rows(((hidden, down_full),), rows)
    backward = [backward_part(chunks - 1 - i * (chunks // parts)) for i in range(parts)]
    token = run_out(
        token,
        (ffn_scatter,),
        [
            lambda t: mid_sum.far_sum(mid_sum.far(t)),
            mid_own,
            middle_back,
            turn,
            attend_back,
        ]
        + backward[:2],
    )
    grad_stream, grad_norm_ffn, grad_attn = kept["grad_stream"], kept["norm_ffn"], kept["grad_attn"]
    _, grad_gate_proj, heads_gain_grad = kept["gate_back"]
    gate_scatter = ScatterRing(((full_in, grad_gate_proj), (grad_attn, mixer)), token)
    token = gate_scatter.sums

    def in_far(token):
        kept["in_sum"] = summed_rows(
            ((grad_gate_proj, gate_full), (kept["backward"][0], mixed_full)), rows
        )
        return kept["in_sum"].far_sum(kept["in_sum"].far(token))

    def leave(token):
        kept["branch_ffn"] = ffn_sum.result(ffn_sum.own(ffn_sum.near(token)))
        kept["outputs"] = (valid * (stream + kept["branch_ffn"])).astype(jnp.bfloat16)
        return kept["outputs"]

    def in_own(token):
        return kept["in_sum"].own(kept["in_sum"].near(token))

    def last_back(token):
        through, kept["norm_attn"] = norm_back(
            stream_in, inverse_in, gain_attn, kept["in_sum"].result(token)
        )
        kept["grad_inputs"] = grad_stream + through
        return kept["grad_inputs"]

    token = run_out(
        token,
        (gate_scatter,),
        backward[2:] + [in_far, in_own, leave, last_back],
    )
    grad_projected, grad_taps, grad_par, _, _ = kept["backward"]
    mixed_scatter = ScatterRing(((full_in, grad_projected),), token)
    branch_ffn, outputs = kept["branch_ffn"], kept["outputs"]
    stat_sums = jnp.stack(
        [
            jnp.sum(valid * stream_in * stream_in),
            jnp.sum(valid * branch_attn * branch_attn),
            jnp.sum(valid * branch_ffn * branch_ffn),
            jnp.sum(valid),
        ]
    )
    local = columns(grad_taps, widths[:3]) + [grad_par[0, :heads_here], grad_par[1, :heads_here]]
    whole = [conv_query, conv_key, conv_value, decay_log, decay_bias]
    common = [stat_sums, grad_norm_ffn, heads_gain_grad[0]]
    def common_over_dp(token):
        kept["common"] = sum_over(after(packed(common + local), token), "dp")
        return kept["common"]

    def common_over_tensor(token):
        sums = unpacked(kept["common"], [a.shape for a in common + local])
        spread = [
            place_slice(part, array, tensor_rank, part.ndim - 1)
            for part, array in zip(sums[3:], whole)
        ]
        kept["common"] = sum_over(after(packed(sums[:3] + spread), token), "tensor")
        return kept["common"]

    def last_over_dp(token):
        kept["last"] = sum_over(after(packed([kept["norm_attn"]]), token), "dp")
        return kept["last"]

    def last_over_tensor(token):
        kept["last"] = sum_over(after(kept["last"], token), "tensor")
        return kept["last"]

    token = run_out(
        mixed_scatter.sums,
        (mixed_scatter,),
        [last_over_dp, last_over_tensor, common_over_dp, common_over_tensor],
    )
    grad_inputs = kept["grad_inputs"]
    owned_gate, owned_up, owned_down = ffn_scatter.results()
    owned_out_gate, owned_output = gate_scatter.results()
    owned_query, owned_key, owned_value, owned_decay, owned_beta = columns(
        mixed_scatter.results()[0], widths
    )
    (
        stat_sums,
        total_ffn_gain,
        total_heads_gain,
        total_conv_query,
        total_conv_key,
        total_conv_value,
        total_decay_log,
        total_decay_bias,
    ) = unpacked(kept["common"], [a.shape for a in common + whole])
    [total_attn_gain] = unpacked(kept["last"], [norm_attn.shape])
    statistics = jnp.sqrt(stat_sums[:3] / (stat_sums[3] * width))
    return (
        outputs,
        statistics,
        grad_inputs,
        total_attn_gain,
        total_ffn_gain,
        total_heads_gain,
        owned_query,
        owned_key,
        owned_value,
        owned_out_gate,
        owned_decay,
        owned_beta,
        owned_output.T,
        total_conv_query,
        total_conv_key,
        total_conv_value,
        total_decay_log,
        total_decay_bias,
        owned_gate,
        owned_up,
        owned_down.T,
    )


def solution(mesh):
    in_specs = (
        P(("dp", "tensor"), None),
        P("dp"),
        P(("dp", "tensor"), None),
        P(),
        P(),
        P(),
        P("dp", "tensor"),
        P("dp", "tensor"),
        P("dp", "tensor"),
        P("dp", "tensor"),
        P("dp", "tensor"),
        P("dp", "tensor"),
        P("tensor", "dp"),
        P(),
        P(),
        P(),
        P(),
        P(),
        P("dp", "tensor"),
        P("dp", "tensor"),
        P("tensor", "dp"),
    )
    out_specs = (
        P(("dp", "tensor"), None),
        P(),
        P(("dp", "tensor"), None),
        P(),
        P(),
        P(),
        P("dp", "tensor"),
        P("dp", "tensor"),
        P("dp", "tensor"),
        P("dp", "tensor"),
        P("dp", "tensor"),
        P("dp", "tensor"),
        P("tensor", "dp"),
        P(),
        P(),
        P(),
        P(),
        P(),
        P("dp", "tensor"),
        P("dp", "tensor"),
        P("tensor", "dp"),
    )
    return jax.shard_map(shards, mesh=mesh, in_specs=in_specs, out_specs=out_specs, check_vma=False)
```

```python
import functools

import jax
import jax.numpy as jnp
from jax import lax
from jax.experimental import pallas as pl
from jax.experimental.pallas import tpu as pltpu
from jax.sharding import PartitionSpec as P

BF=jnp.bfloat16; F32=jnp.float32
DK = 128
CHUNK = 128
HALO = 8


def dot1(a, b, ca=1, cb=0):
    return lax.dot_general(a, b, (((ca,), (cb,)), ((), ())), preferred_element_type=F32)


def split(a):
    if a.dtype == BF:
        return a, None
    high = a.astype(BF)
    return high, (a - high.astype(F32)).astype(BF)


def mm(a, b, ca=1, cb=0):
    a_high, a_low = a if isinstance(a, tuple) else split(a)
    b_high, b_low = b if isinstance(b, tuple) else split(b)
    total = dot1(a_high, b_high, ca, cb)
    if b_low is not None:
        total = total + dot1(a_high, b_low, ca, cb)
    if a_low is not None:
        total = total + dot1(a_low, b_high, ca, cb)
    return total


def exact_sum(ones, values, ca):
    high, rest = split(values)
    middle, low = split(values - high.astype(F32))
    return dot1(ones, high, ca) + (dot1(ones, middle, ca) + dot1(ones, low, ca))


def grids(size):
    return (
        lax.broadcasted_iota(jnp.int32, (size, size), 0),
        lax.broadcasted_iota(jnp.int32, (size, size), 1),
    )


def inverses(couplings):
    size = couplings[0].shape[0]
    i, j = grids(size)
    eye = jnp.where(i == j, 1.0, 0.0).astype(F32)

    def same(bits):
        return lax.shift_right_logical(i, bits) == lax.shift_right_logical(j, bits)

    inside = same(3)
    near = [jnp.where(inside, a, 0.0) for a in couplings]
    second = [split(mm(a, a)) for a in map(split, near)]
    fourth = [mm(a, a) for a in second]
    found = [eye - a for a in near]
    found = [x + mm(x, a) for x, a in zip(found, second)]
    found = [x + mm(x, a) for x, a in zip(found, fourth)]
    bits = 3
    while (1 << bits) < size:
        across = jnp.logical_and(same(bits + 1), jnp.logical_not(same(bits)))
        parts = [split(x) for x in found]
        moved = [mm(jnp.where(across, a, 0.0), x) for a, x in zip(couplings, parts)]
        found = [x - mm(p, y) for x, p, y in zip(found, parts, moved)]
        bits += 1
    return found


def conv_of(taps_ref, ext, columns, rows, start=HALO - 3):
    total = taps_ref[0:1, columns] * ext[start : start + rows, columns]
    for tap in range(1, 4):
        total = total + taps_ref[tap : tap + 1, columns] * ext[
            start + tap : start + tap + rows, columns
        ]
    return total


def decay_of(tail, par_ref):
    i, j = grids(CHUNK)
    ones = jnp.where(i >= j, 1.0, 0.0).astype(BF)
    raised = tail + par_ref[1:2, :]
    log_decay = par_ref[0:1, :] * (
        jnp.maximum(raised, 0.0) + jnp.log1p(jnp.exp(-jnp.abs(raised)))
    )
    return exact_sum(ones, log_decay, 1), log_decay, jax.nn.sigmoid(tail), raised


def fwd_kernel(H, DV, NC, start, p_ref, halo_ref, taps_ref, par_ref, *refs):
    C = CHUNK
    R = NC * C
    W = H * (2 * DK + DV)
    o_ref, u_ref, t_ref, s_ref, S, ext = refs[-6:]
    step = pl.program_id(0)

    if start == 0:

        @pl.when(step == 0)
        def _():
            S[...] = jnp.zeros_like(S)
            ext[0:HALO, :] = jnp.zeros((HALO, W), F32)

        @pl.when(step > 0)
        def _():
            ext[0:HALO, :] = halo_ref[:, 0:W]

    else:

        @pl.when(step == 0)
        def _():
            S[...] = refs[0][...]

        ext[0:HALO, :] = halo_ref[:, 0:W]

    ext[HALO : HALO + R, :] = p_ref[:, 0:W]
    i, j = grids(C)
    low, strict = i >= j, i > j
    idx = [(c, h) for c in range(NC) for h in range(H)]
    rows = [slice(c * C, (c + 1) * C) for c in range(NC)]
    q, k, v, b, g, gr = {}, {}, {}, {}, {}, {}
    for h in range(H):
        for part, out, base, size, factor in (
            (0, q, h * DK, DK, DK**-0.5),
            (1, k, H * DK + h * DK, DK, 1.0),
            (2, v, 2 * H * DK + h * DV, DV, None),
        ):
            mixed = conv_of(taps_ref, ext, slice(base, base + size), R)
            mixed = mixed * jax.nn.sigmoid(mixed)
            if factor is not None:
                mixed = mixed * (
                    lax.rsqrt(jnp.sum(mixed * mixed, axis=1, keepdims=True) + 1e-06) * factor
                )
            mixed = mixed.astype(BF)
            for c in range(NC):
                out[c, h] = mixed[rows[c], :]
    for c in range(NC):
        running, _, beta, _ = decay_of(p_ref[rows[c], W : W + 128], par_ref)
        across = jnp.transpose(running)
        for h in range(H):
            b[c, h] = beta[:, H + h : H + h + 1]
            g[c, h] = running[:, h : h + 1]
            gr[c, h] = across[h : h + 1, :]
    D = {x: jnp.exp(jnp.where(low, g[x] - gr[x], -1e30)) for x in idx}
    A = [jnp.where(strict, dot1(k[x], k[x], 1, 1) * b[x] * D[x], 0.0) for x in idx]
    T = dict(zip(idx, inverses(A)))
    P = {x: dot1(q[x], k[x], 1, 1) * D[x] for x in idx}
    gam = {x: jnp.exp(g[x]) for x in idx}
    Ts = {x: split(T[x]) for x in idx}
    TV = {x: mm(Ts[x], b[x] * v[x].astype(F32)) for x in idx}
    TK = {x: mm(Ts[x], b[x] * gam[x] * k[x].astype(F32)) for x in idx}
    for c in range(NC):
        for h in range(H):
            x = (c, h)
            t_ref[rows[c], h * C : (h + 1) * C] = T[x]
            S0 = S[h * DK : (h + 1) * DK, :]
            s_ref[c, h * DK : (h + 1) * DK, :] = S0
            Ss = split(S0)
            U = TV[x] - mm(TK[x], Ss)
            Us = split(U)
            u_ref[rows[c], h * DV : (h + 1) * DV] = U
            o_ref[rows[c], h * DV : (h + 1) * DV] = gam[x] * mm(q[x], Ss) + mm(P[x], Us)
            last = gr[x][:, C - 1 : C]
            S[h * DK : (h + 1) * DK, :] = jnp.exp(last) * S0 + mm(
                k[x].astype(F32) * jnp.exp(last - g[x]), Us, 0, 0
            )


def bwd_kernel(
    H, DV, end, first, p_ref, halo_ref, taps_ref, par_ref, u_ref, t_ref, s_ref, do_ref, *refs
):
    C = CHUNK
    W = H * (2 * DK + DV)
    dp_ref, dtaps_ref, dpar_ref, dS, carry_ref, ext, dext = refs[-7:]
    step = pl.program_id(0)

    @pl.when(step == 0)
    def _():
        if first:
            dS[...] = jnp.zeros_like(dS)
            dext[C : C + HALO, :] = jnp.zeros((HALO, W), F32)
            dtaps_ref[...] = jnp.zeros_like(dtaps_ref)
            dpar_ref[...] = jnp.zeros_like(dpar_ref)
        else:
            dS[...] = refs[3][...]
            dext[C : C + HALO, :] = refs[4][...]
            dtaps_ref[...] = refs[1][...]
            dpar_ref[...] = refs[2][...]

    @pl.when(step > 0)
    def _():
        dext[C : C + HALO, :] = dext[0:HALO, :]

    @pl.when(step == end)
    def _():
        ext[0:HALO, :] = jnp.zeros((HALO, W), F32)

    @pl.when(step < end)
    def _():
        ext[0:HALO, :] = halo_ref[:, 0:W]

    ext[HALO : HALO + C, :] = p_ref[:, 0:W]
    i, j = grids(C)
    low, strict = i >= j, i > j
    lane = lax.broadcasted_iota(jnp.int32, (C, 128), 1)
    last_row = lax.broadcasted_iota(jnp.int32, (C, 1), 0) == C - 1
    tail = p_ref[:, W : W + 128]
    running, log_decay, beta, raised = decay_of(tail, par_ref)
    across = jnp.transpose(running)
    d_running = jnp.zeros((C, 128), F32)
    d_beta = jnp.zeros((C, 128), F32)

    def gradient_in(columns, mixed, sig, d_act):
        dext[0:C, columns] = d_act * sig * (1.0 + mixed * (1.0 - sig))

    for h in range(H):
        q_columns = slice(h * DK, (h + 1) * DK)
        k_columns = slice(H * DK + h * DK, H * DK + (h + 1) * DK)
        v_columns = slice(2 * H * DK + h * DV, 2 * H * DK + (h + 1) * DV)
        q_mixed = conv_of(taps_ref, ext, q_columns, C)
        k_mixed = conv_of(taps_ref, ext, k_columns, C)
        v_mixed = conv_of(taps_ref, ext, v_columns, C)
        q_sig, k_sig, v_sig = (jax.nn.sigmoid(x) for x in (q_mixed, k_mixed, v_mixed))
        q_act, k_act = q_mixed * q_sig, k_mixed * k_sig
        q_inv = lax.rsqrt(jnp.sum(q_act * q_act, axis=1, keepdims=True) + 1e-06)
        k_inv = lax.rsqrt(jnp.sum(k_act * k_act, axis=1, keepdims=True) + 1e-06)
        q = (q_act * (q_inv * DK**-0.5)).astype(BF)
        k = (k_act * k_inv).astype(BF)
        v = (v_mixed * v_sig).astype(BF)
        b, g, gr = beta[:, H + h : H + h + 1], running[:, h : h + 1], across[h : h + 1, :]
        hv = slice(h * DV, (h + 1) * DV)
        hk = slice(h * DK, (h + 1) * DK)
        U = split(u_ref[:, hv])
        T = split(t_ref[:, h * C : (h + 1) * C])
        S0 = s_ref[0, hk, :]
        Ss = split(S0)
        dO = split(do_ref[:, hv])
        qf, kf = q.astype(F32), k.astype(F32)
        D = jnp.exp(jnp.where(low, g - gr, -1e30))
        kk, qk = dot1(k, k, 1, 1), dot1(q, k, 1, 1)
        bD = b * D
        A, P = jnp.where(strict, kk * bD, 0.0), qk * D
        last = gr[:, C - 1 : C]
        gam, e, G = jnp.exp(g), jnp.exp(last - g), jnp.exp(last)
        dS1 = dS[hk, :]
        dSs = split(dS1)
        dU = mm(P, dO, 0, 0) + mm(kf * e, dSs)
        dR = mm(T, dU, 0, 0)
        dRs = split(dR)
        dS[hk, :] = G * dS1 + mm(qf * gam, dO, 0, 0) - mm(kf * (b * gam), dRs, 0, 0)
        dP = jnp.where(low, mm(dO, U, 1, 1), 0.0)
        dA = jnp.where(strict, -mm(dRs, U, 1, 1), 0.0)
        Rb = v.astype(F32) - gam * mm(k, Ss)
        db = jnp.sum(dR * Rb, axis=1, keepdims=True) + jnp.sum(dA * kk * D, axis=1, keepdims=True)
        dOS = gam * mm(dO, Ss, 1, 1)
        dRS = (b * gam) * mm(dRs, Ss, 1, 1)
        UdS = e * mm(U, dSs, 1, 1)
        M1, M2 = split(dP * D), split(dA * bD)
        dq = dOS + mm(M1, k)
        dk = UdS - dRS + mm(M1, q, 0, 0) + mm(M2, k) + mm(M2, k, 0, 0)
        X = dP * P + dA * A
        uk = jnp.sum(UdS * kf, axis=1, keepdims=True)
        total = jnp.sum(uk, axis=0, keepdims=True) + G * jnp.sum(
            jnp.sum(S0 * dS1, axis=1, keepdims=True), axis=0, keepdims=True
        )
        dg = (
            jnp.sum(dOS * qf - dRS * kf + X - jnp.transpose(X), axis=1, keepdims=True)
            - uk
            + jnp.where(last_row, total, 0.0)
        )
        d_running = jnp.where(lane == h, dg, d_running)
        d_beta = jnp.where(lane == H + h, db, d_beta)
        q_in = jnp.sum(dq * q_act, axis=1, keepdims=True) * (q_inv * q_inv)
        gradient_in(q_columns, q_mixed, q_sig, (q_inv * DK**-0.5) * (dq - q_act * q_in))
        k_in = jnp.sum(dk * k_act, axis=1, keepdims=True) * (k_inv * k_inv)
        gradient_in(k_columns, k_mixed, k_sig, k_inv * (dk - k_act * k_in))
        gradient_in(v_columns, v_mixed, v_sig, b * dR)
    for start in range(0, W, 512):
        columns = slice(start, start + 512)
        here = dext[0:C, columns]
        total = taps_ref[3:4, columns] * here
        dtaps_ref[3:4, columns] += jnp.sum(
            here * ext[HALO : HALO + C, columns], axis=0, keepdims=True
        )
        for tap in range(3):
            total = total + taps_ref[tap : tap + 1, columns] * dext[3 - tap : 3 - tap + C, columns]
            dtaps_ref[tap : tap + 1, columns] += jnp.sum(
                here * ext[HALO - 3 + tap : HALO - 3 + tap + C, columns], axis=0, keepdims=True
            )
        dp_ref[:, columns] = total.astype(BF)
    ones = jnp.where(i >= j, 1.0, 0.0).astype(BF)
    d_log = exact_sum(ones, d_running, 0)
    d_raised = d_log * par_ref[0:1, :] * jax.nn.sigmoid(raised)
    d_tail = d_raised + d_beta * beta * (1.0 - beta)
    dp_ref[:, W : W + 128] = d_tail.astype(BF)
    dpar_ref[0:1, :] += jnp.sum(d_log * log_decay, axis=0, keepdims=True)
    dpar_ref[1:2, :] += jnp.sum(d_raised, axis=0, keepdims=True)
    carry_ref[...] = dext[0:HALO, :]


def room(mebibytes):
    return pltpu.CompilerParams(vmem_limit_bytes=mebibytes * 2**20)


def row_block(rows, width, at=lambda s: s):
    return pl.BlockSpec((rows, width), lambda s: (at(s), 0))


def whole_block(array):
    return pl.BlockSpec(array.shape, lambda s: (0,) * array.ndim)


def mixer_fwd(projected, taps, par, heads, start, count, before=None, NC=2):
    L, wide = projected.shape
    H, C = heads, CHUNK
    W = taps.shape[1]
    DV = W // H - 2 * DK
    f = jax.ShapeDtypeStruct
    base = start // NC
    shapes = [f((L, H * DV), F32), f((L, H * DV), F32), f((L, H * C), F32), f((L // C, H * DK, DV), F32)]
    more, more_specs, aliases = [], [], {}
    if before is not None:
        more = [before[4]] + list(before[:4])
        more_specs = [whole_block(before[4])] + [pl.BlockSpec(memory_space=pl.ANY)] * 4
        aliases = {5 + n: n for n in range(4)}
    return pl.pallas_call(
        functools.partial(fwd_kernel, H, DV, NC, start),
        grid=(count // NC,),
        in_specs=[
            row_block(NC * C, wide, lambda s: base + s),
            row_block(HALO, wide, lambda s: jnp.maximum((base + s) * (NC * C // HALO) - 1, 0)),
            whole_block(taps),
            whole_block(par),
        ]
        + more_specs,
        out_specs=[
            row_block(NC * C, H * DV, lambda s: base + s),
            row_block(NC * C, H * DV, lambda s: base + s),
            row_block(NC * C, H * C, lambda s: base + s),
            pl.BlockSpec((NC, H * DK, DV), lambda s: (base + s, 0, 0)),
            pl.BlockSpec((H * DK, DV), lambda s: (0, 0)),
        ],
        out_shape=shapes + [f((H * DK, DV), F32)],
        scratch_shapes=[pltpu.VMEM((NC * C + HALO, W), F32)],
        input_output_aliases=aliases,
        compiler_params=room(22),
        cost_estimate=pl.CostEstimate(
            flops=3 * 10**9 * count, bytes_accessed=3 * 2**20 * count, transcendentals=0
        ),
        name="mixer_fwd",
    )(projected, projected, taps, par, *more)


def mixer_bwd(projected, taps, par, written, inverse, states, grad_heads, heads, end, count, before=None):
    L, wide = projected.shape
    H, C = heads, CHUNK
    W = taps.shape[1]
    DV = W // H - 2 * DK
    f = jax.ShapeDtypeStruct

    def back(s):
        return end - s

    more, more_specs, aliases = [], [], {}
    if before is not None:
        more = list(before)
        more_specs = [pl.BlockSpec(memory_space=pl.ANY)] + [whole_block(a) for a in before[1:]]
        aliases = {8: 0}
    state, halo = f((H * DK, DV), F32), f((HALO, W), F32)
    return pl.pallas_call(
        functools.partial(bwd_kernel, H, DV, end, before is None),
        grid=(count,),
        in_specs=[
            row_block(C, wide, back),
            row_block(HALO, wide, lambda s: jnp.maximum(back(s) * (C // HALO) - 1, 0)),
            whole_block(taps),
            whole_block(par),
            row_block(C, H * DV, back),
            row_block(C, H * C, back),
            pl.BlockSpec((1, H * DK, DV), lambda s: (back(s), 0, 0)),
            row_block(C, H * DV, back),
        ]
        + more_specs,
        out_specs=[
            row_block(C, wide, back),
            whole_block(taps),
            whole_block(par),
            whole_block(state),
            whole_block(halo),
        ],
        out_shape=[f((L, wide), BF), f(taps.shape, F32), f(par.shape, F32), state, halo],
        scratch_shapes=[pltpu.VMEM((C + HALO, W), F32), pltpu.VMEM((C + HALO, W), F32)],
        input_output_aliases=aliases,
        compiler_params=room(22),
        cost_estimate=pl.CostEstimate(
            flops=6 * 10**9 * count, bytes_accessed=4 * 2**20 * count, transcendentals=0
        ),
        name="mixer_bwd",
    )(projected, projected, taps, par, written, inverse, states, grad_heads, *more)


def gate_fwd_kernel(DV, o_ref, gate_ref, gain_ref, out_ref):
    for start in range(0, o_ref.shape[1], DV):
        cut = slice(start, start + DV)
        heads, gate = o_ref[:, cut], gate_ref[:, cut]
        inverse = lax.rsqrt(jnp.mean(heads * heads, axis=1, keepdims=True) + 1e-05)
        out_ref[:, cut] = (heads * inverse * gain_ref[...] * (gate * jax.nn.sigmoid(gate))).astype(BF)


def gate_fwd(heads_out, gate_proj, gain):
    L, width = heads_out.shape
    rows = L // 8
    return pl.pallas_call(
        functools.partial(gate_fwd_kernel, gain.shape[1]),
        grid=(8,),
        in_specs=[row_block(rows, width), row_block(rows, width), whole_block(gain)],
        out_specs=row_block(rows, width),
        out_shape=jax.ShapeDtypeStruct((L, width), BF),
        compiler_params=room(12),
        cost_estimate=pl.CostEstimate(flops=10**6, bytes_accessed=10**5, transcendentals=0),
        name="gate_fwd",
    )(heads_out, gate_proj, gain)


def gate_bwd_kernel(DV, o_ref, gate_ref, gain_ref, in_ref, do_ref, dgate_ref, dgain_ref):
    @pl.when(pl.program_id(0) == 0)
    def _():
        dgain_ref[...] = jnp.zeros_like(dgain_ref)

    for start in range(0, o_ref.shape[1], DV):
        cut = slice(start, start + DV)
        heads, gate, grad = o_ref[:, cut], gate_ref[:, cut], in_ref[:, cut]
        inverse = lax.rsqrt(jnp.mean(heads * heads, axis=1, keepdims=True) + 1e-05)
        normed = heads * inverse
        sig = jax.nn.sigmoid(gate)
        dgate_ref[:, cut] = (
            grad * (normed * gain_ref[...]) * (sig * (1.0 + gate * (1.0 - sig)))
        ).astype(BF)
        d_scaled = grad * (gate * sig)
        dgain_ref[...] += jnp.sum(d_scaled * normed, axis=0, keepdims=True)
        d_normed = d_scaled * gain_ref[...]
        do_ref[:, cut] = inverse * (
            d_normed - normed * jnp.mean(d_normed * normed, axis=1, keepdims=True)
        )


def gate_bwd(heads_out, gate_proj, gain, grad_mixer):
    L, width = heads_out.shape
    rows = L // 8
    f = jax.ShapeDtypeStruct
    return pl.pallas_call(
        functools.partial(gate_bwd_kernel, gain.shape[1]),
        grid=(8,),
        in_specs=[row_block(rows, width), row_block(rows, width), whole_block(gain), row_block(rows, width)],
        out_specs=[row_block(rows, width), row_block(rows, width), whole_block(gain)],
        out_shape=[f((L, width), F32), f((L, width), BF), f(gain.shape, F32)],
        compiler_params=room(14),
        cost_estimate=pl.CostEstimate(flops=10**6, bytes_accessed=10**5, transcendentals=0),
        name="gate_bwd",
    )(heads_out, gate_proj, gain, grad_mixer)


def at_place(place, n):
    return jnp.where(place < n // 2, 2 * place, 2 * (n - place) - 1)


def place_of(index, n):
    return jnp.where(index % 2 == 0, index // 2, n - (index + 1) // 2)


def ring_pairs(n):
    order = list(range(0, n, 2)) + list(range(n - 1, 0, -2))
    ahead = [(order[i], order[(i + 1) % n]) for i in range(n)]
    return ahead, [(d, s) for s, d in ahead]


def behind(d):
    n = lax.axis_size("dp")
    return at_place((place_of(lax.axis_index("dp"), n) - d + n) % n, n)


def after(values, token):
    return lax.optimization_barrier((values, token))[0]


class GatherRing:
    def __init__(self, shard):
        half = shard.shape[0] // 2
        self.first, self.second = [shard[:half]], [shard[half:]]
        self.n = lax.axis_size("dp")

    def send(self, token):
        ahead, back = ring_pairs(self.n)
        first, second = after((self.first[-1], self.second[-1]), token)
        self.first.append(lax.ppermute(first, "dp", ahead))
        self.second.append(lax.ppermute(second, "dp", back))

    def last(self):
        return self.first[-1], self.second[-1]

    def through(self):
        return len(self.first) == self.n

    def finish(self, widths):
        half = self.first[0].shape[0]
        fulls = [jnp.zeros((self.n * 2 * half, width), BF) for width in widths]
        for hop in range(self.n):
            for piece, at in (
                (self.first[hop], behind(hop) * 2 * half),
                (self.second[hop], behind(self.n - hop) * 2 * half + half),
            ):
                fulls = [
                    lax.dynamic_update_slice(full, part, (at, 0))
                    for full, part in zip(fulls, columns(piece, widths))
                ]
        return fulls


def land_kernel(widths, at_ref, first, second, *refs):
    count = len(widths)
    for arrived, mine, out in (
        (first, refs[:count], refs[-2]),
        (second, refs[count : 2 * count], refs[-1]),
    ):
        start = 0
        for width, term in zip(widths, mine):
            cut = slice(start, start + width)
            out[:, cut] = (arrived[:, cut].astype(F32) + term[...].astype(F32)).astype(BF)
            start += width


def landed(flying, partials, places):
    widths = [partial.shape[1] for partial in partials]
    rows, wide = flying[0].shape
    steps = 2
    block = rows // steps
    sent = pl.BlockSpec((block, wide), lambda s, at: (s, 0))

    def term(width, side):
        return pl.BlockSpec(
            (block, width), lambda s, at: (at[side] * (2 * steps) + side * steps + s, 0)
        )

    terms = [term(width, side) for side in (0, 1) for width in widths]
    return pl.pallas_call(
        functools.partial(land_kernel, widths),
        grid_spec=pltpu.PrefetchScalarGridSpec(
            num_scalar_prefetch=1, grid=(steps,), in_specs=[sent, sent] + terms, out_specs=[sent, sent]
        ),
        out_shape=[jax.ShapeDtypeStruct((rows, wide), BF)] * 2,
        compiler_params=room(10),
        cost_estimate=pl.CostEstimate(flops=10**6, bytes_accessed=10**6, transcendentals=0),
        name="land",
    )(jnp.stack(places).astype(jnp.int32), *flying, *partials, *partials)


class ScatterRing:
    def __init__(self, pairs, token, partials=None):
        self.n = lax.axis_size("dp")
        self.hop = 0
        self.pairs, self.partials = pairs, partials
        self.sums = tuple(
            jnp.concatenate(self.terms_of(place, side, token), axis=1).astype(BF)
            for place, side in ((1, 0), (self.n - 1, 1))
        )

    def terms_of(self, place, side, token):
        terms = []
        for number, (features, grads) in enumerate(self.pairs):
            half = features.shape[1] // self.n // 2
            at = behind(place % self.n) * (2 * half) + side * half
            if self.partials is not None:
                terms.append(lax.dynamic_slice_in_dim(self.partials[number], at, half, 0))
                continue
            left = lax.dynamic_slice_in_dim(features, at, half, 1)
            terms.append(contract_rows(*after((left, grads), token)))
        return terms

    def prepare(self, token):
        self.partials = [
            contract_rows(*after((features, grads), token)).astype(BF)
            for features, grads in self.pairs
        ]
        return self.partials

    def send(self, token):
        ahead, back = ring_pairs(self.n)
        first, second = after(self.sums, token)
        self.flying = lax.ppermute(first, "dp", ahead), lax.ppermute(second, "dp", back)

    def land(self, token):
        self.hop += 1
        flying = after(self.flying, token)
        if self.hop < self.n - 1:
            places = behind((self.hop + 1) % self.n), behind((self.n - 1 - self.hop) % self.n)
            self.sums = tuple(landed(flying, self.partials, places))
            return self.sums
        self.sums = tuple(
            [
                x.astype(F32) + y.astype(F32)
                for x, y in zip(
                    columns(arrived, [part.shape[1] for part in self.partials]),
                    self.terms_of(0, side, ()),
                )
            ]
            for side, arrived in enumerate(flying)
        )
        return self.sums

    def done(self):
        return self.hop == self.n - 1

    def results(self):
        return [jnp.concatenate(halves, axis=0) for halves in zip(*self.sums)]


def slot(token, rings, pieces=(), gathers=()):
    rings = [ring for ring in rings if not ring.done()]
    gathers = [ring for ring in gathers if not ring.through()]
    for ring in rings:
        ring.send(token)
    for ring in gathers:
        ring.send(token)
    for piece in pieces:
        token = piece(token)
    token = [ring.land(token) for ring in rings] or token
    if gathers:
        token = token, [ring.last() for ring in gathers]
    return token


def run_out(token, rings, pieces=(), gathers=()):
    pieces = list(pieces)
    while (
        pieces
        or any(not ring.done() for ring in rings)
        or any(not ring.through() for ring in gathers)
    ):
        token = slot(token, rings, [pieces.pop(0)] if pieces else (), gathers)
    return token


def contract_rows(left, right):
    return lax.dot_general(
        left, right, (((0,), (0,)), ((), ())), preferred_element_type=jnp.float32
    )


def times_transposed(left, right):
    return lax.dot_general(
        left, right, (((1,), (1,)), ((), ())), preferred_element_type=jnp.float32
    )


CORES = [(0, 1), (1, 0), (2, 3), (3, 2)]
PAIRS = [(0, 2), (2, 0), (1, 3), (3, 1)]


class Spread:
    def __init__(self, block):
        self.block = block
        self.plain = lax.axis_size("tensor") != 4
        if not self.plain:
            self.far = lax.ppermute(block, "tensor", PAIRS)
            self.near = lax.ppermute(block, "tensor", CORES)

    def turn(self, token):
        if self.plain:
            return token
        far = after(self.far, token)
        self.far_near = lax.ppermute(far, "tensor", CORES)
        return far

    def rows(self, token=()):
        if self.plain:
            return lax.all_gather(after(self.block, token), "tensor", axis=0, tiled=True)
        rank = lax.axis_index("tensor")
        rows, width = self.block.shape
        out = jnp.zeros((4 * rows, width), self.block.dtype)
        parts = after((self.block, self.near, self.far, self.far_near), token)
        for flip, part in enumerate(parts):
            out = lax.dynamic_update_slice_in_dim(out, part, (rank ^ flip) * rows, 0)
        return out


def spread_rows(block):
    spread = Spread(block)
    spread.turn(())
    return spread.rows()


class RowSum:
    def __init__(self, product, rows):
        self.product, self.rows = product, rows
        self.rank = lax.axis_index("tensor")
        self.plain = lax.axis_size("tensor") != 4

    def term(self, flip, token):
        return self.product((self.rank ^ flip) * self.rows, token)

    def far(self, token):
        if self.plain:
            whole = [self.product(i * self.rows, token) for i in range(lax.axis_size("tensor"))]
            self.total = lax.psum_scatter(
                jnp.concatenate(whole, axis=0), "tensor", scatter_dimension=0, tiled=True
            )
            return self.total
        self.sent = self.term(3, token).astype(BF)
        self.far_near = lax.ppermute(self.sent, "tensor", CORES)
        return self.sent

    def far_sum(self, token):
        if self.plain:
            return token
        total = (self.term(2, token) + self.far_near.astype(F32)).astype(BF)
        self.from_far = lax.ppermute(total, "tensor", PAIRS)
        return total

    def near(self, token):
        if self.plain:
            return token
        sent = self.term(1, token).astype(BF)
        self.from_near = lax.ppermute(sent, "tensor", CORES)
        return sent

    def own(self, token):
        if self.plain:
            return token
        self.mine = self.term(0, token)
        return self.mine

    def result(self, token):
        if self.plain:
            return after(self.total, token)
        mine = after(self.mine, token)
        return mine + self.from_near.astype(F32) + self.from_far.astype(F32)

    def pieces(self):
        return [self.far, self.far_sum, self.near, self.own]


def summed_rows(pairs, rows):
    def product(start, token):
        total = None
        for grads, weight in pairs:
            part, other = after((lax.dynamic_slice_in_dim(grads, start, rows, 0), weight), token)
            part = times_transposed(part, other)
            total = part if total is None else total + part
        return total

    return RowSum(product, rows)


def sum_over(values, axis):
    n = lax.axis_size(axis)
    if n & (n - 1):
        return lax.psum(values, axis)
    step = 1
    while step < n:
        values = values + lax.ppermute(values, axis, [(i, i ^ step) for i in range(n)])
        step *= 2
    return values


def packed(arrays):
    flat = jnp.concatenate([a.reshape(-1) for a in arrays])
    pad = -flat.shape[0] % 1024
    return jnp.pad(flat, (0, pad)).reshape(-1, 128)


def unpacked(values, shapes):
    flat = values.reshape(-1)
    out, start = [], 0
    for shape in shapes:
        size = 1
        for extent in shape:
            size *= extent
        out.append(flat[start : start + size].reshape(shape))
        start += size
    return out


def norm_back(values, inverse, gain, incoming):
    scaled = incoming * gain
    width = values.shape[1]
    grad_values = (
        inverse * scaled
        - values
        * inverse
        * inverse
        * inverse
        * jnp.sum(scaled * values, axis=1, keepdims=True)
        / width
    )
    grad_gain = jnp.sum(incoming * values * inverse, axis=0)
    return (grad_values, grad_gain)


def place_slice(local, whole, rank, axis):
    return lax.dynamic_update_slice_in_dim(
        jnp.zeros_like(whole), local, rank * local.shape[axis], axis
    )


def columns(array, widths):
    out, start = [], 0
    for width in widths:
        out.append(array[:, start : start + width])
        start += width
    return out


def shards(
    inputs,
    lengths,
    cotangent,
    norm_attn,
    norm_ffn,
    norm_heads,
    w_query,
    w_key,
    w_value,
    w_out_gate,
    w_decay,
    w_beta,
    w_output,
    conv_query,
    conv_key,
    conv_value,
    decay_log,
    decay_bias,
    w_ffn_gate,
    w_ffn_up,
    w_ffn_down,
):
    rows = inputs.shape[0]
    width = inputs.shape[1]
    tensor_rank = lax.axis_index("tensor")
    positions = tensor_rank * rows + jnp.arange(rows, dtype=jnp.int32)
    valid = (positions < lengths[0]).astype(jnp.float32)[:, None]
    heads_here = w_decay.shape[1]
    widths = [w.shape[1] for w in (w_query, w_key, w_value, w_decay, w_beta)]
    fill = -sum(widths) % 128
    mixed_shard = jnp.pad(
        jnp.concatenate((w_query, w_key, w_value, w_decay, w_beta), axis=1), ((0, 0), (0, fill))
    )
    ffn_width = w_ffn_gate.shape[1]
    kept = {}
    mixed_ring = GatherRing(mixed_shard)
    mixed_ring.send(())
    inputs, cotangent = after((inputs, cotangent), mixed_ring.last())
    token = run_out(mixed_ring.last(), (), (), (mixed_ring,))

    def arrived(hop):
        at = min(hop, mixed_ring.n - 1)
        return mixed_ring.first[at], mixed_ring.second[at]

    gate_shards = after((w_out_gate, w_output), arrived(3))
    ffn_shards = after((w_ffn_gate, w_ffn_up, w_ffn_down), arrived(4))
    gate_ring = GatherRing(jnp.concatenate((gate_shards[0], gate_shards[1].T), axis=1))
    ffn_ring = GatherRing(
        jnp.concatenate((ffn_shards[0], ffn_shards[1], ffn_shards[2].T), axis=1)
    )
    [mixed_full] = mixed_ring.finish([mixed_shard.shape[1]])

    gain_attn = norm_attn
    gain_ffn = norm_ffn
    stream_in = inputs.astype(jnp.float32)
    grad_out = valid * cotangent.astype(jnp.float32)
    inverse_in = lax.rsqrt(jnp.mean(stream_in * stream_in, axis=1, keepdims=True) + 1e-06)
    full_in = spread_rows((stream_in * inverse_in * gain_attn).astype(jnp.bfloat16))

    def here(array):
        size = array.shape[-1] // lax.axis_size("tensor")
        return lax.dynamic_slice_in_dim(array, tensor_rank * size, size, array.ndim - 1)

    taps = jnp.concatenate((here(conv_query), here(conv_key), here(conv_value)), axis=1)
    par = jnp.pad(
        jnp.stack((-jnp.exp(here(decay_log)), here(decay_bias))), ((0, 6), (0, 128 - heads_here))
    )
    gain_heads = norm_heads[None, :]
    chunks = full_in.shape[0] // CHUNK
    parts = 4

    def project(token):
        kept["projected"] = jnp.dot(
            *after((full_in, mixed_full), token), preferred_element_type=jnp.float32
        )
        kept["forward"] = None
        return kept["projected"]

    def forward_part(start):
        def piece(token):
            kept["forward"] = mixer_fwd(
                after(kept["projected"], token),
                taps,
                par,
                heads_here,
                start,
                chunks // parts,
                kept["forward"],
            )
            return kept["forward"][4]

        return piece

    token = run_out(
        token,
        (),
        [project] + [forward_part(i * (chunks // parts)) for i in range(parts)],
        (gate_ring,),
    )
    projected = kept["projected"]
    heads_out, written, inverse, states, _ = kept["forward"]
    gate_full, output_full = gate_ring.finish([w_out_gate.shape[1], w_output.shape[0]])

    def gate(token):
        kept["gate"] = jnp.dot(
            *after((full_in, gate_full), token), preferred_element_type=jnp.float32
        )
        kept["mixer"] = gate_fwd(heads_out, kept["gate"], gain_heads)
        return kept["mixer"]

    def attend(token):
        kept["attn"] = summed_rows(((kept["mixer"], output_full),), rows)
        return kept["attn"].far_sum(kept["attn"].far(token))

    def attend_own(token):
        return kept["attn"].own(kept["attn"].near(token))

    def middle(token):
        kept["branch"] = kept["attn"].result(token)
        stream = stream_in + kept["branch"]
        kept["stream"] = stream
        kept["inverse"] = lax.rsqrt(jnp.mean(stream * stream, axis=1, keepdims=True) + 1e-06)
        normed = (stream * kept["inverse"] * gain_ffn).astype(jnp.bfloat16)
        kept["full_mid"] = spread_rows(normed)
        return normed

    token = run_out(token, (), [gate, attend, attend_own, middle], (ffn_ring,))
    gate_proj, mixer, branch_attn = kept["gate"], kept["mixer"], kept["branch"]
    stream, inverse_mid, full_mid = kept["stream"], kept["inverse"], kept["full_mid"]
    ffn_gate_full, ffn_up_full, down_full = ffn_ring.finish(
        [ffn_width, ffn_width, w_ffn_down.shape[0]]
    )
    grad_ffn = spread_rows(after(grad_out.astype(jnp.bfloat16), full_mid))

    token, full_mid_in = after((token, full_mid), ffn_ring.last())
    ffn_gate = jnp.dot(full_mid_in, ffn_gate_full, preferred_element_type=jnp.float32)
    ffn_up = jnp.dot(full_mid_in, ffn_up_full, preferred_element_type=jnp.float32)
    sigma = jax.nn.sigmoid(ffn_gate)
    silu_gate = ffn_gate * sigma
    hidden = (silu_gate * ffn_up).astype(jnp.bfloat16)
    grad_hidden = jnp.dot(grad_ffn, down_full, preferred_element_type=jnp.float32)
    grad_gate_in = grad_hidden * ffn_up * sigma * (1.0 + ffn_gate * (1.0 - sigma))
    grad_gate_in = grad_gate_in.astype(jnp.bfloat16)
    grad_up_in = (grad_hidden * silu_gate).astype(jnp.bfloat16)
    token = grad_gate_in, grad_up_in, hidden
    ffn_scatter = ScatterRing(
        ((full_mid, grad_gate_in), (full_mid, grad_up_in), (grad_ffn, hidden)), token
    )
    token = ffn_scatter.sums
    mid_sum = summed_rows(((grad_gate_in, ffn_gate_full), (grad_up_in, ffn_up_full)), rows)

    def mid_own(token):
        return mid_sum.own(mid_sum.near(token))

    def middle_back(token):
        through, kept["norm_ffn"] = norm_back(stream, inverse_mid, gain_ffn, mid_sum.result(token))
        kept["grad_stream"] = grad_out + through
        low = kept["grad_stream"].astype(jnp.bfloat16)
        kept["spread"] = Spread(low)
        return low

    def turn(token):
        token = ffn_sum.far_sum(ffn_sum.far(kept["spread"].turn(token)))
        kept["grad_attn"] = kept["spread"].rows(token)
        return kept["grad_attn"]

    def attend_back(token):
        grad_mixer = jnp.dot(
            *after((kept["grad_attn"], output_full), token), preferred_element_type=jnp.float32
        )
        kept["gate_back"] = gate_bwd(heads_out, gate_proj, gain_heads, grad_mixer)
        kept["backward"] = None
        return kept["gate_back"][0]

    def backward_part(end):
        def piece(token):
            kept["backward"] = mixer_bwd(
                projected,
                taps,
                par,
                written,
                inverse,
                states,
                after(kept["gate_back"][0], token),
                heads_here,
                end,
                chunks // parts,
                kept["backward"],
            )
            return kept["backward"][3]

        return piece

    ffn_sum = summed_rows(((hidden, down_full),), rows)
    backward = [backward_part(chunks - 1 - i * (chunks // parts)) for i in range(parts)]
    token = run_out(
        token,
        (ffn_scatter,),
        [
            ffn_scatter.prepare,
            lambda t: mid_sum.far_sum(mid_sum.far(t)),
            mid_own,
            middle_back,
            turn,
            attend_back,
        ]
        + backward[:1],
    )
    grad_stream, grad_norm_ffn, grad_attn = kept["grad_stream"], kept["norm_ffn"], kept["grad_attn"]
    _, grad_gate_proj, heads_gain_grad = kept["gate_back"]
    gate_scatter = ScatterRing(
        ((full_in, grad_gate_proj), (grad_attn, mixer)), token
    )
    token = token, gate_scatter.sums

    def in_far(token):
        kept["in_sum"] = summed_rows(
            ((grad_gate_proj, gate_full), (kept["backward"][0], mixed_full)), rows
        )
        return kept["in_sum"].far(token)

    def leave(token):
        kept["branch_ffn"] = ffn_sum.result(token)
        kept["outputs"] = (valid * (stream + kept["branch_ffn"])).astype(jnp.bfloat16)
        return kept["outputs"]

    def in_far_sum(token):
        return kept["in_sum"].far_sum(token)

    def in_near(token):
        return kept["in_sum"].near(token)

    def in_own(token):
        return kept["in_sum"].own(token)

    def last_back(token):
        through, kept["norm_attn"] = norm_back(
            stream_in, inverse_in, gain_attn, kept["in_sum"].result(token)
        )
        kept["grad_inputs"] = grad_stream + through
        return kept["grad_inputs"]

    token = run_out(
        token,
        (gate_scatter,),
        [gate_scatter.prepare]
        + backward[1:]
        + [in_far, in_far_sum, lambda t: in_near(ffn_sum.near(t))],
    )
    grad_projected, grad_taps, grad_par, _, _ = kept["backward"]
    mixed_scatter = ScatterRing(((full_in, grad_projected),), token)
    token = token, mixed_scatter.sums
    token = slot(token, (mixed_scatter,), [ffn_sum.own, mixed_scatter.prepare])
    token = slot(token, (mixed_scatter,), [leave, in_own])
    branch_ffn, outputs = kept["branch_ffn"], kept["outputs"]
    stat_sums = jnp.stack(
        [
            jnp.sum(valid * stream_in * stream_in),
            jnp.sum(valid * branch_attn * branch_attn),
            jnp.sum(valid * branch_ffn * branch_ffn),
            jnp.sum(valid),
        ]
    )
    local = columns(grad_taps, widths[:3]) + [grad_par[0, :heads_here], grad_par[1, :heads_here]]
    whole = [conv_query, conv_key, conv_value, decay_log, decay_bias]
    common = [stat_sums, grad_norm_ffn, heads_gain_grad[0]]
    def common_over_dp(token):
        kept["common"] = sum_over(after(packed(common + local), token), "dp")
        return kept["common"]

    def common_over_tensor(token):
        sums = unpacked(kept["common"], [a.shape for a in common + local])
        spread = [
            place_slice(part, array, tensor_rank, part.ndim - 1)
            for part, array in zip(sums[3:], whole)
        ]
        kept["common"] = sum_over(after(packed(sums[:3] + spread), token), "tensor")
        return kept["common"]

    def last_over_dp(token):
        kept["last"] = sum_over(after(packed([kept["norm_attn"]]), token), "dp")
        return kept["last"]

    def last_over_tensor(token):
        kept["last"] = sum_over(after(kept["last"], token), "tensor")
        return kept["last"]

    token = run_out(
        token,
        (mixed_scatter,),
        [last_back, common_over_dp, last_over_dp, common_over_tensor, last_over_tensor],
    )
    grad_inputs = kept["grad_inputs"]
    owned_gate, owned_up, owned_down = ffn_scatter.results()
    owned_out_gate, owned_output = gate_scatter.results()
    owned_query, owned_key, owned_value, owned_decay, owned_beta = columns(
        mixed_scatter.results()[0], widths
    )
    (
        stat_sums,
        total_ffn_gain,
        total_heads_gain,
        total_conv_query,
        total_conv_key,
        total_conv_value,
        total_decay_log,
        total_decay_bias,
    ) = unpacked(kept["common"], [a.shape for a in common + whole])
    [total_attn_gain] = unpacked(kept["last"], [norm_attn.shape])
    statistics = jnp.sqrt(stat_sums[:3] / (stat_sums[3] * width))
    return (
        outputs,
        statistics,
        grad_inputs,
        total_attn_gain,
        total_ffn_gain,
        total_heads_gain,
        owned_query,
        owned_key,
        owned_value,
        owned_out_gate,
        owned_decay,
        owned_beta,
        owned_output.T,
        total_conv_query,
        total_conv_key,
        total_conv_value,
        total_decay_log,
        total_decay_bias,
        owned_gate,
        owned_up,
        owned_down.T,
    )


def solution(mesh):
    in_specs = (
        P(("dp", "tensor"), None),
        P("dp"),
        P(("dp", "tensor"), None),
        P(),
        P(),
        P(),
        P("dp", "tensor"),
        P("dp", "tensor"),
        P("dp", "tensor"),
        P("dp", "tensor"),
        P("dp", "tensor"),
        P("dp", "tensor"),
        P("tensor", "dp"),
        P(),
        P(),
        P(),
        P(),
        P(),
        P("dp", "tensor"),
        P("dp", "tensor"),
        P("tensor", "dp"),
    )
    out_specs = (
        P(("dp", "tensor"), None),
        P(),
        P(("dp", "tensor"), None),
        P(),
        P(),
        P(),
        P("dp", "tensor"),
        P("dp", "tensor"),
        P("dp", "tensor"),
        P("dp", "tensor"),
        P("dp", "tensor"),
        P("dp", "tensor"),
        P("tensor", "dp"),
        P(),
        P(),
        P(),
        P(),
        P(),
        P("dp", "tensor"),
        P("dp", "tensor"),
        P("tensor", "dp"),
    )
    return jax.shard_map(shards, mesh=mesh, in_specs=in_specs, out_specs=out_specs, check_vma=False)
```

```python
import functools

import jax
import jax.numpy as jnp
from jax import lax
from jax.experimental import pallas as pl
from jax.experimental.pallas import tpu as pltpu
from jax.sharding import PartitionSpec as P

BF=jnp.bfloat16; F32=jnp.float32
DK = 128
CHUNK = 128
HALO = 8


def dot1(a, b, ca=1, cb=0):
    return lax.dot_general(a, b, (((ca,), (cb,)), ((), ())), preferred_element_type=F32)


def split(a):
    if a.dtype == BF:
        return a, None
    high = a.astype(BF)
    return high, (a - high.astype(F32)).astype(BF)


def mm(a, b, ca=1, cb=0):
    a_high, a_low = a if isinstance(a, tuple) else split(a)
    b_high, b_low = b if isinstance(b, tuple) else split(b)
    total = dot1(a_high, b_high, ca, cb)
    if b_low is not None:
        total = total + dot1(a_high, b_low, ca, cb)
    if a_low is not None:
        total = total + dot1(a_low, b_high, ca, cb)
    return total


def exact_sum(ones, values, ca):
    high, rest = split(values)
    middle, low = split(values - high.astype(F32))
    return dot1(ones, high, ca) + (dot1(ones, middle, ca) + dot1(ones, low, ca))


def grids(size):
    return (
        lax.broadcasted_iota(jnp.int32, (size, size), 0),
        lax.broadcasted_iota(jnp.int32, (size, size), 1),
    )


def inverses(couplings):
    size = couplings[0].shape[0]
    i, j = grids(size)
    eye = jnp.where(i == j, 1.0, 0.0).astype(F32)

    def same(bits):
        return lax.shift_right_logical(i, bits) == lax.shift_right_logical(j, bits)

    inside = same(3)
    near = [jnp.where(inside, a, 0.0) for a in couplings]
    second = [split(mm(a, a)) for a in map(split, near)]
    fourth = [mm(a, a) for a in second]
    found = [eye - a for a in near]
    found = [x + mm(x, a) for x, a in zip(found, second)]
    found = [x + mm(x, a) for x, a in zip(found, fourth)]
    bits = 3
    while (1 << bits) < size:
        across = jnp.logical_and(same(bits + 1), jnp.logical_not(same(bits)))
        parts = [split(x) for x in found]
        moved = [mm(jnp.where(across, a, 0.0), x) for a, x in zip(couplings, parts)]
        found = [x - mm(p, y) for x, p, y in zip(found, parts, moved)]
        bits += 1
    return found


def conv_of(taps_ref, ext, columns, rows, start=HALO - 3):
    total = taps_ref[0:1, columns] * ext[start : start + rows, columns]
    for tap in range(1, 4):
        total = total + taps_ref[tap : tap + 1, columns] * ext[
            start + tap : start + tap + rows, columns
        ]
    return total


def decay_of(tail, par_ref):
    i, j = grids(CHUNK)
    ones = jnp.where(i >= j, 1.0, 0.0).astype(BF)
    raised = tail + par_ref[1:2, :]
    log_decay = par_ref[0:1, :] * (
        jnp.maximum(raised, 0.0) + jnp.log1p(jnp.exp(-jnp.abs(raised)))
    )
    return exact_sum(ones, log_decay, 1), log_decay, jax.nn.sigmoid(tail), raised


def fwd_kernel(H, DV, NC, start, p_ref, halo_ref, taps_ref, par_ref, *refs):
    C = CHUNK
    R = NC * C
    W = H * (2 * DK + DV)
    o_ref, u_ref, t_ref, s_ref, S, ext = refs[-6:]
    step = pl.program_id(0)

    if start == 0:

        @pl.when(step == 0)
        def _():
            S[...] = jnp.zeros_like(S)
            ext[0:HALO, :] = jnp.zeros((HALO, W), F32)

        @pl.when(step > 0)
        def _():
            ext[0:HALO, :] = halo_ref[:, 0:W]

    else:

        @pl.when(step == 0)
        def _():
            S[...] = refs[0][...]

        ext[0:HALO, :] = halo_ref[:, 0:W]

    ext[HALO : HALO + R, :] = p_ref[:, 0:W]
    i, j = grids(C)
    low, strict = i >= j, i > j
    idx = [(c, h) for c in range(NC) for h in range(H)]
    rows = [slice(c * C, (c + 1) * C) for c in range(NC)]
    q, k, v, b, g, gr = {}, {}, {}, {}, {}, {}
    for h in range(H):
        for part, out, base, size, factor in (
            (0, q, h * DK, DK, DK**-0.5),
            (1, k, H * DK + h * DK, DK, 1.0),
            (2, v, 2 * H * DK + h * DV, DV, None),
        ):
            mixed = conv_of(taps_ref, ext, slice(base, base + size), R)
            mixed = mixed * jax.nn.sigmoid(mixed)
            if factor is not None:
                mixed = mixed * (
                    lax.rsqrt(jnp.sum(mixed * mixed, axis=1, keepdims=True) + 1e-06) * factor
                )
            mixed = mixed.astype(BF)
            for c in range(NC):
                out[c, h] = mixed[rows[c], :]
    for c in range(NC):
        running, _, beta, _ = decay_of(p_ref[rows[c], W : W + 128], par_ref)
        across = jnp.transpose(running)
        for h in range(H):
            b[c, h] = beta[:, H + h : H + h + 1]
            g[c, h] = running[:, h : h + 1]
            gr[c, h] = across[h : h + 1, :]
    D = {x: jnp.exp(jnp.where(low, g[x] - gr[x], -1e30)) for x in idx}
    A = [jnp.where(strict, dot1(k[x], k[x], 1, 1) * b[x] * D[x], 0.0) for x in idx]
    T = dict(zip(idx, inverses(A)))
    P = {x: dot1(q[x], k[x], 1, 1) * D[x] for x in idx}
    gam = {x: jnp.exp(g[x]) for x in idx}
    Ts = {x: split(T[x]) for x in idx}
    TV = {x: mm(Ts[x], b[x] * v[x].astype(F32)) for x in idx}
    TK = {x: mm(Ts[x], b[x] * gam[x] * k[x].astype(F32)) for x in idx}
    for c in range(NC):
        for h in range(H):
            x = (c, h)
            t_ref[rows[c], h * C : (h + 1) * C] = T[x]
            S0 = S[h * DK : (h + 1) * DK, :]
            s_ref[c, h * DK : (h + 1) * DK, :] = S0
            Ss = split(S0)
            U = TV[x] - mm(TK[x], Ss)
            Us = split(U)
            u_ref[rows[c], h * DV : (h + 1) * DV] = U
            o_ref[rows[c], h * DV : (h + 1) * DV] = gam[x] * mm(q[x], Ss) + mm(P[x], Us)
            last = gr[x][:, C - 1 : C]
            S[h * DK : (h + 1) * DK, :] = jnp.exp(last) * S0 + mm(
                k[x].astype(F32) * jnp.exp(last - g[x]), Us, 0, 0
            )


def bwd_kernel(
    H, DV, end, first, p_ref, halo_ref, taps_ref, par_ref, u_ref, t_ref, s_ref, do_ref, *refs
):
    C = CHUNK
    W = H * (2 * DK + DV)
    dp_ref, dtaps_ref, dpar_ref, dS, carry_ref, ext, dext = refs[-7:]
    step = pl.program_id(0)

    @pl.when(step == 0)
    def _():
        if first:
            dS[...] = jnp.zeros_like(dS)
            dext[C : C + HALO, :] = jnp.zeros((HALO, W), F32)
            dtaps_ref[...] = jnp.zeros_like(dtaps_ref)
            dpar_ref[...] = jnp.zeros_like(dpar_ref)
        else:
            dS[...] = refs[3][...]
            dext[C : C + HALO, :] = refs[4][...]
            dtaps_ref[...] = refs[1][...]
            dpar_ref[...] = refs[2][...]

    @pl.when(step > 0)
    def _():
        dext[C : C + HALO, :] = dext[0:HALO, :]

    @pl.when(step == end)
    def _():
        ext[0:HALO, :] = jnp.zeros((HALO, W), F32)

    @pl.when(step < end)
    def _():
        ext[0:HALO, :] = halo_ref[:, 0:W]

    ext[HALO : HALO + C, :] = p_ref[:, 0:W]
    i, j = grids(C)
    low, strict = i >= j, i > j
    lane = lax.broadcasted_iota(jnp.int32, (C, 128), 1)
    last_row = lax.broadcasted_iota(jnp.int32, (C, 1), 0) == C - 1
    tail = p_ref[:, W : W + 128]
    running, log_decay, beta, raised = decay_of(tail, par_ref)
    across = jnp.transpose(running)
    d_running = jnp.zeros((C, 128), F32)
    d_beta = jnp.zeros((C, 128), F32)

    def gradient_in(columns, mixed, sig, d_act):
        dext[0:C, columns] = d_act * sig * (1.0 + mixed * (1.0 - sig))

    for h in range(H):
        q_columns = slice(h * DK, (h + 1) * DK)
        k_columns = slice(H * DK + h * DK, H * DK + (h + 1) * DK)
        v_columns = slice(2 * H * DK + h * DV, 2 * H * DK + (h + 1) * DV)
        q_mixed = conv_of(taps_ref, ext, q_columns, C)
        k_mixed = conv_of(taps_ref, ext, k_columns, C)
        v_mixed = conv_of(taps_ref, ext, v_columns, C)
        q_sig, k_sig, v_sig = (jax.nn.sigmoid(x) for x in (q_mixed, k_mixed, v_mixed))
        q_act, k_act = q_mixed * q_sig, k_mixed * k_sig
        q_inv = lax.rsqrt(jnp.sum(q_act * q_act, axis=1, keepdims=True) + 1e-06)
        k_inv = lax.rsqrt(jnp.sum(k_act * k_act, axis=1, keepdims=True) + 1e-06)
        q = (q_act * (q_inv * DK**-0.5)).astype(BF)
        k = (k_act * k_inv).astype(BF)
        v = (v_mixed * v_sig).astype(BF)
        b, g, gr = beta[:, H + h : H + h + 1], running[:, h : h + 1], across[h : h + 1, :]
        hv = slice(h * DV, (h + 1) * DV)
        hk = slice(h * DK, (h + 1) * DK)
        U = split(u_ref[:, hv])
        T = split(t_ref[:, h * C : (h + 1) * C])
        S0 = s_ref[0, hk, :]
        Ss = split(S0)
        dO = split(do_ref[:, hv])
        qf, kf = q.astype(F32), k.astype(F32)
        D = jnp.exp(jnp.where(low, g - gr, -1e30))
        kk, qk = dot1(k, k, 1, 1), dot1(q, k, 1, 1)
        bD = b * D
        A, P = jnp.where(strict, kk * bD, 0.0), qk * D
        last = gr[:, C - 1 : C]
        gam, e, G = jnp.exp(g), jnp.exp(last - g), jnp.exp(last)
        dS1 = dS[hk, :]
        dSs = split(dS1)
        dU = mm(P, dO, 0, 0) + mm(kf * e, dSs)
        dR = mm(T, dU, 0, 0)
        dRs = split(dR)
        dS[hk, :] = G * dS1 + mm(qf * gam, dO, 0, 0) - mm(kf * (b * gam), dRs, 0, 0)
        dP = jnp.where(low, mm(dO, U, 1, 1), 0.0)
        dA = jnp.where(strict, -mm(dRs, U, 1, 1), 0.0)
        Rb = v.astype(F32) - gam * mm(k, Ss)
        db = jnp.sum(dR * Rb, axis=1, keepdims=True) + jnp.sum(dA * kk * D, axis=1, keepdims=True)
        dOS = gam * mm(dO, Ss, 1, 1)
        dRS = (b * gam) * mm(dRs, Ss, 1, 1)
        UdS = e * mm(U, dSs, 1, 1)
        M1, M2 = split(dP * D), split(dA * bD)
        dq = dOS + mm(M1, k)
        dk = UdS - dRS + mm(M1, q, 0, 0) + mm(M2, k) + mm(M2, k, 0, 0)
        X = dP * P + dA * A
        uk = jnp.sum(UdS * kf, axis=1, keepdims=True)
        total = jnp.sum(uk, axis=0, keepdims=True) + G * jnp.sum(
            jnp.sum(S0 * dS1, axis=1, keepdims=True), axis=0, keepdims=True
        )
        dg = (
            jnp.sum(dOS * qf - dRS * kf + X - jnp.transpose(X), axis=1, keepdims=True)
            - uk
            + jnp.where(last_row, total, 0.0)
        )
        d_running = jnp.where(lane == h, dg, d_running)
        d_beta = jnp.where(lane == H + h, db, d_beta)
        q_in = jnp.sum(dq * q_act, axis=1, keepdims=True) * (q_inv * q_inv)
        gradient_in(q_columns, q_mixed, q_sig, (q_inv * DK**-0.5) * (dq - q_act * q_in))
        k_in = jnp.sum(dk * k_act, axis=1, keepdims=True) * (k_inv * k_inv)
        gradient_in(k_columns, k_mixed, k_sig, k_inv * (dk - k_act * k_in))
        gradient_in(v_columns, v_mixed, v_sig, b * dR)
    for start in range(0, W, 512):
        columns = slice(start, start + 512)
        here = dext[0:C, columns]
        total = taps_ref[3:4, columns] * here
        dtaps_ref[3:4, columns] += jnp.sum(
            here * ext[HALO : HALO + C, columns], axis=0, keepdims=True
        )
        for tap in range(3):
            total = total + taps_ref[tap : tap + 1, columns] * dext[3 - tap : 3 - tap + C, columns]
            dtaps_ref[tap : tap + 1, columns] += jnp.sum(
                here * ext[HALO - 3 + tap : HALO - 3 + tap + C, columns], axis=0, keepdims=True
            )
        dp_ref[:, columns] = total.astype(BF)
    ones = jnp.where(i >= j, 1.0, 0.0).astype(BF)
    d_log = exact_sum(ones, d_running, 0)
    d_raised = d_log * par_ref[0:1, :] * jax.nn.sigmoid(raised)
    d_tail = d_raised + d_beta * beta * (1.0 - beta)
    dp_ref[:, W : W + 128] = d_tail.astype(BF)
    dpar_ref[0:1, :] += jnp.sum(d_log * log_decay, axis=0, keepdims=True)
    dpar_ref[1:2, :] += jnp.sum(d_raised, axis=0, keepdims=True)
    carry_ref[...] = dext[0:HALO, :]


def room(mebibytes):
    return pltpu.CompilerParams(vmem_limit_bytes=mebibytes * 2**20)


def row_block(rows, width, at=lambda s: s):
    return pl.BlockSpec((rows, width), lambda s: (at(s), 0))


def whole_block(array):
    return pl.BlockSpec(array.shape, lambda s: (0,) * array.ndim)


def mixer_fwd(projected, taps, par, heads, start, count, before=None, NC=2):
    L, wide = projected.shape
    H, C = heads, CHUNK
    W = taps.shape[1]
    DV = W // H - 2 * DK
    f = jax.ShapeDtypeStruct
    base = start // NC
    shapes = [f((L, H * DV), F32), f((L, H * DV), F32), f((L, H * C), F32), f((L // C, H * DK, DV), F32)]
    more, more_specs, aliases = [], [], {}
    if before is not None:
        more = [before[4]] + list(before[:4])
        more_specs = [whole_block(before[4])] + [pl.BlockSpec(memory_space=pl.ANY)] * 4
        aliases = {5 + n: n for n in range(4)}
    return pl.pallas_call(
        functools.partial(fwd_kernel, H, DV, NC, start),
        grid=(count // NC,),
        in_specs=[
            row_block(NC * C, wide, lambda s: base + s),
            row_block(HALO, wide, lambda s: jnp.maximum((base + s) * (NC * C // HALO) - 1, 0)),
            whole_block(taps),
            whole_block(par),
        ]
        + more_specs,
        out_specs=[
            row_block(NC * C, H * DV, lambda s: base + s),
            row_block(NC * C, H * DV, lambda s: base + s),
            row_block(NC * C, H * C, lambda s: base + s),
            pl.BlockSpec((NC, H * DK, DV), lambda s: (base + s, 0, 0)),
            pl.BlockSpec((H * DK, DV), lambda s: (0, 0)),
        ],
        out_shape=shapes + [f((H * DK, DV), F32)],
        scratch_shapes=[pltpu.VMEM((NC * C + HALO, W), F32)],
        input_output_aliases=aliases,
        compiler_params=room(22),
        cost_estimate=pl.CostEstimate(
            flops=3 * 10**9 * count, bytes_accessed=3 * 2**20 * count, transcendentals=0
        ),
        name="mixer_fwd",
    )(projected, projected, taps, par, *more)


def mixer_bwd(projected, taps, par, written, inverse, states, grad_heads, heads, end, count, before=None):
    L, wide = projected.shape
    H, C = heads, CHUNK
    W = taps.shape[1]
    DV = W // H - 2 * DK
    f = jax.ShapeDtypeStruct

    def back(s):
        return end - s

    more, more_specs, aliases = [], [], {}
    if before is not None:
        more = list(before)
        more_specs = [pl.BlockSpec(memory_space=pl.ANY)] + [whole_block(a) for a in before[1:]]
        aliases = {8: 0}
    state, halo = f((H * DK, DV), F32), f((HALO, W), F32)
    return pl.pallas_call(
        functools.partial(bwd_kernel, H, DV, end, before is None),
        grid=(count,),
        in_specs=[
            row_block(C, wide, back),
            row_block(HALO, wide, lambda s: jnp.maximum(back(s) * (C // HALO) - 1, 0)),
            whole_block(taps),
            whole_block(par),
            row_block(C, H * DV, back),
            row_block(C, H * C, back),
            pl.BlockSpec((1, H * DK, DV), lambda s: (back(s), 0, 0)),
            row_block(C, H * DV, back),
        ]
        + more_specs,
        out_specs=[
            row_block(C, wide, back),
            whole_block(taps),
            whole_block(par),
            whole_block(state),
            whole_block(halo),
        ],
        out_shape=[f((L, wide), BF), f(taps.shape, F32), f(par.shape, F32), state, halo],
        scratch_shapes=[pltpu.VMEM((C + HALO, W), F32), pltpu.VMEM((C + HALO, W), F32)],
        input_output_aliases=aliases,
        compiler_params=room(22),
        cost_estimate=pl.CostEstimate(
            flops=6 * 10**9 * count, bytes_accessed=4 * 2**20 * count, transcendentals=0
        ),
        name="mixer_bwd",
    )(projected, projected, taps, par, written, inverse, states, grad_heads, *more)


def gate_fwd_kernel(DV, o_ref, gate_ref, gain_ref, out_ref):
    for start in range(0, o_ref.shape[1], DV):
        cut = slice(start, start + DV)
        heads, gate = o_ref[:, cut], gate_ref[:, cut]
        inverse = lax.rsqrt(jnp.mean(heads * heads, axis=1, keepdims=True) + 1e-05)
        out_ref[:, cut] = (heads * inverse * gain_ref[...] * (gate * jax.nn.sigmoid(gate))).astype(BF)


def gate_fwd(heads_out, gate_proj, gain):
    L, width = heads_out.shape
    rows = L // 8
    return pl.pallas_call(
        functools.partial(gate_fwd_kernel, gain.shape[1]),
        grid=(8,),
        in_specs=[row_block(rows, width), row_block(rows, width), whole_block(gain)],
        out_specs=row_block(rows, width),
        out_shape=jax.ShapeDtypeStruct((L, width), BF),
        compiler_params=room(12),
        cost_estimate=pl.CostEstimate(flops=10**6, bytes_accessed=10**5, transcendentals=0),
        name="gate_fwd",
    )(heads_out, gate_proj, gain)


def gate_bwd_kernel(DV, o_ref, gate_ref, gain_ref, in_ref, do_ref, dgate_ref, dgain_ref):
    @pl.when(pl.program_id(0) == 0)
    def _():
        dgain_ref[...] = jnp.zeros_like(dgain_ref)

    for start in range(0, o_ref.shape[1], DV):
        cut = slice(start, start + DV)
        heads, gate, grad = o_ref[:, cut], gate_ref[:, cut], in_ref[:, cut]
        inverse = lax.rsqrt(jnp.mean(heads * heads, axis=1, keepdims=True) + 1e-05)
        normed = heads * inverse
        sig = jax.nn.sigmoid(gate)
        dgate_ref[:, cut] = (
            grad * (normed * gain_ref[...]) * (sig * (1.0 + gate * (1.0 - sig)))
        ).astype(BF)
        d_scaled = grad * (gate * sig)
        dgain_ref[...] += jnp.sum(d_scaled * normed, axis=0, keepdims=True)
        d_normed = d_scaled * gain_ref[...]
        do_ref[:, cut] = inverse * (
            d_normed - normed * jnp.mean(d_normed * normed, axis=1, keepdims=True)
        )


def gate_bwd(heads_out, gate_proj, gain, grad_mixer):
    L, width = heads_out.shape
    rows = L // 8
    f = jax.ShapeDtypeStruct
    return pl.pallas_call(
        functools.partial(gate_bwd_kernel, gain.shape[1]),
        grid=(8,),
        in_specs=[row_block(rows, width), row_block(rows, width), whole_block(gain), row_block(rows, width)],
        out_specs=[row_block(rows, width), row_block(rows, width), whole_block(gain)],
        out_shape=[f((L, width), F32), f((L, width), BF), f(gain.shape, F32)],
        compiler_params=room(14),
        cost_estimate=pl.CostEstimate(flops=10**6, bytes_accessed=10**5, transcendentals=0),
        name="gate_bwd",
    )(heads_out, gate_proj, gain, grad_mixer)


def at_place(place, n):
    return jnp.where(place < n // 2, 2 * place, 2 * (n - place) - 1)


def place_of(index, n):
    return jnp.where(index % 2 == 0, index // 2, n - (index + 1) // 2)


def ring_pairs(n):
    order = list(range(0, n, 2)) + list(range(n - 1, 0, -2))
    ahead = [(order[i], order[(i + 1) % n]) for i in range(n)]
    return ahead, [(d, s) for s, d in ahead]


def behind(d):
    n = lax.axis_size("dp")
    return at_place((place_of(lax.axis_index("dp"), n) - d + n) % n, n)


def after(values, token):
    return lax.optimization_barrier((values, token))[0]


class GatherRing:
    def __init__(self, shard):
        half = shard.shape[0] // 2
        self.first, self.second = [shard[:half]], [shard[half:]]
        self.n = lax.axis_size("dp")

    def send(self, token):
        ahead, back = ring_pairs(self.n)
        first, second = after((self.first[-1], self.second[-1]), token)
        self.first.append(lax.ppermute(first, "dp", ahead))
        self.second.append(lax.ppermute(second, "dp", back))

    def last(self):
        return self.first[-1], self.second[-1]

    def through(self):
        return len(self.first) == self.n

    def finish(self, widths, token=None):
        half = self.first[0].shape[0]
        if token is None:
            token = self.first[1 % self.n], self.second[1 % self.n]
        nothing = after(jnp.zeros((), BF), token)
        fulls = [jnp.broadcast_to(nothing, (self.n * 2 * half, width)) for width in widths]
        for hop in range(self.n):
            for piece, at in (
                (self.first[hop], behind(hop) * 2 * half),
                (self.second[hop], behind(self.n - hop) * 2 * half + half),
            ):
                fulls = [
                    lax.dynamic_update_slice(full, part, (at, 0))
                    for full, part in zip(fulls, columns(piece, widths))
                ]
        return fulls


def land_kernel(widths, at_ref, first, second, *refs):
    count = len(widths)
    for arrived, mine, out in (
        (first, refs[:count], refs[-2]),
        (second, refs[count : 2 * count], refs[-1]),
    ):
        start = 0
        for width, term in zip(widths, mine):
            cut = slice(start, start + width)
            out[:, cut] = (arrived[:, cut].astype(F32) + term[...].astype(F32)).astype(BF)
            start += width


def landed(flying, partials, places):
    widths = [partial.shape[1] for partial in partials]
    rows, wide = flying[0].shape
    steps = 2
    block = rows // steps
    sent = pl.BlockSpec((block, wide), lambda s, at: (s, 0))

    def term(width, side):
        return pl.BlockSpec(
            (block, width), lambda s, at: (at[side] * (2 * steps) + side * steps + s, 0)
        )

    terms = [term(width, side) for side in (0, 1) for width in widths]
    return pl.pallas_call(
        functools.partial(land_kernel, widths),
        grid_spec=pltpu.PrefetchScalarGridSpec(
            num_scalar_prefetch=1, grid=(steps,), in_specs=[sent, sent] + terms, out_specs=[sent, sent]
        ),
        out_shape=[jax.ShapeDtypeStruct((rows, wide), BF)] * 2,
        compiler_params=room(10),
        cost_estimate=pl.CostEstimate(flops=10**6, bytes_accessed=10**6, transcendentals=0),
        name="land",
    )(jnp.stack(places).astype(jnp.int32), *flying, *partials, *partials)


class ScatterRing:
    def __init__(self, pairs, token, partials=None):
        self.n = lax.axis_size("dp")
        self.hop = 0
        self.pairs, self.partials = pairs, partials
        self.sums = tuple(
            jnp.concatenate(self.terms_of(place, side, token), axis=1).astype(BF)
            for place, side in ((1, 0), (self.n - 1, 1))
        )

    def terms_of(self, place, side, token):
        terms = []
        for number, (features, grads) in enumerate(self.pairs):
            half = features.shape[1] // self.n // 2
            at = behind(place % self.n) * (2 * half) + side * half
            if self.partials is not None:
                terms.append(lax.dynamic_slice_in_dim(self.partials[number], at, half, 0))
                continue
            left = lax.dynamic_slice_in_dim(features, at, half, 1)
            terms.append(contract_rows(*after((left, grads), token)))
        return terms

    def prepare(self, token):
        self.partials = [
            contract_rows(*after((features, grads), token)).astype(BF)
            for features, grads in self.pairs
        ]
        return self.partials

    def send(self, token):
        ahead, back = ring_pairs(self.n)
        first, second = after(self.sums, token)
        self.flying = lax.ppermute(first, "dp", ahead), lax.ppermute(second, "dp", back)

    def land(self, token):
        self.hop += 1
        flying = after(self.flying, token)
        if self.hop < self.n - 1:
            places = behind((self.hop + 1) % self.n), behind((self.n - 1 - self.hop) % self.n)
            self.sums = tuple(landed(flying, self.partials, places))
            return self.sums
        self.sums = tuple(
            [
                x.astype(F32) + y.astype(F32)
                for x, y in zip(
                    columns(arrived, [part.shape[1] for part in self.partials]),
                    self.terms_of(0, side, ()),
                )
            ]
            for side, arrived in enumerate(flying)
        )
        return self.sums

    def done(self):
        return self.hop == self.n - 1

    def results(self):
        return [jnp.concatenate(halves, axis=0) for halves in zip(*self.sums)]


def slot(token, rings, pieces=(), gathers=()):
    rings = [ring for ring in rings if not ring.done()]
    gathers = [ring for ring in gathers if not ring.through()]
    for ring in rings:
        ring.send(token)
    for ring in gathers:
        ring.send(token)
    for piece in pieces:
        token = piece(token)
    token = [ring.land(token) for ring in rings] or token
    if gathers:
        token = token, [ring.last() for ring in gathers]
    return token


def run_out(token, rings, pieces=(), gathers=()):
    pieces = list(pieces)
    while (
        pieces
        or any(not ring.done() for ring in rings)
        or any(not ring.through() for ring in gathers)
    ):
        token = slot(token, rings, [pieces.pop(0)] if pieces else (), gathers)
    return token


def contract_rows(left, right):
    return lax.dot_general(
        left, right, (((0,), (0,)), ((), ())), preferred_element_type=jnp.float32
    )


def times_transposed(left, right):
    return lax.dot_general(
        left, right, (((1,), (1,)), ((), ())), preferred_element_type=jnp.float32
    )


CORES = [(0, 1), (1, 0), (2, 3), (3, 2)]
PAIRS = [(0, 2), (2, 0), (1, 3), (3, 1)]


class Spread:
    def __init__(self, block):
        self.block = block
        self.plain = lax.axis_size("tensor") != 4
        if not self.plain:
            self.far = lax.ppermute(block, "tensor", PAIRS)
            self.near = lax.ppermute(block, "tensor", CORES)

    def turn(self, token):
        if self.plain:
            return token
        far = after(self.far, token)
        self.far_near = lax.ppermute(far, "tensor", CORES)
        return far

    def rows(self, token=()):
        if self.plain:
            return lax.all_gather(after(self.block, token), "tensor", axis=0, tiled=True)
        rank = lax.axis_index("tensor")
        rows, width = self.block.shape
        out = jnp.zeros((4 * rows, width), self.block.dtype)
        parts = after((self.block, self.near, self.far, self.far_near), token)
        for flip, part in enumerate(parts):
            out = lax.dynamic_update_slice_in_dim(out, part, (rank ^ flip) * rows, 0)
        return out


def spread_rows(block):
    spread = Spread(block)
    spread.turn(())
    return spread.rows()


class RowSum:
    def __init__(self, product, rows):
        self.product, self.rows = product, rows
        self.rank = lax.axis_index("tensor")
        self.plain = lax.axis_size("tensor") != 4

    def term(self, flip, token):
        return self.product((self.rank ^ flip) * self.rows, token)

    def far(self, token):
        if self.plain:
            whole = [self.product(i * self.rows, token) for i in range(lax.axis_size("tensor"))]
            self.total = lax.psum_scatter(
                jnp.concatenate(whole, axis=0), "tensor", scatter_dimension=0, tiled=True
            )
            return self.total
        self.sent = self.term(3, token).astype(BF)
        self.far_near = lax.ppermute(self.sent, "tensor", CORES)
        return self.sent

    def far_sum(self, token):
        if self.plain:
            return token
        total = (self.term(2, token) + self.far_near.astype(F32)).astype(BF)
        self.from_far = lax.ppermute(total, "tensor", PAIRS)
        return total

    def near(self, token):
        if self.plain:
            return token
        sent = self.term(1, token).astype(BF)
        self.from_near = lax.ppermute(sent, "tensor", CORES)
        return sent

    def own(self, token):
        if self.plain:
            return token
        self.mine = self.term(0, token)
        return self.mine

    def result(self, token):
        if self.plain:
            return after(self.total, token)
        mine = after(self.mine, token)
        return mine + self.from_near.astype(F32) + self.from_far.astype(F32)

    def pieces(self):
        return [self.far, self.far_sum, self.near, self.own]


def summed_rows(pairs, rows):
    def product(start, token):
        total = None
        for grads, weight in pairs:
            part, other = after((lax.dynamic_slice_in_dim(grads, start, rows, 0), weight), token)
            part = times_transposed(part, other)
            total = part if total is None else total + part
        return total

    return RowSum(product, rows)


def sum_over(values, axis):
    n = lax.axis_size(axis)
    if n & (n - 1):
        return lax.psum(values, axis)
    step = 1
    while step < n:
        values = values + lax.ppermute(values, axis, [(i, i ^ step) for i in range(n)])
        step *= 2
    return values


def packed(arrays):
    flat = jnp.concatenate([a.reshape(-1) for a in arrays])
    pad = -flat.shape[0] % 1024
    return jnp.pad(flat, (0, pad)).reshape(-1, 128)


def unpacked(values, shapes):
    flat = values.reshape(-1)
    out, start = [], 0
    for shape in shapes:
        size = 1
        for extent in shape:
            size *= extent
        out.append(flat[start : start + size].reshape(shape))
        start += size
    return out


def norm_back(values, inverse, gain, incoming):
    scaled = incoming * gain
    width = values.shape[1]
    grad_values = (
        inverse * scaled
        - values
        * inverse
        * inverse
        * inverse
        * jnp.sum(scaled * values, axis=1, keepdims=True)
        / width
    )
    grad_gain = jnp.sum(incoming * values * inverse, axis=0)
    return (grad_values, grad_gain)


def place_slice(local, whole, rank, axis):
    return lax.dynamic_update_slice_in_dim(
        jnp.zeros_like(whole), local, rank * local.shape[axis], axis
    )


def columns(array, widths):
    out, start = [], 0
    for width in widths:
        out.append(array[:, start : start + width])
        start += width
    return out


def shards(
    inputs,
    lengths,
    cotangent,
    norm_attn,
    norm_ffn,
    norm_heads,
    w_query,
    w_key,
    w_value,
    w_out_gate,
    w_decay,
    w_beta,
    w_output,
    conv_query,
    conv_key,
    conv_value,
    decay_log,
    decay_bias,
    w_ffn_gate,
    w_ffn_up,
    w_ffn_down,
):
    rows = inputs.shape[0]
    width = inputs.shape[1]
    tensor_rank = lax.axis_index("tensor")
    positions = tensor_rank * rows + jnp.arange(rows, dtype=jnp.int32)
    valid = (positions < lengths[0]).astype(jnp.float32)[:, None]
    heads_here = w_decay.shape[1]
    widths = [w.shape[1] for w in (w_query, w_key, w_value, w_decay, w_beta)]
    fill = -sum(widths) % 128
    mixed_shard = jnp.pad(
        jnp.concatenate((w_query, w_key, w_value, w_decay, w_beta), axis=1), ((0, 0), (0, fill))
    )
    ffn_width = w_ffn_gate.shape[1]
    kept = {}
    mixed_ring = GatherRing(mixed_shard)
    mixed_ring.send(())
    inputs, cotangent = after((inputs, cotangent), mixed_ring.last())
    token = run_out(mixed_ring.last(), (), (), (mixed_ring,))

    def arrived(hop):
        at = min(hop, mixed_ring.n - 1)
        return mixed_ring.first[at], mixed_ring.second[at]

    gate_shards = after((w_out_gate, w_output), arrived(3))
    gate_ring = GatherRing(jnp.concatenate((gate_shards[0], gate_shards[1].T), axis=1))
    [mixed_full] = mixed_ring.finish([mixed_shard.shape[1]])

    gain_attn = norm_attn
    gain_ffn = norm_ffn
    stream_in = inputs.astype(jnp.float32)
    grad_out = valid * cotangent.astype(jnp.float32)
    inverse_in = lax.rsqrt(jnp.mean(stream_in * stream_in, axis=1, keepdims=True) + 1e-06)
    full_in = spread_rows((stream_in * inverse_in * gain_attn).astype(jnp.bfloat16))

    def here(array):
        size = array.shape[-1] // lax.axis_size("tensor")
        return lax.dynamic_slice_in_dim(array, tensor_rank * size, size, array.ndim - 1)

    taps = jnp.concatenate((here(conv_query), here(conv_key), here(conv_value)), axis=1)
    par = jnp.pad(
        jnp.stack((-jnp.exp(here(decay_log)), here(decay_bias))), ((0, 6), (0, 128 - heads_here))
    )
    gain_heads = norm_heads[None, :]
    chunks = full_in.shape[0] // CHUNK
    parts = 4

    def project(token):
        kept["projected"] = jnp.dot(
            *after((full_in, mixed_full), token), preferred_element_type=jnp.float32
        )
        kept["forward"] = None
        return kept["projected"]

    def forward_part(start):
        def piece(token):
            kept["forward"] = mixer_fwd(
                after(kept["projected"], token),
                taps,
                par,
                heads_here,
                start,
                chunks // parts,
                kept["forward"],
            )
            return kept["forward"][4]

        return piece

    token = run_out(
        token,
        (),
        [project] + [forward_part(i * (chunks // parts)) for i in range(parts)],
        (gate_ring,),
    )
    projected = kept["projected"]
    heads_out, written, inverse, states, _ = kept["forward"]
    ffn_shards = after((w_ffn_gate, w_ffn_up, w_ffn_down), arrived(4))
    ffn_ring = GatherRing(
        jnp.concatenate((ffn_shards[0], ffn_shards[1], ffn_shards[2].T), axis=1)
    )
    gate_full, output_full = gate_ring.finish(
        [w_out_gate.shape[1], w_output.shape[0]], arrived(5)
    )

    def gate(token):
        kept["gate"] = jnp.dot(
            *after((full_in, gate_full), token), preferred_element_type=jnp.float32
        )
        kept["mixer"] = gate_fwd(heads_out, kept["gate"], gain_heads)
        return kept["mixer"]

    def attend(token):
        kept["attn"] = summed_rows(((kept["mixer"], output_full),), rows)
        return kept["attn"].far_sum(kept["attn"].far(token))

    def attend_own(token):
        return kept["attn"].own(kept["attn"].near(token))

    def middle(token):
        kept["branch"] = kept["attn"].result(token)
        stream = stream_in + kept["branch"]
        kept["stream"] = stream
        kept["inverse"] = lax.rsqrt(jnp.mean(stream * stream, axis=1, keepdims=True) + 1e-06)
        normed = (stream * kept["inverse"] * gain_ffn).astype(jnp.bfloat16)
        kept["full_mid"] = spread_rows(normed)
        return normed

    token = run_out(token, (), [gate, attend, attend_own, middle], (ffn_ring,))
    gate_proj, mixer, branch_attn = kept["gate"], kept["mixer"], kept["branch"]
    stream, inverse_mid, full_mid = kept["stream"], kept["inverse"], kept["full_mid"]
    ffn_gate_full, ffn_up_full, down_full = ffn_ring.finish(
        [ffn_width, ffn_width, w_ffn_down.shape[0]]
    )
    grad_ffn = spread_rows(after(grad_out.astype(jnp.bfloat16), full_mid))

    token, full_mid_in = after((token, full_mid), ffn_ring.last())
    ffn_gate = jnp.dot(full_mid_in, ffn_gate_full, preferred_element_type=jnp.float32)
    ffn_up = jnp.dot(full_mid_in, ffn_up_full, preferred_element_type=jnp.float32)
    sigma = jax.nn.sigmoid(ffn_gate)
    silu_gate = ffn_gate * sigma
    hidden = (silu_gate * ffn_up).astype(jnp.bfloat16)
    grad_hidden = jnp.dot(grad_ffn, down_full, preferred_element_type=jnp.float32)
    grad_gate_in = grad_hidden * ffn_up * sigma * (1.0 + ffn_gate * (1.0 - sigma))
    grad_gate_in = grad_gate_in.astype(jnp.bfloat16)
    grad_up_in = (grad_hidden * silu_gate).astype(jnp.bfloat16)
    token = grad_gate_in, grad_up_in, hidden
    ffn_scatter = ScatterRing(
        ((full_mid, grad_gate_in), (full_mid, grad_up_in), (grad_ffn, hidden)), token
    )
    token = ffn_scatter.sums
    mid_sum = summed_rows(((grad_gate_in, ffn_gate_full), (grad_up_in, ffn_up_full)), rows)

    def mid_own(token):
        return mid_sum.own(mid_sum.near(token))

    def middle_back(token):
        through, kept["norm_ffn"] = norm_back(stream, inverse_mid, gain_ffn, mid_sum.result(token))
        kept["grad_stream"] = grad_out + through
        low = kept["grad_stream"].astype(jnp.bfloat16)
        kept["spread"] = Spread(low)
        return low

    def turn(token):
        token = ffn_sum.far_sum(ffn_sum.far(kept["spread"].turn(token)))
        kept["grad_attn"] = kept["spread"].rows(token)
        return kept["grad_attn"]

    def attend_back(token):
        grad_mixer = jnp.dot(
            *after((kept["grad_attn"], output_full), token), preferred_element_type=jnp.float32
        )
        kept["gate_back"] = gate_bwd(heads_out, gate_proj, gain_heads, grad_mixer)
        kept["backward"] = None
        return kept["gate_back"][0]

    def backward_part(end):
        def piece(token):
            kept["backward"] = mixer_bwd(
                projected,
                taps,
                par,
                written,
                inverse,
                states,
                after(kept["gate_back"][0], token),
                heads_here,
                end,
                chunks // parts,
                kept["backward"],
            )
            return kept["backward"][3]

        return piece

    ffn_sum = summed_rows(((hidden, down_full),), rows)
    backward = [backward_part(chunks - 1 - i * (chunks // parts)) for i in range(parts)]
    token = run_out(
        token,
        (ffn_scatter,),
        [
            ffn_scatter.prepare,
            lambda t: mid_sum.far_sum(mid_sum.far(t)),
            mid_own,
            middle_back,
            turn,
            attend_back,
        ]
        + backward[:1],
    )
    grad_stream, grad_norm_ffn, grad_attn = kept["grad_stream"], kept["norm_ffn"], kept["grad_attn"]
    _, grad_gate_proj, heads_gain_grad = kept["gate_back"]
    gate_scatter = ScatterRing(
        ((full_in, grad_gate_proj), (grad_attn, mixer)), token
    )
    token = token, gate_scatter.sums

    def in_far(token):
        kept["in_sum"] = summed_rows(
            ((grad_gate_proj, gate_full), (kept["backward"][0], mixed_full)), rows
        )
        return kept["in_sum"].far(token)

    def leave(token):
        kept["branch_ffn"] = ffn_sum.result(token)
        kept["outputs"] = (valid * (stream + kept["branch_ffn"])).astype(jnp.bfloat16)
        return kept["outputs"]

    def in_far_sum(token):
        return kept["in_sum"].far_sum(token)

    def in_near(token):
        return kept["in_sum"].near(token)

    def in_own(token):
        return kept["in_sum"].own(token)

    def last_back(token):
        through, kept["norm_attn"] = norm_back(
            stream_in, inverse_in, gain_attn, kept["in_sum"].result(token)
        )
        kept["grad_inputs"] = grad_stream + through
        return kept["grad_inputs"]

    token = run_out(
        token,
        (gate_scatter,),
        [gate_scatter.prepare]
        + backward[1:]
        + [in_far, in_far_sum, lambda t: in_near(ffn_sum.near(t))],
    )
    grad_projected, grad_taps, grad_par, _, _ = kept["backward"]
    mixed_scatter = ScatterRing(((full_in, grad_projected),), token)
    token = token, mixed_scatter.sums
    token = slot(token, (mixed_scatter,), [ffn_sum.own, mixed_scatter.prepare])
    token = slot(token, (mixed_scatter,), [leave, in_own])
    branch_ffn, outputs = kept["branch_ffn"], kept["outputs"]
    stat_sums = jnp.stack(
        [
            jnp.sum(valid * stream_in * stream_in),
            jnp.sum(valid * branch_attn * branch_attn),
            jnp.sum(valid * branch_ffn * branch_ffn),
            jnp.sum(valid),
        ]
    )
    local = columns(grad_taps, widths[:3]) + [grad_par[0, :heads_here], grad_par[1, :heads_here]]
    whole = [conv_query, conv_key, conv_value, decay_log, decay_bias]
    common = [stat_sums, grad_norm_ffn, heads_gain_grad[0], norm_attn]
    def common_over_dp(token):
        parts = common[:3] + [kept["norm_attn"]] + local
        kept["common"] = sum_over(after(packed(parts), token), "dp")
        return kept["common"]

    def common_over_tensor(token):
        sums = unpacked(kept["common"], [a.shape for a in common + local])
        spread = [
            place_slice(part, array, tensor_rank, part.ndim - 1)
            for part, array in zip(sums[4:], whole)
        ]
        kept["common"] = sum_over(after(packed(sums[:4] + spread), token), "tensor")
        return kept["common"]

    token = run_out(
        token,
        (mixed_scatter,),
        [last_back, common_over_dp, common_over_tensor],
    )
    grad_inputs = kept["grad_inputs"]
    owned_gate, owned_up, owned_down = ffn_scatter.results()
    owned_out_gate, owned_output = gate_scatter.results()
    owned_query, owned_key, owned_value, owned_decay, owned_beta = columns(
        mixed_scatter.results()[0], widths
    )
    (
        stat_sums,
        total_ffn_gain,
        total_heads_gain,
        total_attn_gain,
        total_conv_query,
        total_conv_key,
        total_conv_value,
        total_decay_log,
        total_decay_bias,
    ) = unpacked(kept["common"], [a.shape for a in common + whole])
    statistics = jnp.sqrt(stat_sums[:3] / (stat_sums[3] * width))
    return (
        outputs,
        statistics,
        grad_inputs,
        total_attn_gain,
        total_ffn_gain,
        total_heads_gain,
        owned_query,
        owned_key,
        owned_value,
        owned_out_gate,
        owned_decay,
        owned_beta,
        owned_output.T,
        total_conv_query,
        total_conv_key,
        total_conv_value,
        total_decay_log,
        total_decay_bias,
        owned_gate,
        owned_up,
        owned_down.T,
    )


def solution(mesh):
    in_specs = (
        P(("dp", "tensor"), None),
        P("dp"),
        P(("dp", "tensor"), None),
        P(),
        P(),
        P(),
        P("dp", "tensor"),
        P("dp", "tensor"),
        P("dp", "tensor"),
        P("dp", "tensor"),
        P("dp", "tensor"),
        P("dp", "tensor"),
        P("tensor", "dp"),
        P(),
        P(),
        P(),
        P(),
        P(),
        P("dp", "tensor"),
        P("dp", "tensor"),
        P("tensor", "dp"),
    )
    out_specs = (
        P(("dp", "tensor"), None),
        P(),
        P(("dp", "tensor"), None),
        P(),
        P(),
        P(),
        P("dp", "tensor"),
        P("dp", "tensor"),
        P("dp", "tensor"),
        P("dp", "tensor"),
        P("dp", "tensor"),
        P("dp", "tensor"),
        P("tensor", "dp"),
        P(),
        P(),
        P(),
        P(),
        P(),
        P("dp", "tensor"),
        P("dp", "tensor"),
        P("tensor", "dp"),
    )
    return jax.shard_map(shards, mesh=mesh, in_specs=in_specs, out_specs=out_specs, check_vma=False)
```

```python
import functools

import jax
import jax.numpy as jnp
from jax import lax
from jax.experimental import pallas as pl
from jax.experimental.pallas import tpu as pltpu
from jax.sharding import PartitionSpec as P

BF=jnp.bfloat16; F32=jnp.float32
DK = 128
CHUNK = 128
HALO = 8


def dot1(a, b, ca=1, cb=0):
    return lax.dot_general(a, b, (((ca,), (cb,)), ((), ())), preferred_element_type=F32)


def split(a):
    if a.dtype == BF:
        return a, None
    high = a.astype(BF)
    return high, (a - high.astype(F32)).astype(BF)


def mm(a, b, ca=1, cb=0):
    a_high, a_low = a if isinstance(a, tuple) else split(a)
    b_high, b_low = b if isinstance(b, tuple) else split(b)
    total = dot1(a_high, b_high, ca, cb)
    if b_low is not None:
        total = total + dot1(a_high, b_low, ca, cb)
    if a_low is not None:
        total = total + dot1(a_low, b_high, ca, cb)
    return total


def exact_sum(ones, values, ca):
    high, rest = split(values)
    middle, low = split(values - high.astype(F32))
    return dot1(ones, high, ca) + (dot1(ones, middle, ca) + dot1(ones, low, ca))


def grids(size):
    return (
        lax.broadcasted_iota(jnp.int32, (size, size), 0),
        lax.broadcasted_iota(jnp.int32, (size, size), 1),
    )


def inverses(couplings):
    size = couplings[0].shape[0]
    i, j = grids(size)
    eye = jnp.where(i == j, 1.0, 0.0).astype(F32)

    def same(bits):
        return lax.shift_right_logical(i, bits) == lax.shift_right_logical(j, bits)

    inside = same(3)
    near = [jnp.where(inside, a, 0.0) for a in couplings]
    second = [split(mm(a, a)) for a in map(split, near)]
    fourth = [mm(a, a) for a in second]
    found = [eye - a for a in near]
    found = [x + mm(x, a) for x, a in zip(found, second)]
    found = [x + mm(x, a) for x, a in zip(found, fourth)]
    bits = 3
    while (1 << bits) < size:
        across = jnp.logical_and(same(bits + 1), jnp.logical_not(same(bits)))
        parts = [split(x) for x in found]
        moved = [mm(jnp.where(across, a, 0.0), x) for a, x in zip(couplings, parts)]
        found = [x - mm(p, y) for x, p, y in zip(found, parts, moved)]
        bits += 1
    return found


def conv_of(taps_ref, ext, columns, rows, start=HALO - 3):
    total = taps_ref[0:1, columns] * ext[start : start + rows, columns]
    for tap in range(1, 4):
        total = total + taps_ref[tap : tap + 1, columns] * ext[
            start + tap : start + tap + rows, columns
        ]
    return total


def decay_of(tail, par_ref):
    i, j = grids(CHUNK)
    ones = jnp.where(i >= j, 1.0, 0.0).astype(BF)
    raised = tail + par_ref[1:2, :]
    log_decay = par_ref[0:1, :] * (
        jnp.maximum(raised, 0.0) + jnp.log1p(jnp.exp(-jnp.abs(raised)))
    )
    return exact_sum(ones, log_decay, 1), log_decay, jax.nn.sigmoid(tail), raised


def fwd_kernel(H, DV, NC, start, p_ref, halo_ref, taps_ref, par_ref, *refs):
    C = CHUNK
    R = NC * C
    W = H * (2 * DK + DV)
    o_ref, u_ref, t_ref, s_ref, S, ext = refs[-6:]
    step = pl.program_id(0)

    if start == 0:

        @pl.when(step == 0)
        def _():
            S[...] = jnp.zeros_like(S)
            ext[0:HALO, :] = jnp.zeros((HALO, W), F32)

        @pl.when(step > 0)
        def _():
            ext[0:HALO, :] = halo_ref[:, 0:W]

    else:

        @pl.when(step == 0)
        def _():
            S[...] = refs[0][...]

        ext[0:HALO, :] = halo_ref[:, 0:W]

    ext[HALO : HALO + R, :] = p_ref[:, 0:W]
    i, j = grids(C)
    low, strict = i >= j, i > j
    idx = [(c, h) for c in range(NC) for h in range(H)]
    rows = [slice(c * C, (c + 1) * C) for c in range(NC)]
    q, k, v, b, g, gr = {}, {}, {}, {}, {}, {}
    for h in range(H):
        for part, out, base, size, factor in (
            (0, q, h * DK, DK, DK**-0.5),
            (1, k, H * DK + h * DK, DK, 1.0),
            (2, v, 2 * H * DK + h * DV, DV, None),
        ):
            mixed = conv_of(taps_ref, ext, slice(base, base + size), R)
            mixed = mixed * jax.nn.sigmoid(mixed)
            if factor is not None:
                mixed = mixed * (
                    lax.rsqrt(jnp.sum(mixed * mixed, axis=1, keepdims=True) + 1e-06) * factor
                )
            mixed = mixed.astype(BF)
            for c in range(NC):
                out[c, h] = mixed[rows[c], :]
    for c in range(NC):
        running, _, beta, _ = decay_of(p_ref[rows[c], W : W + 128], par_ref)
        across = jnp.transpose(running)
        for h in range(H):
            b[c, h] = beta[:, H + h : H + h + 1]
            g[c, h] = running[:, h : h + 1]
            gr[c, h] = across[h : h + 1, :]
    D = {x: jnp.exp(jnp.where(low, g[x] - gr[x], -1e30)) for x in idx}
    A = [jnp.where(strict, dot1(k[x], k[x], 1, 1) * b[x] * D[x], 0.0) for x in idx]
    T = dict(zip(idx, inverses(A)))
    P = {x: dot1(q[x], k[x], 1, 1) * D[x] for x in idx}
    gam = {x: jnp.exp(g[x]) for x in idx}
    Ts = {x: split(T[x]) for x in idx}
    TV = {x: mm(Ts[x], b[x] * v[x].astype(F32)) for x in idx}
    TK = {x: mm(Ts[x], b[x] * gam[x] * k[x].astype(F32)) for x in idx}
    for c in range(NC):
        for h in range(H):
            x = (c, h)
            t_ref[rows[c], h * C : (h + 1) * C] = T[x]
            S0 = S[h * DK : (h + 1) * DK, :]
            s_ref[c, h * DK : (h + 1) * DK, :] = S0
            Ss = split(S0)
            U = TV[x] - mm(TK[x], Ss)
            Us = split(U)
            u_ref[rows[c], h * DV : (h + 1) * DV] = U
            o_ref[rows[c], h * DV : (h + 1) * DV] = gam[x] * mm(q[x], Ss) + mm(P[x], Us)
            last = gr[x][:, C - 1 : C]
            S[h * DK : (h + 1) * DK, :] = jnp.exp(last) * S0 + mm(
                k[x].astype(F32) * jnp.exp(last - g[x]), Us, 0, 0
            )


def bwd_kernel(
    H, DV, end, first, p_ref, halo_ref, taps_ref, par_ref, u_ref, t_ref, s_ref, do_ref, *refs
):
    C = CHUNK
    W = H * (2 * DK + DV)
    dp_ref, dtaps_ref, dpar_ref, dS, carry_ref, ext, dext = refs[-7:]
    step = pl.program_id(0)

    @pl.when(step == 0)
    def _():
        if first:
            dS[...] = jnp.zeros_like(dS)
            dext[C : C + HALO, :] = jnp.zeros((HALO, W), F32)
            dtaps_ref[...] = jnp.zeros_like(dtaps_ref)
            dpar_ref[...] = jnp.zeros_like(dpar_ref)
        else:
            dS[...] = refs[3][...]
            dext[C : C + HALO, :] = refs[4][...]
            dtaps_ref[...] = refs[1][...]
            dpar_ref[...] = refs[2][...]

    @pl.when(step > 0)
    def _():
        dext[C : C + HALO, :] = dext[0:HALO, :]

    @pl.when(step == end)
    def _():
        ext[0:HALO, :] = jnp.zeros((HALO, W), F32)

    @pl.when(step < end)
    def _():
        ext[0:HALO, :] = halo_ref[:, 0:W]

    ext[HALO : HALO + C, :] = p_ref[:, 0:W]
    i, j = grids(C)
    low, strict = i >= j, i > j
    lane = lax.broadcasted_iota(jnp.int32, (C, 128), 1)
    last_row = lax.broadcasted_iota(jnp.int32, (C, 1), 0) == C - 1
    tail = p_ref[:, W : W + 128]
    running, log_decay, beta, raised = decay_of(tail, par_ref)
    across = jnp.transpose(running)
    d_running = jnp.zeros((C, 128), F32)
    d_beta = jnp.zeros((C, 128), F32)

    def gradient_in(columns, mixed, sig, d_act):
        dext[0:C, columns] = d_act * sig * (1.0 + mixed * (1.0 - sig))

    for h in range(H):
        q_columns = slice(h * DK, (h + 1) * DK)
        k_columns = slice(H * DK + h * DK, H * DK + (h + 1) * DK)
        v_columns = slice(2 * H * DK + h * DV, 2 * H * DK + (h + 1) * DV)
        q_mixed = conv_of(taps_ref, ext, q_columns, C)
        k_mixed = conv_of(taps_ref, ext, k_columns, C)
        v_mixed = conv_of(taps_ref, ext, v_columns, C)
        q_sig, k_sig, v_sig = (jax.nn.sigmoid(x) for x in (q_mixed, k_mixed, v_mixed))
        q_act, k_act = q_mixed * q_sig, k_mixed * k_sig
        q_inv = lax.rsqrt(jnp.sum(q_act * q_act, axis=1, keepdims=True) + 1e-06)
        k_inv = lax.rsqrt(jnp.sum(k_act * k_act, axis=1, keepdims=True) + 1e-06)
        q = (q_act * (q_inv * DK**-0.5)).astype(BF)
        k = (k_act * k_inv).astype(BF)
        v = (v_mixed * v_sig).astype(BF)
        b, g, gr = beta[:, H + h : H + h + 1], running[:, h : h + 1], across[h : h + 1, :]
        hv = slice(h * DV, (h + 1) * DV)
        hk = slice(h * DK, (h + 1) * DK)
        U = split(u_ref[:, hv])
        T = split(t_ref[:, h * C : (h + 1) * C])
        S0 = s_ref[0, hk, :]
        Ss = split(S0)
        dO = split(do_ref[:, hv])
        qf, kf = q.astype(F32), k.astype(F32)
        D = jnp.exp(jnp.where(low, g - gr, -1e30))
        kk, qk = dot1(k, k, 1, 1), dot1(q, k, 1, 1)
        bD = b * D
        A, P = jnp.where(strict, kk * bD, 0.0), qk * D
        last = gr[:, C - 1 : C]
        gam, e, G = jnp.exp(g), jnp.exp(last - g), jnp.exp(last)
        dS1 = dS[hk, :]
        dSs = split(dS1)
        dU = mm(P, dO, 0, 0) + mm(kf * e, dSs)
        dR = mm(T, dU, 0, 0)
        dRs = split(dR)
        dS[hk, :] = G * dS1 + mm(qf * gam, dO, 0, 0) - mm(kf * (b * gam), dRs, 0, 0)
        dP = jnp.where(low, mm(dO, U, 1, 1), 0.0)
        dA = jnp.where(strict, -mm(dRs, U, 1, 1), 0.0)
        Rb = v.astype(F32) - gam * mm(k, Ss)
        db = jnp.sum(dR * Rb, axis=1, keepdims=True) + jnp.sum(dA * kk * D, axis=1, keepdims=True)
        dOS = gam * mm(dO, Ss, 1, 1)
        dRS = (b * gam) * mm(dRs, Ss, 1, 1)
        UdS = e * mm(U, dSs, 1, 1)
        M1, M2 = split(dP * D), split(dA * bD)
        dq = dOS + mm(M1, k)
        dk = UdS - dRS + mm(M1, q, 0, 0) + mm(M2, k) + mm(M2, k, 0, 0)
        X = dP * P + dA * A
        uk = jnp.sum(UdS * kf, axis=1, keepdims=True)
        total = jnp.sum(uk, axis=0, keepdims=True) + G * jnp.sum(
            jnp.sum(S0 * dS1, axis=1, keepdims=True), axis=0, keepdims=True
        )
        dg = (
            jnp.sum(dOS * qf - dRS * kf + X - jnp.transpose(X), axis=1, keepdims=True)
            - uk
            + jnp.where(last_row, total, 0.0)
        )
        d_running = jnp.where(lane == h, dg, d_running)
        d_beta = jnp.where(lane == H + h, db, d_beta)
        q_in = jnp.sum(dq * q_act, axis=1, keepdims=True) * (q_inv * q_inv)
        gradient_in(q_columns, q_mixed, q_sig, (q_inv * DK**-0.5) * (dq - q_act * q_in))
        k_in = jnp.sum(dk * k_act, axis=1, keepdims=True) * (k_inv * k_inv)
        gradient_in(k_columns, k_mixed, k_sig, k_inv * (dk - k_act * k_in))
        gradient_in(v_columns, v_mixed, v_sig, b * dR)
    for start in range(0, W, 512):
        columns = slice(start, start + 512)
        here = dext[0:C, columns]
        total = taps_ref[3:4, columns] * here
        dtaps_ref[3:4, columns] += jnp.sum(
            here * ext[HALO : HALO + C, columns], axis=0, keepdims=True
        )
        for tap in range(3):
            total = total + taps_ref[tap : tap + 1, columns] * dext[3 - tap : 3 - tap + C, columns]
            dtaps_ref[tap : tap + 1, columns] += jnp.sum(
                here * ext[HALO - 3 + tap : HALO - 3 + tap + C, columns], axis=0, keepdims=True
            )
        dp_ref[:, columns] = total.astype(BF)
    ones = jnp.where(i >= j, 1.0, 0.0).astype(BF)
    d_log = exact_sum(ones, d_running, 0)
    d_raised = d_log * par_ref[0:1, :] * jax.nn.sigmoid(raised)
    d_tail = d_raised + d_beta * beta * (1.0 - beta)
    dp_ref[:, W : W + 128] = d_tail.astype(BF)
    dpar_ref[0:1, :] += jnp.sum(d_log * log_decay, axis=0, keepdims=True)
    dpar_ref[1:2, :] += jnp.sum(d_raised, axis=0, keepdims=True)
    carry_ref[...] = dext[0:HALO, :]


def room(mebibytes):
    return pltpu.CompilerParams(vmem_limit_bytes=mebibytes * 2**20)


def row_block(rows, width, at=lambda s: s):
    return pl.BlockSpec((rows, width), lambda s: (at(s), 0))


def whole_block(array):
    return pl.BlockSpec(array.shape, lambda s: (0,) * array.ndim)


def mixer_fwd(projected, taps, par, heads, start, count, before=None, NC=2):
    L, wide = projected.shape
    H, C = heads, CHUNK
    W = taps.shape[1]
    DV = W // H - 2 * DK
    f = jax.ShapeDtypeStruct
    base = start // NC
    shapes = [f((L, H * DV), F32), f((L, H * DV), F32), f((L, H * C), F32), f((L // C, H * DK, DV), F32)]
    more, more_specs, aliases = [], [], {}
    if before is not None:
        more = [before[4]] + list(before[:4])
        more_specs = [whole_block(before[4])] + [pl.BlockSpec(memory_space=pl.ANY)] * 4
        aliases = {5 + n: n for n in range(4)}
    return pl.pallas_call(
        functools.partial(fwd_kernel, H, DV, NC, start),
        grid=(count // NC,),
        in_specs=[
            row_block(NC * C, wide, lambda s: base + s),
            row_block(HALO, wide, lambda s: jnp.maximum((base + s) * (NC * C // HALO) - 1, 0)),
            whole_block(taps),
            whole_block(par),
        ]
        + more_specs,
        out_specs=[
            row_block(NC * C, H * DV, lambda s: base + s),
            row_block(NC * C, H * DV, lambda s: base + s),
            row_block(NC * C, H * C, lambda s: base + s),
            pl.BlockSpec((NC, H * DK, DV), lambda s: (base + s, 0, 0)),
            pl.BlockSpec((H * DK, DV), lambda s: (0, 0)),
        ],
        out_shape=shapes + [f((H * DK, DV), F32)],
        scratch_shapes=[pltpu.VMEM((NC * C + HALO, W), F32)],
        input_output_aliases=aliases,
        compiler_params=room(18),
        cost_estimate=pl.CostEstimate(
            flops=3 * 10**9 * count, bytes_accessed=3 * 2**20 * count, transcendentals=0
        ),
        name="mixer_fwd",
    )(projected, projected, taps, par, *more)


def mixer_bwd(projected, taps, par, written, inverse, states, grad_heads, heads, end, count, before=None):
    L, wide = projected.shape
    H, C = heads, CHUNK
    W = taps.shape[1]
    DV = W // H - 2 * DK
    f = jax.ShapeDtypeStruct

    def back(s):
        return end - s

    more, more_specs, aliases = [], [], {}
    if before is not None:
        more = list(before)
        more_specs = [pl.BlockSpec(memory_space=pl.ANY)] + [whole_block(a) for a in before[1:]]
        aliases = {8: 0}
    state, halo = f((H * DK, DV), F32), f((HALO, W), F32)
    return pl.pallas_call(
        functools.partial(bwd_kernel, H, DV, end, before is None),
        grid=(count,),
        in_specs=[
            row_block(C, wide, back),
            row_block(HALO, wide, lambda s: jnp.maximum(back(s) * (C // HALO) - 1, 0)),
            whole_block(taps),
            whole_block(par),
            row_block(C, H * DV, back),
            row_block(C, H * C, back),
            pl.BlockSpec((1, H * DK, DV), lambda s: (back(s), 0, 0)),
            row_block(C, H * DV, back),
        ]
        + more_specs,
        out_specs=[
            row_block(C, wide, back),
            whole_block(taps),
            whole_block(par),
            whole_block(state),
            whole_block(halo),
        ],
        out_shape=[f((L, wide), BF), f(taps.shape, F32), f(par.shape, F32), state, halo],
        scratch_shapes=[pltpu.VMEM((C + HALO, W), F32), pltpu.VMEM((C + HALO, W), F32)],
        input_output_aliases=aliases,
        compiler_params=room(16),
        cost_estimate=pl.CostEstimate(
            flops=6 * 10**9 * count, bytes_accessed=4 * 2**20 * count, transcendentals=0
        ),
        name="mixer_bwd",
    )(projected, projected, taps, par, written, inverse, states, grad_heads, *more)


def gate_fwd_kernel(DV, o_ref, gate_ref, gain_ref, out_ref):
    for start in range(0, o_ref.shape[1], DV):
        cut = slice(start, start + DV)
        heads, gate = o_ref[:, cut], gate_ref[:, cut]
        inverse = lax.rsqrt(jnp.mean(heads * heads, axis=1, keepdims=True) + 1e-05)
        out_ref[:, cut] = (heads * inverse * gain_ref[...] * (gate * jax.nn.sigmoid(gate))).astype(BF)


def gate_fwd(heads_out, gate_proj, gain):
    L, width = heads_out.shape
    rows = L // 8
    return pl.pallas_call(
        functools.partial(gate_fwd_kernel, gain.shape[1]),
        grid=(8,),
        in_specs=[row_block(rows, width), row_block(rows, width), whole_block(gain)],
        out_specs=row_block(rows, width),
        out_shape=jax.ShapeDtypeStruct((L, width), BF),
        compiler_params=room(8),
        cost_estimate=pl.CostEstimate(flops=10**6, bytes_accessed=10**5, transcendentals=0),
        name="gate_fwd",
    )(heads_out, gate_proj, gain)


def gate_bwd_kernel(DV, o_ref, gate_ref, gain_ref, in_ref, do_ref, dgate_ref, dgain_ref):
    @pl.when(pl.program_id(0) == 0)
    def _():
        dgain_ref[...] = jnp.zeros_like(dgain_ref)

    for start in range(0, o_ref.shape[1], DV):
        cut = slice(start, start + DV)
        heads, gate, grad = o_ref[:, cut], gate_ref[:, cut], in_ref[:, cut]
        inverse = lax.rsqrt(jnp.mean(heads * heads, axis=1, keepdims=True) + 1e-05)
        normed = heads * inverse
        sig = jax.nn.sigmoid(gate)
        dgate_ref[:, cut] = (
            grad * (normed * gain_ref[...]) * (sig * (1.0 + gate * (1.0 - sig)))
        ).astype(BF)
        d_scaled = grad * (gate * sig)
        dgain_ref[...] += jnp.sum(d_scaled * normed, axis=0, keepdims=True)
        d_normed = d_scaled * gain_ref[...]
        do_ref[:, cut] = inverse * (
            d_normed - normed * jnp.mean(d_normed * normed, axis=1, keepdims=True)
        )


def gate_bwd(heads_out, gate_proj, gain, grad_mixer):
    L, width = heads_out.shape
    rows = L // 8
    f = jax.ShapeDtypeStruct
    return pl.pallas_call(
        functools.partial(gate_bwd_kernel, gain.shape[1]),
        grid=(8,),
        in_specs=[row_block(rows, width), row_block(rows, width), whole_block(gain), row_block(rows, width)],
        out_specs=[row_block(rows, width), row_block(rows, width), whole_block(gain)],
        out_shape=[f((L, width), F32), f((L, width), BF), f(gain.shape, F32)],
        compiler_params=room(8),
        cost_estimate=pl.CostEstimate(flops=10**6, bytes_accessed=10**5, transcendentals=0),
        name="gate_bwd",
    )(heads_out, gate_proj, gain, grad_mixer)


def at_place(place, n):
    return jnp.where(place < n // 2, 2 * place, 2 * (n - place) - 1)


def place_of(index, n):
    return jnp.where(index % 2 == 0, index // 2, n - (index + 1) // 2)


def ring_pairs(n):
    order = list(range(0, n, 2)) + list(range(n - 1, 0, -2))
    ahead = [(order[i], order[(i + 1) % n]) for i in range(n)]
    return ahead, [(d, s) for s, d in ahead]


def behind(d):
    n = lax.axis_size("dp")
    return at_place((place_of(lax.axis_index("dp"), n) - d + n) % n, n)


def after(values, token):
    return lax.optimization_barrier((values, token))[0]


class GatherRing:
    def __init__(self, shard):
        half = shard.shape[0] // 2
        self.first, self.second = [shard[:half]], [shard[half:]]
        self.n = lax.axis_size("dp")

    def send(self, token):
        ahead, back = ring_pairs(self.n)
        first, second = after((self.first[-1], self.second[-1]), token)
        self.first.append(lax.ppermute(first, "dp", ahead))
        self.second.append(lax.ppermute(second, "dp", back))

    def last(self):
        return self.first[-1], self.second[-1]

    def through(self):
        return len(self.first) == self.n

    def finish(self, widths, token=None):
        half = self.first[0].shape[0]
        if token is None:
            token = self.first[1 % self.n], self.second[1 % self.n]
        nothing = after(jnp.zeros((), BF), token)
        fulls = [jnp.broadcast_to(nothing, (self.n * 2 * half, width)) for width in widths]
        for hop in range(self.n):
            for piece, at in (
                (self.first[hop], behind(hop) * 2 * half),
                (self.second[hop], behind(self.n - hop) * 2 * half + half),
            ):
                fulls = [
                    lax.dynamic_update_slice(full, part, (at, 0))
                    for full, part in zip(fulls, columns(piece, widths))
                ]
        return fulls


def land_kernel(widths, at_ref, first, second, *refs):
    count = len(widths)
    for arrived, mine, out in (
        (first, refs[:count], refs[-2]),
        (second, refs[count : 2 * count], refs[-1]),
    ):
        start = 0
        for width, term in zip(widths, mine):
            cut = slice(start, start + width)
            out[:, cut] = (arrived[:, cut].astype(F32) + term[...].astype(F32)).astype(BF)
            start += width


def landed(flying, partials, places):
    widths = [partial.shape[1] for partial in partials]
    rows, wide = flying[0].shape
    steps = 2
    block = rows // steps
    sent = pl.BlockSpec((block, wide), lambda s, at: (s, 0))

    def term(width, side):
        return pl.BlockSpec(
            (block, width), lambda s, at: (at[side] * (2 * steps) + side * steps + s, 0)
        )

    terms = [term(width, side) for side in (0, 1) for width in widths]
    return pl.pallas_call(
        functools.partial(land_kernel, widths),
        grid_spec=pltpu.PrefetchScalarGridSpec(
            num_scalar_prefetch=1, grid=(steps,), in_specs=[sent, sent] + terms, out_specs=[sent, sent]
        ),
        out_shape=[jax.ShapeDtypeStruct((rows, wide), BF)] * 2,
        compiler_params=room(8),
        cost_estimate=pl.CostEstimate(flops=10**6, bytes_accessed=10**6, transcendentals=0),
        name="land",
    )(jnp.stack(places).astype(jnp.int32), *flying, *partials, *partials)


class ScatterRing:
    def __init__(self, pairs, token, partials=None):
        self.n = lax.axis_size("dp")
        self.hop = 0
        self.pairs, self.partials = pairs, partials
        self.sums = tuple(
            jnp.concatenate(self.terms_of(place, side, token), axis=1).astype(BF)
            for place, side in ((1, 0), (self.n - 1, 1))
        )

    def terms_of(self, place, side, token):
        terms = []
        for number, (features, grads) in enumerate(self.pairs):
            half = features.shape[1] // self.n // 2
            at = behind(place % self.n) * (2 * half) + side * half
            if self.partials is not None:
                terms.append(lax.dynamic_slice_in_dim(self.partials[number], at, half, 0))
                continue
            left = lax.dynamic_slice_in_dim(features, at, half, 1)
            terms.append(contract_rows(*after((left, grads), token)))
        return terms

    def prepare(self, token):
        self.partials = [
            contract_rows(*after((features, grads), token)).astype(BF)
            for features, grads in self.pairs
        ]
        return self.partials

    def send(self, token):
        ahead, back = ring_pairs(self.n)
        first, second = after(self.sums, token)
        self.flying = lax.ppermute(first, "dp", ahead), lax.ppermute(second, "dp", back)

    def land(self, token):
        self.hop += 1
        flying = after(self.flying, token)
        if self.hop < self.n - 1:
            places = behind((self.hop + 1) % self.n), behind((self.n - 1 - self.hop) % self.n)
            self.sums = tuple(landed(flying, self.partials, places))
            return self.sums
        self.sums = tuple(
            [
                x.astype(F32) + y.astype(F32)
                for x, y in zip(
                    columns(arrived, [part.shape[1] for part in self.partials]),
                    self.terms_of(0, side, ()),
                )
            ]
            for side, arrived in enumerate(flying)
        )
        return self.sums

    def done(self):
        return self.hop == self.n - 1

    def results(self):
        return [jnp.concatenate(halves, axis=0) for halves in zip(*self.sums)]


def slot(token, rings, pieces=(), gathers=()):
    rings = [ring for ring in rings if not ring.done()]
    gathers = [ring for ring in gathers if not ring.through()]
    for ring in rings:
        ring.send(token)
    for ring in gathers:
        ring.send(token)
    for piece in pieces:
        token = piece(token)
    token = [ring.land(token) for ring in rings] or token
    if gathers:
        token = token, [ring.last() for ring in gathers]
    return token


def run_out(token, rings, pieces=(), gathers=()):
    pieces = list(pieces)
    while (
        pieces
        or any(not ring.done() for ring in rings)
        or any(not ring.through() for ring in gathers)
    ):
        token = slot(token, rings, [pieces.pop(0)] if pieces else (), gathers)
    return token


def contract_rows(left, right):
    return lax.dot_general(
        left, right, (((0,), (0,)), ((), ())), preferred_element_type=jnp.float32
    )


def times_transposed(left, right):
    return lax.dot_general(
        left, right, (((1,), (1,)), ((), ())), preferred_element_type=jnp.float32
    )


CORES = [(0, 1), (1, 0), (2, 3), (3, 2)]
PAIRS = [(0, 2), (2, 0), (1, 3), (3, 1)]


class Spread:
    def __init__(self, block):
        self.block = block
        self.plain = lax.axis_size("tensor") != 4
        if not self.plain:
            self.far = lax.ppermute(block, "tensor", PAIRS)
            self.near = lax.ppermute(block, "tensor", CORES)

    def turn(self, token):
        if self.plain:
            return token
        far = after(self.far, token)
        self.far_near = lax.ppermute(far, "tensor", CORES)
        return far

    def rows(self, token=()):
        if self.plain:
            return lax.all_gather(after(self.block, token), "tensor", axis=0, tiled=True)
        rank = lax.axis_index("tensor")
        rows, width = self.block.shape
        out = jnp.zeros((4 * rows, width), self.block.dtype)
        parts = after((self.block, self.near, self.far, self.far_near), token)
        for flip, part in enumerate(parts):
            out = lax.dynamic_update_slice_in_dim(out, part, (rank ^ flip) * rows, 0)
        return out


def spread_rows(block):
    spread = Spread(block)
    spread.turn(())
    return spread.rows()


class RowSum:
    def __init__(self, product, rows):
        self.product, self.rows = product, rows
        self.rank = lax.axis_index("tensor")
        self.plain = lax.axis_size("tensor") != 4

    def term(self, flip, token):
        return self.product((self.rank ^ flip) * self.rows, token)

    def far(self, token):
        if self.plain:
            whole = [self.product(i * self.rows, token) for i in range(lax.axis_size("tensor"))]
            self.total = lax.psum_scatter(
                jnp.concatenate(whole, axis=0), "tensor", scatter_dimension=0, tiled=True
            )
            return self.total
        self.sent = self.term(3, token).astype(BF)
        self.far_near = lax.ppermute(self.sent, "tensor", CORES)
        return self.sent

    def far_sum(self, token):
        if self.plain:
            return token
        total = (self.term(2, token) + self.far_near.astype(F32)).astype(BF)
        self.from_far = lax.ppermute(total, "tensor", PAIRS)
        return total

    def near(self, token):
        if self.plain:
            return token
        sent = self.term(1, token).astype(BF)
        self.from_near = lax.ppermute(sent, "tensor", CORES)
        return sent

    def own(self, token):
        if self.plain:
            return token
        self.mine = self.term(0, token)
        return self.mine

    def result(self, token):
        if self.plain:
            return after(self.total, token)
        mine = after(self.mine, token)
        return mine + self.from_near.astype(F32) + self.from_far.astype(F32)

    def pieces(self):
        return [self.far, self.far_sum, self.near, self.own]


def summed_rows(pairs, rows):
    def product(start, token):
        total = None
        for grads, weight in pairs:
            part, other = after((lax.dynamic_slice_in_dim(grads, start, rows, 0), weight), token)
            part = times_transposed(part, other)
            total = part if total is None else total + part
        return total

    return RowSum(product, rows)


def sum_over(values, axis):
    n = lax.axis_size(axis)
    if n & (n - 1):
        return lax.psum(values, axis)
    step = 1
    while step < n:
        values = values + lax.ppermute(values, axis, [(i, i ^ step) for i in range(n)])
        step *= 2
    return values


def packed(arrays):
    flat = jnp.concatenate([a.reshape(-1) for a in arrays])
    pad = -flat.shape[0] % 1024
    return jnp.pad(flat, (0, pad)).reshape(-1, 128)


def unpacked(values, shapes):
    flat = values.reshape(-1)
    out, start = [], 0
    for shape in shapes:
        size = 1
        for extent in shape:
            size *= extent
        out.append(flat[start : start + size].reshape(shape))
        start += size
    return out


def norm_back(values, inverse, gain, incoming):
    scaled = incoming * gain
    width = values.shape[1]
    grad_values = (
        inverse * scaled
        - values
        * inverse
        * inverse
        * inverse
        * jnp.sum(scaled * values, axis=1, keepdims=True)
        / width
    )
    grad_gain = jnp.sum(incoming * values * inverse, axis=0)
    return (grad_values, grad_gain)


def place_slice(local, whole, rank, axis):
    return lax.dynamic_update_slice_in_dim(
        jnp.zeros_like(whole), local, rank * local.shape[axis], axis
    )


def columns(array, widths):
    out, start = [], 0
    for width in widths:
        out.append(array[:, start : start + width])
        start += width
    return out


def shards(
    inputs,
    lengths,
    cotangent,
    norm_attn,
    norm_ffn,
    norm_heads,
    w_query,
    w_key,
    w_value,
    w_out_gate,
    w_decay,
    w_beta,
    w_output,
    conv_query,
    conv_key,
    conv_value,
    decay_log,
    decay_bias,
    w_ffn_gate,
    w_ffn_up,
    w_ffn_down,
):
    rows = inputs.shape[0]
    width = inputs.shape[1]
    tensor_rank = lax.axis_index("tensor")
    positions = tensor_rank * rows + jnp.arange(rows, dtype=jnp.int32)
    valid = (positions < lengths[0]).astype(jnp.float32)[:, None]
    heads_here = w_decay.shape[1]
    widths = [w.shape[1] for w in (w_query, w_key, w_value, w_decay, w_beta)]
    fill = -sum(widths) % 128
    mixed_shard = jnp.pad(
        jnp.concatenate((w_query, w_key, w_value, w_decay, w_beta), axis=1), ((0, 0), (0, fill))
    )
    ffn_width = w_ffn_gate.shape[1]
    kept = {}
    mixed_ring = GatherRing(mixed_shard)
    mixed_ring.send(())
    inputs, cotangent = after((inputs, cotangent), mixed_ring.last())
    token = run_out(mixed_ring.last(), (), (), (mixed_ring,))

    def arrived(hop):
        at = min(hop, mixed_ring.n - 1)
        return mixed_ring.first[at], mixed_ring.second[at]

    gate_shards = after((w_out_gate, w_output), arrived(3))
    gate_ring = GatherRing(jnp.concatenate((gate_shards[0], gate_shards[1].T), axis=1))
    [mixed_full] = mixed_ring.finish([mixed_shard.shape[1]])

    gain_attn = norm_attn
    gain_ffn = norm_ffn
    stream_in = inputs.astype(jnp.float32)
    grad_out = valid * cotangent.astype(jnp.float32)
    inverse_in = lax.rsqrt(jnp.mean(stream_in * stream_in, axis=1, keepdims=True) + 1e-06)
    full_in = spread_rows((stream_in * inverse_in * gain_attn).astype(jnp.bfloat16))

    def here(array):
        size = array.shape[-1] // lax.axis_size("tensor")
        return lax.dynamic_slice_in_dim(array, tensor_rank * size, size, array.ndim - 1)

    taps = jnp.concatenate((here(conv_query), here(conv_key), here(conv_value)), axis=1)
    par = jnp.pad(
        jnp.stack((-jnp.exp(here(decay_log)), here(decay_bias))), ((0, 6), (0, 128 - heads_here))
    )
    gain_heads = norm_heads[None, :]
    chunks = full_in.shape[0] // CHUNK
    parts = 4

    def project(token):
        kept["projected"] = jnp.dot(
            *after((full_in, mixed_full), token), preferred_element_type=jnp.float32
        )
        kept["forward"] = None
        return kept["projected"]

    def forward_part(start):
        def piece(token):
            kept["forward"] = mixer_fwd(
                after(kept["projected"], token),
                taps,
                par,
                heads_here,
                start,
                chunks // parts,
                kept["forward"],
            )
            return kept["forward"][4]

        return piece

    token = run_out(
        token,
        (),
        [project] + [forward_part(i * (chunks // parts)) for i in range(parts)],
        (gate_ring,),
    )
    projected = kept["projected"]
    heads_out, written, inverse, states, _ = kept["forward"]
    ffn_shards = after((w_ffn_gate, w_ffn_up, w_ffn_down), arrived(4))
    ffn_ring = GatherRing(
        jnp.concatenate((ffn_shards[0], ffn_shards[1], ffn_shards[2].T), axis=1)
    )
    gate_full, output_full = gate_ring.finish(
        [w_out_gate.shape[1], w_output.shape[0]], arrived(5)
    )

    def gate(token):
        kept["gate"] = jnp.dot(
            *after((full_in, gate_full), token), preferred_element_type=jnp.float32
        )
        kept["mixer"] = gate_fwd(heads_out, kept["gate"], gain_heads)
        return kept["mixer"]

    def attend(token):
        kept["attn"] = summed_rows(((kept["mixer"], output_full),), rows)
        return kept["attn"].far_sum(kept["attn"].far(token))

    def attend_own(token):
        return kept["attn"].own(kept["attn"].near(token))

    def middle(token):
        kept["branch"] = kept["attn"].result(token)
        stream = stream_in + kept["branch"]
        kept["stream"] = stream
        kept["inverse"] = lax.rsqrt(jnp.mean(stream * stream, axis=1, keepdims=True) + 1e-06)
        normed = (stream * kept["inverse"] * gain_ffn).astype(jnp.bfloat16)
        kept["full_mid"] = spread_rows(normed)
        return normed

    token = run_out(token, (), [gate, attend, attend_own, middle], (ffn_ring,))
    gate_proj, mixer, branch_attn = kept["gate"], kept["mixer"], kept["branch"]
    stream, inverse_mid, full_mid = kept["stream"], kept["inverse"], kept["full_mid"]
    ffn_gate_full, ffn_up_full, down_full = ffn_ring.finish(
        [ffn_width, ffn_width, w_ffn_down.shape[0]]
    )
    grad_ffn = spread_rows(after(grad_out.astype(jnp.bfloat16), full_mid))

    token, full_mid_in = after((token, full_mid), ffn_ring.last())
    ffn_gate = jnp.dot(full_mid_in, ffn_gate_full, preferred_element_type=jnp.float32)
    ffn_up = jnp.dot(full_mid_in, ffn_up_full, preferred_element_type=jnp.float32)
    sigma = jax.nn.sigmoid(ffn_gate)
    silu_gate = ffn_gate * sigma
    hidden = (silu_gate * ffn_up).astype(jnp.bfloat16)
    grad_hidden = jnp.dot(grad_ffn, down_full, preferred_element_type=jnp.float32)
    grad_gate_in = grad_hidden * ffn_up * sigma * (1.0 + ffn_gate * (1.0 - sigma))
    grad_gate_in = grad_gate_in.astype(jnp.bfloat16)
    grad_up_in = (grad_hidden * silu_gate).astype(jnp.bfloat16)
    token = grad_gate_in, grad_up_in, hidden
    ffn_scatter = ScatterRing(
        ((full_mid, grad_gate_in), (full_mid, grad_up_in), (grad_ffn, hidden)), token
    )
    token = ffn_scatter.sums
    mid_sum = summed_rows(((grad_gate_in, ffn_gate_full), (grad_up_in, ffn_up_full)), rows)

    def mid_own(token):
        return mid_sum.own(mid_sum.near(token))

    def middle_back(token):
        through, kept["norm_ffn"] = norm_back(stream, inverse_mid, gain_ffn, mid_sum.result(token))
        kept["grad_stream"] = grad_out + through
        low = kept["grad_stream"].astype(jnp.bfloat16)
        kept["spread"] = Spread(low)
        return low

    def turn(token):
        token = ffn_sum.far_sum(ffn_sum.far(kept["spread"].turn(token)))
        kept["grad_attn"] = kept["spread"].rows(token)
        return kept["grad_attn"]

    def attend_back(token):
        grad_mixer = jnp.dot(
            *after((kept["grad_attn"], output_full), token), preferred_element_type=jnp.float32
        )
        kept["gate_back"] = gate_bwd(heads_out, gate_proj, gain_heads, grad_mixer)
        kept["backward"] = None
        return kept["gate_back"][0]

    def backward_part(end):
        def piece(token):
            kept["backward"] = mixer_bwd(
                projected,
                taps,
                par,
                written,
                inverse,
                states,
                after(kept["gate_back"][0], token),
                heads_here,
                end,
                chunks // parts,
                kept["backward"],
            )
            return kept["backward"][3]

        return piece

    ffn_sum = summed_rows(((hidden, down_full),), rows)
    backward = [backward_part(chunks - 1 - i * (chunks // parts)) for i in range(parts)]
    token = run_out(
        token,
        (ffn_scatter,),
        [
            ffn_scatter.prepare,
            lambda t: mid_sum.far_sum(mid_sum.far(t)),
            mid_own,
            middle_back,
            turn,
            attend_back,
        ]
        + backward[:1],
    )
    grad_stream, grad_norm_ffn, grad_attn = kept["grad_stream"], kept["norm_ffn"], kept["grad_attn"]
    _, grad_gate_proj, heads_gain_grad = kept["gate_back"]
    gate_scatter = ScatterRing(
        ((full_in, grad_gate_proj), (grad_attn, mixer)), token
    )
    token = token, gate_scatter.sums

    def in_far(token):
        kept["in_sum"] = summed_rows(
            ((grad_gate_proj, gate_full), (kept["backward"][0], mixed_full)), rows
        )
        return kept["in_sum"].far(token)

    def leave(token):
        kept["branch_ffn"] = ffn_sum.result(token)
        kept["outputs"] = (valid * (stream + kept["branch_ffn"])).astype(jnp.bfloat16)
        return kept["outputs"]

    def in_far_sum(token):
        return kept["in_sum"].far_sum(token)

    def in_near(token):
        return kept["in_sum"].near(token)

    def in_own(token):
        return kept["in_sum"].own(token)

    def last_back(token):
        through, kept["norm_attn"] = norm_back(
            stream_in, inverse_in, gain_attn, kept["in_sum"].result(token)
        )
        kept["grad_inputs"] = grad_stream + through
        return kept["grad_inputs"]

    token = run_out(
        token,
        (gate_scatter,),
        [gate_scatter.prepare]
        + backward[1:]
        + [in_far, in_far_sum, lambda t: in_near(ffn_sum.near(t))],
    )
    grad_projected, grad_taps, grad_par, _, _ = kept["backward"]
    mixed_scatter = ScatterRing(((full_in, grad_projected),), token)
    token = token, mixed_scatter.sums
    token = slot(token, (mixed_scatter,), [ffn_sum.own, mixed_scatter.prepare])
    token = slot(token, (mixed_scatter,), [leave, in_own])
    branch_ffn, outputs = kept["branch_ffn"], kept["outputs"]
    stat_sums = jnp.stack(
        [
            jnp.sum(valid * stream_in * stream_in),
            jnp.sum(valid * branch_attn * branch_attn),
            jnp.sum(valid * branch_ffn * branch_ffn),
            jnp.sum(valid),
        ]
    )
    local = columns(grad_taps, widths[:3]) + [grad_par[0, :heads_here], grad_par[1, :heads_here]]
    whole = [conv_query, conv_key, conv_value, decay_log, decay_bias]
    common = [stat_sums, grad_norm_ffn, heads_gain_grad[0], norm_attn]
    def common_over_dp(token):
        parts = common[:3] + [kept["norm_attn"]] + local
        kept["common"] = sum_over(after(packed(parts), token), "dp")
        return kept["common"]

    def common_over_tensor(token):
        sums = unpacked(kept["common"], [a.shape for a in common + local])
        spread = [
            place_slice(part, array, tensor_rank, part.ndim - 1)
            for part, array in zip(sums[4:], whole)
        ]
        kept["common"] = sum_over(after(packed(sums[:4] + spread), token), "tensor")
        return kept["common"]

    token = run_out(
        token,
        (mixed_scatter,),
        [last_back, common_over_dp, common_over_tensor],
    )
    grad_inputs = kept["grad_inputs"]
    owned_gate, owned_up, owned_down = ffn_scatter.results()
    owned_out_gate, owned_output = gate_scatter.results()
    owned_query, owned_key, owned_value, owned_decay, owned_beta = columns(
        mixed_scatter.results()[0], widths
    )
    (
        stat_sums,
        total_ffn_gain,
        total_heads_gain,
        total_attn_gain,
        total_conv_query,
        total_conv_key,
        total_conv_value,
        total_decay_log,
        total_decay_bias,
    ) = unpacked(kept["common"], [a.shape for a in common + whole])
    statistics = jnp.sqrt(stat_sums[:3] / (stat_sums[3] * width))
    return (
        outputs,
        statistics,
        grad_inputs,
        total_attn_gain,
        total_ffn_gain,
        total_heads_gain,
        owned_query,
        owned_key,
        owned_value,
        owned_out_gate,
        owned_decay,
        owned_beta,
        owned_output.T,
        total_conv_query,
        total_conv_key,
        total_conv_value,
        total_decay_log,
        total_decay_bias,
        owned_gate,
        owned_up,
        owned_down.T,
    )


def solution(mesh):
    in_specs = (
        P(("dp", "tensor"), None),
        P("dp"),
        P(("dp", "tensor"), None),
        P(),
        P(),
        P(),
        P("dp", "tensor"),
        P("dp", "tensor"),
        P("dp", "tensor"),
        P("dp", "tensor"),
        P("dp", "tensor"),
        P("dp", "tensor"),
        P("tensor", "dp"),
        P(),
        P(),
        P(),
        P(),
        P(),
        P("dp", "tensor"),
        P("dp", "tensor"),
        P("tensor", "dp"),
    )
    out_specs = (
        P(("dp", "tensor"), None),
        P(),
        P(("dp", "tensor"), None),
        P(),
        P(),
        P(),
        P("dp", "tensor"),
        P("dp", "tensor"),
        P("dp", "tensor"),
        P("dp", "tensor"),
        P("dp", "tensor"),
        P("dp", "tensor"),
        P("tensor", "dp"),
        P(),
        P(),
        P(),
        P(),
        P(),
        P("dp", "tensor"),
        P("dp", "tensor"),
        P("tensor", "dp"),
    )
    return jax.shard_map(shards, mesh=mesh, in_specs=in_specs, out_specs=out_specs, check_vma=False)
```
